768 devices in a mesh: gx: 48 (over z, x_lo, core), gy: 16 (over y, x_hi).
Axes of the slice: x: 4 (x_hi: 2, x_lo: 2; x = x_hi * 2 + x_lo), y: 8, z: 12, core: 2. Of those that a mesh axis runs over, the one named last changes fastest.
Arguments:
- state: float32 [5, 384, 128, 128], P(None, 'gx', 'gy'), may hold values from -1.2 to 5, as said below
- eddy: float32 [384, 128, 128], P('gx', 'gy'), may hold values from 0.05 to 0.5
- adjoint: float32 [5, 384, 128, 128], P(None, 'gx', 'gy'), may hold values from -6 to 6
Outputs:
- grad_state: float32 [5, 384, 128, 128], P(None, 'gx', 'gy')
- grad_eddy: float32 [384, 128, 128], P('gx', 'gy')
The draws below stay inside these ranges and needn't reach their ends.
Inputs may be any that keep to these rules, and one draw needn't show every extreme that they name: `state`: component 0 is the density, 1 to 3 the momenta, 4 the total energy; density and pressure lie in 0.7 to 1.4 and every velocity component in -0.8 to 0.8 in every cell.
All inputs are finite; a program needn't handle non-finite values.
Results may differ from the reference program's by a relative error of at most 0.0003.
Values sent between devices are 32-bit elements; how exact they have to be, the bound alone decides.
No kernel may reach another device: no remote copies, remote signals or barrier semaphores. Data moves between devices by JAX's collectives and lax.ppermute only.
A program may use at most 192 MiB of HBM per device.

```python
import math
import jax
import jax.numpy as jnp
from jax import lax

CX = 8
NZ = 128
NX = 384
NY = 128


def draw_state(key, part):
    key = jax.random.fold_in(key, 11)
    key_list = jax.random.split(key, 3)
    grid_shape = (NX, NY, NZ)
    specific_heaviness = 0.7 * jnp.exp(math.log(2.0) * jax.random.uniform(key_list[0], grid_shape, jnp.float32))
    thermodynamic_push = 0.7 * jnp.exp(math.log(2.0) * jax.random.uniform(key_list[1], grid_shape, jnp.float32))
    velocity = jnp.clip(0.25 * jax.random.normal(key_list[2], (3,) + grid_shape, jnp.float32), -0.75, 0.75)
    energy = thermodynamic_push / 0.4 + 0.5 * specific_heaviness * jnp.sum(velocity * velocity, axis=0)
    return jnp.concatenate([specific_heaviness[None], specific_heaviness * velocity, energy[None]], axis=0)


def block_scale(stream_key, shape, cuts, smallest, top_value):
    level, own = 1.0, jax.random.fold_in(stream_key, 6)
    for dim, parts in cuts:
        draws = jnp.exp(jax.random.uniform(jax.random.fold_in(own, dim), (parts,), jnp.float32, smallest / len(cuts), top_value / len(cuts)))
        level = level * jnp.repeat(draws, shape[dim] // parts).reshape([-1 if axis == dim else 1 for axis in range(len(shape))])
    return level


def bell_draw(own_key, dims, deviation, limit, cuts=(), kind=jnp.bfloat16):
    drawn = jax.random.normal(own_key, dims, jnp.float32) * deviation
    if len(cuts) > 0:
        drawn = block_scale(own_key, dims, cuts, -0.22, 0.18) * drawn
    return jnp.clip(drawn, min=-limit, max=limit).astype(kind)


def setup_inputs(seed: int = 0) -> dict:
    splits = jax.random.split(jax.random.key(seed), 4)
    return {
        "state": draw_state(jax.random.fold_in(splits[3], 71), 0),
        "eddy": jnp.clip(jnp.exp(math.log(0.5) - 2.3025851 * jax.random.uniform(splits[1], (NX, NY, NZ), jnp.float32) ** block_scale(splits[1], (NX, NY, NZ), ((0, 48), (1, 16)), -0.2, 0.2)), 0.05, 0.5),
        "adjoint": bell_draw(splits[2], (5, NX, NY, NZ), 1.0, 6.0, ((1, 48), (2, 16)), jnp.float32),
    }


HEAT_RATIO = 1.4
SPLIT_SPEED = 4.0
MOLECULAR_DRAG = 0.05
PRANDTL = 0.72
TIME_STEP = 0.04
SMOOTH_EPS = 1e-06

def trimmed_array(values, left_x, right_x, left_y, right_y):
    return values[..., left_x:values.shape[-3] - right_x, left_y:values.shape[-2] - right_y, :]

def along_z(values, offset):
    return jnp.roll(values, -offset, axis=-1)

def weno_face(far_left, near_left, centre_cell, near_right, far_right):
    smooth_one = 13.0 / 12.0 * (far_left - 2.0 * near_left + centre_cell) ** 2 + 0.25 * (far_left - 4.0 * near_left + 3.0 * centre_cell) ** 2
    smooth_two = 13.0 / 12.0 * (near_left - 2.0 * centre_cell + near_right) ** 2 + 0.25 * (near_left - near_right) ** 2
    smooth_three = 13.0 / 12.0 * (centre_cell - 2.0 * near_right + far_right) ** 2 + 0.25 * (3.0 * centre_cell - 4.0 * near_right + far_right) ** 2
    guess_one = (2.0 * far_left - 7.0 * near_left + 11.0 * centre_cell) / 6.0
    guess_two = (-near_left + 5.0 * centre_cell + 2.0 * near_right) / 6.0
    guess_three = (2.0 * centre_cell + 5.0 * near_right - far_right) / 6.0
    weight_one = 0.1 / (SMOOTH_EPS + smooth_one) ** 2
    weight_two = 0.6 / (SMOOTH_EPS + smooth_two) ** 2
    weight_three = 0.3 / (SMOOTH_EPS + smooth_three) ** 2
    return (weight_one * guess_one + weight_two * guess_two + weight_three * guess_three) / (weight_one + weight_two + weight_three)

def face_sum(plus_part, minus_part, picker):
    right_going = weno_face(picker(plus_part, -2), picker(plus_part, -1), picker(plus_part, 0), picker(plus_part, 1), picker(plus_part, 2))
    left_going = weno_face(picker(minus_part, 3), picker(minus_part, 2), picker(minus_part, 1), picker(minus_part, 0), picker(minus_part, -1))
    return right_going + left_going

def pick_x(values, offset):
    return trimmed_array(values, 2 + offset, 3 - offset, 3, 3)

def pick_y(values, offset):
    return trimmed_array(values, 3, 3, 2 + offset, 3 - offset)

def pick_z(values, offset):
    return along_z(trimmed_array(values, 3, 3, 3, 3), offset)

def slope_first_coordinate(values):
    return 0.5 * (trimmed_array(values, 3, 1, 2, 2) - trimmed_array(values, 1, 3, 2, 2))

def slope_second_coordinate(values):
    return 0.5 * (trimmed_array(values, 2, 2, 3, 1) - trimmed_array(values, 2, 2, 1, 3))

def slope_third_coordinate(values):
    interior = trimmed_array(values, 2, 2, 2, 2)
    return 0.5 * (along_z(interior, 1) - along_z(interior, -1))

def section_rate(conserved, turbulent_mixing_array):
    specific_heaviness = conserved[0]
    momenta = conserved[1:4]
    energy = conserved[4]
    velocity = momenta / specific_heaviness
    kinetic = 0.5 * lax.optimization_barrier(jnp.sum(momenta * velocity, axis=0))
    thermodynamic_push = (HEAT_RATIO - 1.0) * (energy - kinetic)
    thermal_level = thermodynamic_push / specific_heaviness

    def split_parts(direction):
        normal_speed = velocity[direction]
        components = [momenta[direction], momenta[0] * normal_speed, momenta[1] * normal_speed, momenta[2] * normal_speed, (energy + thermodynamic_push) * normal_speed]
        components[1 + direction] = components[1 + direction] + thermodynamic_push
        fluxes = jnp.stack(components)
        return (0.5 * (fluxes + SPLIT_SPEED * conserved), 0.5 * (fluxes - SPLIT_SPEED * conserved))
    plus_x, minus_x = split_parts(0)
    faces_x = face_sum(plus_x, minus_x, pick_x)
    change = faces_x[..., 1:, :, :] - faces_x[..., :-1, :, :]
    plus_y, minus_y = split_parts(1)
    faces_y = face_sum(plus_y, minus_y, pick_y)
    change = change + faces_y[..., 1:, :] - faces_y[..., :-1, :]
    plus_z, minus_z = split_parts(2)
    faces_z = face_sum(plus_z, minus_z, pick_z)
    change = change + faces_z - along_z(faces_z, -1)
    gradients = [slope_first_coordinate(velocity), slope_second_coordinate(velocity), slope_third_coordinate(velocity)]
    thermal_slopes = [slope_first_coordinate(thermal_level), slope_second_coordinate(thermal_level), slope_third_coordinate(thermal_level)]
    core_thermal_level = trimmed_array(thermal_level, 2, 2, 2, 2)
    total_drag_array = MOLECULAR_DRAG * jnp.exp(0.7 * jnp.log(core_thermal_level)) + trimmed_array(turbulent_mixing_array, 2, 2, 2, 2)
    heat_flow = total_drag_array * (HEAT_RATIO / ((HEAT_RATIO - 1.0) * PRANDTL))
    spread = gradients[0][0] + gradients[1][1] + gradients[2][2]
    core_flow_speed = trimmed_array(velocity, 2, 2, 2, 2)
    viscous_fluxes = []
    for coordinate_index in range(3):
        shear_tensor = []
        for j in range(3):
            stress = total_drag_array * (gradients[coordinate_index][j] + gradients[j][coordinate_index])
            if j == coordinate_index:
                stress = stress - 2.0 / 3.0 * total_drag_array * spread
            shear_tensor.append(stress)
        mechanical_power = core_flow_speed[0] * shear_tensor[0] + core_flow_speed[1] * shear_tensor[1] + core_flow_speed[2] * shear_tensor[2] + heat_flow * thermal_slopes[coordinate_index]
        viscous_fluxes.append(jnp.stack(shear_tensor + [mechanical_power]))
    diffusion = 0.5 * (trimmed_array(viscous_fluxes[0], 2, 0, 1, 1) - trimmed_array(viscous_fluxes[0], 0, 2, 1, 1))
    diffusion = diffusion + 0.5 * (trimmed_array(viscous_fluxes[1], 1, 1, 2, 0) - trimmed_array(viscous_fluxes[1], 1, 1, 0, 2))
    inner_flux = trimmed_array(viscous_fluxes[2], 1, 1, 1, 1)
    diffusion = diffusion + 0.5 * (along_z(inner_flux, 1) - along_z(inner_flux, -1))
    return jnp.concatenate([jnp.zeros_like(diffusion[:1]), diffusion], axis=0) - change

def grid_rate(conserved, eddy):
    blocks = conserved.shape[1] // CX
    padded = jnp.pad(conserved, ((0, 0), (3, 3), (3, 3), (0, 0)), mode='wrap')
    eddy_pad = jnp.pad(eddy, ((3, 3), (3, 3), (0, 0)), mode='wrap')

    def per_block(block_index):
        start_row = (block_index * CX).astype(jnp.int32)
        segment = lax.dynamic_slice_in_dim(padded, start_row, CX + 6, 1)
        eddy_segment = lax.dynamic_slice_in_dim(eddy_pad, start_row, CX + 6, 0)
        return section_rate(segment, eddy_segment)
    stacked = lax.map(per_block, jnp.arange(blocks, dtype=jnp.int32))
    return jnp.moveaxis(stacked, 0, 1).reshape(conserved.shape)

def grid_pull(conserved, eddy, cotangent):
    blocks = conserved.shape[1] // CX
    padded = jnp.pad(conserved, ((0, 0), (6, 6), (6, 6), (0, 0)), mode='wrap')
    eddy_pad = jnp.pad(eddy, ((6, 6), (6, 6), (0, 0)), mode='wrap')
    cot_pad = jnp.pad(cotangent, ((0, 0), (3, 3), (3, 3), (0, 0)), mode='wrap')

    def per_block(block_index):
        start_row = (block_index * CX).astype(jnp.int32)
        segment = lax.dynamic_slice_in_dim(padded, start_row, CX + 12, 1)
        eddy_segment = lax.dynamic_slice_in_dim(eddy_pad, start_row, CX + 12, 0)
        cot_segment = lax.dynamic_slice_in_dim(cot_pad, start_row, CX + 6, 1)
        _, backward = jax.vjp(section_rate, segment, eddy_segment)
        grad_part, eddy_part = backward(cot_segment)
        return (trimmed_array(grad_part, 6, 6, 6, 6), trimmed_array(eddy_part, 6, 6, 6, 6))
    grad_blocks, eddy_blocks = lax.map(per_block, jnp.arange(blocks, dtype=jnp.int32))
    return (jnp.moveaxis(grad_blocks, 0, 1).reshape(conserved.shape), eddy_blocks.reshape(eddy.shape))

def reference(state, eddy, adjoint):
    section_one = state + TIME_STEP * grid_rate(state, eddy)
    section_two = 0.75 * state + 0.25 * (section_one + TIME_STEP * grid_rate(section_one, eddy))
    grad_part, eddy_part = grid_pull(section_two, eddy, adjoint)
    adjoint_two = 2.0 / 3.0 * (adjoint + TIME_STEP * grad_part)
    eddy_sum = 2.0 / 3.0 * TIME_STEP * eddy_part
    adjoint_zero = adjoint / 3.0 + 0.75 * adjoint_two
    grad_part, eddy_part = grid_pull(section_one, eddy, adjoint_two)
    adjoint_one = 0.25 * (adjoint_two + TIME_STEP * grad_part)
    eddy_sum = eddy_sum + 0.25 * TIME_STEP * eddy_part
    grad_part, eddy_part = grid_pull(state, eddy, adjoint_one)
    grad_state = adjoint_zero + adjoint_one + TIME_STEP * grad_part
    grad_eddy = eddy_sum + TIME_STEP * eddy_part
    return (grad_state, grad_eddy)
```

```python
import functools

import jax
import jax.numpy as jnp
from jax import lax
from jax.experimental import pallas as pl
from jax.experimental.pallas import tpu as pltpu
from jax.sharding import PartitionSpec as P

HEAT_RATIO = 1.4
MOLECULAR_DRAG = 0.05
PRANDTL = 0.72
TIME_STEP = 0.04
SMOOTH_EPS = 1e-06
CONDUCTION = HEAT_RATIO / ((HEAT_RATIO - 1.0) * PRANDTL)
SMALL = 0.75 * SMOOTH_EPS

PITCH = 16
PLANE = 14 * PITCH


def frame(left):
    return (2, 6, 0) if left else (0, 0, 8)


def get(ref, start, stride=1, count=8):
    if stride == 1:
        return ref[pl.ds(start, count), :]
    return ref[pl.ds(start, count, stride=stride), :]


def put(ref, start, value, stride=1, count=8):
    if stride == 1:
        ref[pl.ds(start, count), :] = value
    else:
        ref[pl.ds(start, count, stride=stride), :] = value


def add(ref, start, value, stride=1):
    put(ref, start, get(ref, start, stride) + value, stride)


def ahead(value, offset):
    return pltpu.roll(value, (-offset) % 128, 1)


def quick_inverse(value):
    return pl.reciprocal(value, approx=True)


def weno_parts(d1, d2, d3, d4):
    a1, a2, a3, a4 = 2.75 * d1, 2.5 * d2, 2.5 * d3, 2.75 * d4
    i1 = quick_inverse((d1 * d1 + SMALL) + d2 * (a2 - a1))
    i2 = quick_inverse((d2 * d2 + SMALL) + d3 * (d3 - 1.25 * d2))
    i3 = quick_inverse((d4 * d4 + SMALL) + d3 * (a3 - a4))
    w1, w2, w3 = i1 * i1, 6.0 * (i2 * i2), 3.0 * (i3 * i3)
    n1 = 5.0 * d2 - 2.0 * d1
    n2 = d2 + 2.0 * d3
    n3 = 4.0 * d3 - d4
    inverse = quick_inverse(w1 + w2 + w3)
    mean = (w1 * n1 + w2 * n2 + w3 * n3) * inverse
    return (i1, i2, i3), (w1, w2, w3), (n1, n2, n3), inverse, mean, (a1, a2, a3, a4)


def weno_rise(d1, d2, d3, d4):
    return weno_parts(d1, d2, d3, d4)[4]


def weno_pull(d1, d2, d3, d4, cot):
    (i1, i2, i3), (w1, w2, w3), (n1, n2, n3), inverse, mean, (a1, a2, a3, a4) = weno_parts(
        d1, d2, d3, d4
    )
    scaled = cot * inverse * (1.0 / 6.0)
    e1, e2, e3 = w1 * scaled, w2 * scaled, w3 * scaled
    g1 = (e1 * i1) * (2.0 * (mean - n1))
    g2 = (e2 * i2) * (2.0 * (mean - n2))
    g3 = (e3 * i3) * (2.0 * (mean - n3))
    c1 = g1 * (2.0 * d1 - 1.1 * a2) - 2.0 * e1
    c2 = g1 * (2.0 * a2 - a1) + g2 * (2.0 * d2 - 1.25 * d3) + (5.0 * e1 + e2)
    c3 = g2 * (2.0 * d3 - 1.25 * d2) + g3 * (2.0 * a3 - a4) + (2.0 * e2 + 4.0 * e3)
    c4 = g3 * (2.0 * d4 - 1.1 * a3) - e3
    return c1, c2, c3, c4


def split_flux(cells, speed, push, direction):
    fluxes = [cells[1 + direction]]
    for j in range(3):
        momentum_flux = cells[1 + j] * speed
        fluxes.append(momentum_flux + push if j == direction else momentum_flux)
    fluxes.append((cells[4] + push) * speed)
    plus, minus = [], []
    for flux, cell in zip(fluxes, cells):
        half, double = 0.5 * flux, 2.0 * cell
        plus.append(half + double)
        minus.append(half - double)
    return plus, minus


def pull_split_flux(cells, velocity, push, inverse_rho, direction, plus_cot, minus_cot):
    cot = [0.5 * (a + b) for a, b in zip(plus_cot, minus_cot)]
    out = [2.0 * (a - b) for a, b in zip(plus_cot, minus_cot)]
    speed = velocity[direction]
    speed_cot = cot[4] * (cells[4] + push)
    for j in range(3):
        speed_cot = speed_cot + cot[1 + j] * cells[1 + j]
        out[1 + j] = out[1 + j] + cot[1 + j] * speed
    through = cot[4] * speed
    out[4] = out[4] + through
    pull_push(out, velocity, cot[1 + direction] + through)
    speed_cot = speed_cot * inverse_rho
    out[1 + direction] = out[1 + direction] + cot[0] + speed_cot
    out[0] = out[0] - speed_cot * speed
    return out


def pull_push(out, velocity, push_cot):
    scaled = 0.4 * push_cot
    out[4] = out[4] + scaled
    square = velocity[0] * velocity[0] + velocity[1] * velocity[1] + velocity[2] * velocity[2]
    out[0] = out[0] + 0.5 * (scaled * square)
    for j in range(3):
        out[1 + j] = out[1 + j] - scaled * velocity[j]


def fill_prim(padded, prim):
    def body(i, carry):
        row = pl.multiple_of(i * 8, 8)
        cells = [get(padded, c * PLANE + row) for c in range(6)]
        inverse = 1.0 / cells[0]
        velocity = [cells[1 + j] * inverse for j in range(3)]
        kinetic = 0.5 * (
            cells[1] * velocity[0] + cells[2] * velocity[1] + cells[3] * velocity[2]
        )
        push = (HEAT_RATIO - 1.0) * (cells[4] - kinetic)
        thermal = push * inverse
        molecular = MOLECULAR_DRAG * jnp.exp(0.7 * jnp.log(thermal))
        values = velocity + [thermal, molecular + cells[5], push, inverse, molecular]
        for k, value in enumerate(values):
            put(prim, k * PLANE + row, value)
        return carry

    lax.fori_loop(0, 28, body, 0)


def line_layout(direction, front):
    if direction == 0:
        return lambda lead: lead * PITCH + (front + 3), 1
    return lambda lead: lead + (3 * PITCH + front), PITCH


def fill_split(padded, prim, split, direction, front):
    place, stride = line_layout(direction, front)

    def body(lead, carry):
        row = place(lead)
        cells = [get(padded, c * PLANE + row, stride) for c in range(5)]
        speed = get(prim, direction * PLANE + row, stride)
        push = get(prim, 5 * PLANE + row, stride)
        plus, minus = split_flux(cells, speed, push, direction)
        for c in range(5):
            put(split, pl.multiple_of((c * 14 + lead) * 8, 8), plus[c])
            put(split, pl.multiple_of(((5 + c) * 14 + lead) * 8, 8), minus[c])
        return carry

    lax.fori_loop(0, 14, body, 0)


def split_rows(component, lead):
    return pl.multiple_of((component * 14 + lead) * 8, 8)


def line_rate(padded, prim, split, faces, rate, direction, front, first):
    fill_split(padded, prim, split, direction, front)

    def body(f, carry):
        for c in range(5):
            p = [get(split, split_rows(c, f + k)) for k in range(5)]
            m = [get(split, split_rows(5 + c, f + 1 + k)) for k in range(5)]
            dp = [p[k + 1] - p[k] for k in range(4)]
            dm = [m[k + 1] - m[k] for k in range(4)]
            rise = weno_rise(*dp) - weno_rise(dm[3], dm[2], dm[1], dm[0])
            face = (p[2] + m[2]) + (1.0 / 6.0) * rise
            put(faces, pl.multiple_of((c * 9 + f) * 8, 8), face)
        return carry

    lax.fori_loop(0, 9, body, 0)

    def collect(o, carry):
        for c in range(5):
            low = get(faces, pl.multiple_of((c * 9 + o) * 8, 8))
            high = get(faces, pl.multiple_of((c * 9 + o) * 8 + 8, 8))
            if direction == 0:
                row, stride = pl.multiple_of((c * 8 + o) * 8, 8), 1
            else:
                row, stride = c * 64 + o, 8
            value = low - high
            if not first:
                value = value + get(rate, row, stride)
            put(rate, row, value, stride)
        return carry

    lax.fori_loop(0, 8, collect, 0)


def line_pull(padded, prim, split, split_cot, cot, grad, direction, front):
    place, stride = line_layout(direction, front)
    fill_split(padded, prim, split, direction, front)

    def clear(i, carry):
        put(split_cot, pl.multiple_of(i * 8, 8), jnp.zeros((8, 128), jnp.float32))
        return carry

    lax.fori_loop(0, 140, clear, 0)

    def body(f, carry):
        for c in range(5):
            p = [get(split, split_rows(c, f + k)) for k in range(5)]
            m = [get(split, split_rows(5 + c, f + 1 + k)) for k in range(5)]
            dp = [p[k + 1] - p[k] for k in range(4)]
            dm = [m[k + 1] - m[k] for k in range(4)]
            face = get(cot, c * PLANE + place(f + 3), stride) - get(
                cot, c * PLANE + place(f + 2), stride
            )
            c1, c2, c3, c4 = weno_pull(*dp, face)
            for k, value in enumerate((-c1, c1 - c2, (face + c2) - c3, c3 - c4, c4)):
                add(split_cot, split_rows(c, f + k), value)
            c1, c2, c3, c4 = weno_pull(dm[3], dm[2], dm[1], dm[0], -face)
            for k, value in enumerate((-c4, c4 - c3, (face + c3) - c2, c2 - c1, c1)):
                add(split_cot, split_rows(5 + c, f + 1 + k), value)
        return carry

    lax.fori_loop(0, 9, body, 0)

    def finish(lead, carry):
        row = place(lead)
        cells = [get(padded, c * PLANE + row, stride) for c in range(5)]
        velocity = [get(prim, c * PLANE + row, stride) for c in range(3)]
        push = get(prim, 5 * PLANE + row, stride)
        inverse = get(prim, 6 * PLANE + row, stride)
        plus = [get(split_cot, split_rows(c, lead)) for c in range(5)]
        minus = [get(split_cot, split_rows(5 + c, lead)) for c in range(5)]
        out = pull_split_flux(cells, velocity, push, inverse, direction, plus, minus)
        for c in range(5):
            add(grad, c * PLANE + row, out[c], stride)
        return carry

    lax.fori_loop(0, 14, finish, 0)


def column_rate(padded, prim, rate, front):
    def body(o, carry):
        row = (o + 3) * PITCH + (front + 3)
        cells = [get(padded, c * PLANE + row) for c in range(5)]
        plus, minus = split_flux(cells, get(prim, 2 * PLANE + row), get(prim, 5 * PLANE + row), 2)
        for c in range(5):
            dp = ahead(plus[c], 1) - plus[c]
            next_minus = ahead(minus[c], 1)
            dm = next_minus - minus[c]
            rise = weno_rise(ahead(dp, -2), ahead(dp, -1), dp, ahead(dp, 1)) - weno_rise(
                ahead(dm, 2), ahead(dm, 1), dm, ahead(dm, -1)
            )
            face = (plus[c] + next_minus) + (1.0 / 6.0) * rise
            add(rate, pl.multiple_of((c * 8 + o) * 8, 8), ahead(face, -1) - face)
        return carry

    lax.fori_loop(0, 8, body, 0)


def column_pull(padded, prim, cot, grad, front):
    def body(o, carry):
        row = (o + 3) * PITCH + (front + 3)
        cells = [get(padded, c * PLANE + row) for c in range(5)]
        velocity = [get(prim, c * PLANE + row) for c in range(3)]
        push = get(prim, 5 * PLANE + row)
        inverse = get(prim, 6 * PLANE + row)
        plus, minus = split_flux(cells, velocity[2], push, 2)
        plus_cot, minus_cot = [], []
        for c in range(5):
            own = get(cot, c * PLANE + row)
            face = ahead(own, 1) - own
            dp = ahead(plus[c], 1) - plus[c]
            c1, c2, c3, c4 = weno_pull(ahead(dp, -2), ahead(dp, -1), dp, ahead(dp, 1), face)
            total = (c3 + ahead(c1, 2)) + (ahead(c2, 1) + ahead(c4, -1))
            plus_cot.append(face + (ahead(total, -1) - total))
            dm = ahead(minus[c], 1) - minus[c]
            c1, c2, c3, c4 = weno_pull(ahead(dm, 2), ahead(dm, 1), dm, ahead(dm, -1), -face)
            total = (c3 + ahead(c1, -2)) + (ahead(c2, -1) + ahead(c4, 1))
            minus_cot.append(ahead(face + total, -1) - total)
        out = pull_split_flux(cells, velocity, push, inverse, 2, plus_cot, minus_cot)
        for c in range(5):
            add(grad, c * PLANE + row, out[c])
        return carry

    lax.fori_loop(0, 8, body, 0)


def slopes(prim, row, stride, count):
    fields = [get(prim, j * PLANE + row, stride) for j in range(count)]
    table = [[], [], []]
    for j in range(count):
        start = j * PLANE + row
        table[0].append(
            0.5 * (get(prim, start + PITCH, stride) - get(prim, start - PITCH, stride))
        )
        table[1].append(0.5 * (get(prim, start + 1, stride) - get(prim, start - 1, stride)))
        table[2].append(0.5 * (ahead(fields[j], 1) - ahead(fields[j], -1)))
    return fields, table


def strain(table, k, j):
    return table[k][j] + table[j][k]


def viscous_fluxes(prim, row, stride, directions):
    fields, table = slopes(prim, row, stride, 4)
    drag = get(prim, 4 * PLANE + row, stride)
    spread = (2.0 / 3.0) * (table[0][0] + table[1][1] + table[2][2])
    out = {}
    for k in directions:
        stress = []
        for j in range(3):
            shape = strain(table, k, j)
            stress.append(drag * (shape - spread if j == k else shape))
        power = (
            fields[0] * stress[0]
            + fields[1] * stress[1]
            + fields[2] * stress[2]
            + CONDUCTION * (drag * table[k][3])
        )
        out[k] = stress + [power]
    return out


def viscous_rate(prim, flux_x, flux_y, rate, front):
    def store(ref, row, stride, values):
        for c in range(4):
            put(ref, c * PLANE + row, values[c], stride)

    for edge in (2, 11):
        row = edge * PITCH + (front + 3)
        store(flux_x, row, 1, viscous_fluxes(prim, row, 1, (0,))[0])
        row = 3 * PITCH + (front + edge)
        store(flux_y, row, PITCH, viscous_fluxes(prim, row, PITCH, (1,))[1])

    def body(o, carry):
        row = (o + 3) * PITCH + (front + 3)
        values = viscous_fluxes(prim, row, 1, (0, 1, 2))
        store(flux_x, row, 1, values[0])
        store(flux_y, row, 1, values[1])
        for c in range(4):
            change = 0.5 * (ahead(values[2][c], 1) - ahead(values[2][c], -1))
            add(rate, pl.multiple_of(((1 + c) * 8 + o) * 8, 8), change)
        return carry

    lax.fori_loop(0, 8, body, 0)

    def collect(o, carry):
        row = (o + 3) * PITCH + (front + 3)
        for c in range(4):
            start = c * PLANE + row
            change = (get(flux_x, start + PITCH) - get(flux_x, start - PITCH)) + (
                get(flux_y, start + 1) - get(flux_y, start - 1)
            )
            add(rate, pl.multiple_of(((1 + c) * 8 + o) * 8, 8), 0.5 * change)
        return carry

    lax.fori_loop(0, 8, collect, 0)


def total_of(terms):
    out = terms[0]
    for term in terms[1:]:
        out = out + term
    return out


def viscous_pull_at(prim, cot, prim_cot, row, stride, directions):
    fields, table = slopes(prim, row, stride, 4)
    drag = get(prim, 4 * PLANE + row, stride)
    spread = (2.0 / 3.0) * (table[0][0] + table[1][1] + table[2][2])
    field_cot = [[], [], []]
    drag_cot, spread_cot = [], []
    slope_cot = [[[] for _ in range(4)] for _ in range(3)]
    for k in directions:
        flux_cot = []
        for c in range(4):
            start = (1 + c) * PLANE + row
            if k == 2:
                own = get(cot, start, stride)
                flux_cot.append(0.5 * (ahead(own, -1) - ahead(own, 1)))
            else:
                step = PITCH if k == 0 else 1
                flux_cot.append(
                    0.5 * (get(cot, start - step, stride) - get(cot, start + step, stride))
                )
        power = flux_cot[3]
        heat = CONDUCTION * power
        drag_cot.append(heat * table[k][3])
        slope_cot[k][3].append(heat * drag)
        for j in range(3):
            shape = strain(table, k, j)
            if j == k:
                shape = shape - spread
            stress_cot = flux_cot[j] + fields[j] * power
            field_cot[j].append(power * (drag * shape))
            drag_cot.append(stress_cot * shape)
            scaled = drag * stress_cot
            slope_cot[k][j].append(scaled)
            slope_cot[j][k].append(scaled)
            if j == k:
                spread_cot.append(scaled)
    spread_total = (2.0 / 3.0) * total_of(spread_cot)
    for j in range(3):
        slope_cot[j][j].append(-spread_total)
    put(prim_cot, 4 * PLANE + row, total_of(drag_cot), stride)
    for j in range(4):
        start = j * PLANE + row
        here = list(field_cot[j]) if j < 3 else []
        if slope_cot[2][j]:
            value = total_of(slope_cot[2][j])
            here.append(0.5 * (ahead(value, -1) - ahead(value, 1)))
        if here:
            add(prim_cot, start, total_of(here), stride)
        for k, step in ((0, PITCH), (1, 1)):
            if slope_cot[k][j]:
                value = 0.5 * total_of(slope_cot[k][j])
                add(prim_cot, start + step, value, stride)
                add(prim_cot, start - step, -value, stride)


def viscous_pull(prim, cot, prim_cot, grad, front):
    clear_rows(prim_cot, 5 * 28)
    for edge in (2, 11):
        row = edge * PITCH + (front + 3)
        viscous_pull_at(prim, cot, prim_cot, row, 1, (0,))
        row = 3 * PITCH + (front + edge)
        viscous_pull_at(prim, cot, prim_cot, row, PITCH, (1,))

    def body(o, carry):
        row = (o + 3) * PITCH + (front + 3)
        viscous_pull_at(prim, cot, prim_cot, row, 1, (0, 1, 2))
        return carry

    lax.fori_loop(0, 8, body, 0)

    def finish(i, carry):
        row = pl.multiple_of(i * 8, 8)
        velocity = [get(prim, j * PLANE + row) for j in range(3)]
        thermal = get(prim, 3 * PLANE + row)
        inverse = get(prim, 6 * PLANE + row)
        molecular = get(prim, 7 * PLANE + row)
        velocity_cot = [get(prim_cot, j * PLANE + row) for j in range(3)]
        drag_cot = get(prim_cot, 4 * PLANE + row)
        thermal_cot = get(prim_cot, 3 * PLANE + row) + 0.7 * (drag_cot * molecular) / thermal
        out = [get(grad, c * PLANE + row) for c in range(6)]
        push_cot = thermal_cot * inverse
        out[0] = out[0] - push_cot * thermal
        pull_push(out, velocity, push_cot)
        for j in range(3):
            scaled = velocity_cot[j] * inverse
            out[1 + j] = out[1 + j] + scaled
            out[0] = out[0] - scaled * velocity[j]
        out[5] = out[5] + drag_cot
        for c in range(6):
            put(grad, c * PLANE + row, out[c])
        return carry

    lax.fori_loop(0, 28, finish, 0)


def clear_rows(ref, groups):
    def body(i, carry):
        put(ref, pl.multiple_of(i * 8, 8), jnp.zeros((8, 128), jnp.float32))
        return carry

    lax.fori_loop(0, groups, body, 0)


def assemble(padded, own, from_y, from_x, left):
    front, first, outer = frame(left)
    for c in range(6):
        for x in range(8):
            row = c * PLANE + (first + x) * PITCH + front
            put(padded, row + first, get(own, (c * 8 + x) * 8))
            put(padded, row + outer, get(from_y, (c * 8 + x) * 6, count=6), count=6)
        for x in range(6):
            row = c * PLANE + (outer + x) * PITCH
            for half in (0, 8):
                put(padded, row + half, get(from_x, (c * 6 + x) * PITCH + half))


def start_kernel(state, eddy, own, send_y):
    for i in range(40):
        put(own, i * 8, get(state, i * 8))
    for i in range(8):
        put(own, 320 + i * 8, get(eddy, i * 8))
    for i in range(48):
        put(send_y, i * 6, get(own, i * 8 + 2, count=6), count=6)


def side_kernel(left, own, from_y, send_x):
    front, first, outer = frame(left)
    begin = 2 if left else 0
    for c in range(6):
        for x in range(6):
            row = (c * 6 + x) * PITCH + front
            source = c * 8 + begin + x
            put(send_x, row + first, get(own, source * 8))
            put(send_x, row + outer, get(from_y, source * 6, count=6), count=6)


def section_kernel(left, keep, weight, *refs):
    if keep:
        own, from_y, from_x, base, out, send_y = refs[:6]
        padded, prim, split, faces, rate, flux_x, flux_y = refs[6:]
    else:
        own, from_y, from_x, out, send_y = refs[:5]
        padded, prim, split, faces, rate, flux_x, flux_y = refs[5:]
    front, first, outer = frame(left)
    assemble(padded, own, from_y, from_x, left)
    fill_prim(padded, prim)
    line_rate(padded, prim, split, faces, rate, 0, front, True)
    line_rate(padded, prim, split, faces, rate, 1, front, False)
    column_rate(padded, prim, rate, front)
    viscous_rate(prim, flux_x, flux_y, rate, front)
    for x in range(8):
        row = (x + 3) * PITCH + (front + 3)
        for c in range(5):
            place = (c * 8 + x) * 8
            value = weight * get(padded, c * PLANE + row) + (weight * TIME_STEP) * get(rate, place)
            if keep:
                value = value + keep * get(base, place)
            put(out, place, value)
        put(out, (40 + x) * 8, get(padded, 5 * PLANE + row))
    begin = 0 if left else 2
    for i in range(48):
        put(send_y, i * 6, get(out, i * 8 + begin, count=6), count=6)


def pull_section(left, scale, padded, prim, split, split_cot, cot, prim_cot, grad):
    front, first, outer = frame(left)
    fill_prim(padded, prim)
    viscous_pull(prim, cot, prim_cot, grad, front)
    line_pull(padded, prim, split, split_cot, cot, grad, 1, front)
    line_pull(padded, prim, split, split_cot, cot, grad, 0, front)
    column_pull(padded, prim, cot, grad, front)


def hand_back(left, grad, send_x, rest):
    front, first, outer = frame(left)
    for c in range(6):
        for x in range(6):
            for half in (0, 8):
                put(
                    send_x,
                    (c * 6 + x) * PITCH + half,
                    get(grad, c * PLANE + (outer + x) * PITCH + half),
                )
        for x in range(8):
            for half in (0, 8):
                put(
                    rest,
                    (c * 8 + x) * PITCH + half,
                    get(grad, c * PLANE + (first + x) * PITCH + half),
                )


def last_section_kernel(
    own, from_y, from_x, adjoint, adjoint_y, adjoint_x, send_x, rest, *scratch
):
    padded, prim, split, split_cot, cot, prim_cot, grad = scratch
    front, first, outer = frame(True)
    scale = 2.0 / 3.0
    assemble(padded, own, from_y, from_x, True)
    clear_rows(cot, 5 * 28)
    clear_rows(grad, 6 * 28)
    for c in range(5):
        for x in range(5):
            row = c * PLANE + (6 + x) * PITCH + front
            put(cot, row + 3, get(adjoint_y, (c * 8 + x) * 3, count=3), count=3)
            put(cot, row + 6, get(adjoint, (c * 8 + x) * 8, count=5), count=5)
        for x in range(3):
            row = c * PLANE + (3 + x) * PITCH + front
            put(cot, row + 3, get(adjoint_x, (c * 3 + x) * 8))
    for c in range(5):
        for x in range(8):
            row = c * PLANE + (3 + x) * PITCH + (front + 3)
            value = scale * get(cot, row)
            put(grad, row, value)
            put(cot, row, TIME_STEP * value)
    pull_section(True, scale, padded, prim, split, split_cot, cot, prim_cot, grad)
    hand_back(True, grad, send_x, rest)


def adjoint_y_kernel(adjoint, send_y):
    for i in range(40):
        put(send_y, i * 3, get(adjoint, i * 8 + 5, count=3), count=3)


def adjoint_x_kernel(adjoint, from_y, send_x):
    for c in range(5):
        for x in range(3):
            source = c * 8 + 5 + x
            put(send_x, (c * 3 + x) * 8, get(from_y, source * 3, count=3), count=3)
            put(send_x, (c * 3 + x) * 8 + 3, get(adjoint, source * 8, count=5), count=5)


def take_folded(rest, from_y, left):
    begin = 2 if left else 0
    for i in range(48):
        row = i * 8 + begin
        put(rest, row, get(rest, row, count=6) + get(from_y, i * 6, count=6), count=6)


def earlier_section_kernel(left, scale, own, from_y, from_x, rest_in, folded_y, *refs):
    send_x, rest = refs[:2]
    padded, prim, split, split_cot, cot, prim_cot, grad, folded = refs[2:]
    front, first, outer = frame(left)
    assemble(padded, own, from_y, from_x, left)
    clear_rows(cot, 5 * 28)
    clear_rows(grad, 6 * 28)
    for i in range(48):
        put(folded, i * 8, get(rest_in, i * 8))
    take_folded(folded, folded_y, not left)
    for c in range(6):
        for x in range(8):
            row = c * PLANE + (3 + x) * PITCH + (front + 3)
            value = get(folded, (c * 8 + x) * 8)
            if c < 5:
                value = scale * value
                put(cot, row, TIME_STEP * value)
            put(grad, row, value)
    pull_section(left, scale, padded, prim, split, split_cot, cot, prim_cot, grad)
    hand_back(left, grad, send_x, rest)


def fold_kernel(left, rest_in, from_x, rest, send_y, work):
    front, first, outer = frame(left)
    begin = 2 if left else 0
    for c in range(6):
        for x in range(8):
            for half in (0, 8):
                row = (c * 8 + x) * PITCH + half
                value = get(rest_in, row)
                if begin <= x < begin + 6:
                    value = value + get(from_x, (c * 6 + x - begin) * PITCH + half)
                put(work, row, value)
    for i in range(48):
        put(rest, i * 8, get(work, i * PITCH + front + first))
        put(send_y, i * 6, get(work, i * PITCH + front + outer, count=6), count=6)


def end_kernel(adjoint, rest_two, folded_two, rest_zero, folded_zero, grad_state, grad_eddy, work):
    for i in range(40):
        put(work, i * 8, get(rest_two, i * 8))
    for i in range(40):
        row = i * 8 + 2
        put(work, row, get(work, row, count=6) + get(folded_two, i * 6, count=6), count=6)
    for i in range(40):
        value = (1.0 / 3.0) * get(adjoint, i * 8) + 0.75 * get(work, i * 8)
        put(grad_state, i * 8, value + get(rest_zero, i * 8))
        row = i * 8 + 2
        put(
            grad_state,
            row,
            get(grad_state, row, count=6) + get(folded_zero, i * 6, count=6),
            count=6,
        )
    for i in range(8):
        put(grad_eddy, i * 8, get(rest_zero, 320 + i * 8))
        row = i * 8 + 2
        put(
            grad_eddy,
            row,
            get(grad_eddy, row, count=6) + get(folded_zero, (40 + i) * 6, count=6),
            count=6,
        )


def run(kernel, operands, outs, scratch=()):
    return pl.pallas_call(
        kernel,
        out_shape=[jax.ShapeDtypeStruct((rows, 128), jnp.float32) for rows in outs],
        in_specs=[pl.BlockSpec(memory_space=pltpu.VMEM)] * len(operands),
        out_specs=[pl.BlockSpec(memory_space=pltpu.VMEM)] * len(outs),
        scratch_shapes=[pltpu.VMEM((rows, 128), jnp.float32) for rows in scratch],
        compiler_params=pltpu.CompilerParams(vmem_limit_bytes=24 * 1024 * 1024),
    )(*operands)


def shifted(values, axis, up):
    count = lax.axis_size(axis)
    step = 1 if up else count - 1
    return lax.ppermute(values, axis, [(i, (i + step) % count) for i in range(count)])


def pipeline(state, eddy, adjoint):
    section_scratch = (6 * PLANE, 8 * PLANE, 1120, 360, 320, 4 * PLANE, 4 * PLANE)
    pull_scratch = (6 * PLANE, 8 * PLANE, 1120, 1120, 5 * PLANE, 5 * PLANE, 6 * PLANE)

    def surround(own, send_y, left):
        from_y = shifted(send_y, "gy", left)
        (send_x,) = run(functools.partial(side_kernel, left), [own, from_y], [576])
        return own, from_y, shifted(send_x, "gx", left)

    def fold(send_x, rest, left):
        from_x = shifted(send_x, "gx", not left)
        rest, send_y = run(functools.partial(fold_kernel, left), [rest, from_x], [384, 288], [768])
        return rest, shifted(send_y, "gy", not left)

    own, send_y = run(start_kernel, [state, eddy], [384, 288])
    zero = surround(own, send_y, True)
    own, send_y = run(
        functools.partial(section_kernel, True, 0.0, 1.0), list(zero), [384, 288], section_scratch
    )
    one = surround(own, send_y, False)
    own, send_y = run(
        functools.partial(section_kernel, False, 0.75, 0.25),
        [*one, state],
        [384, 288],
        section_scratch,
    )
    two = surround(own, send_y, True)
    (adjoint_send,) = run(adjoint_y_kernel, [adjoint], [120])
    adjoint_y = shifted(adjoint_send, "gy", True)
    (adjoint_send,) = run(adjoint_x_kernel, [adjoint, adjoint_y], [120])
    adjoint_x = shifted(adjoint_send, "gx", True)
    send_x, rest = run(
        last_section_kernel, [*two, adjoint, adjoint_y, adjoint_x], [576, 768], pull_scratch
    )
    rest_two, folded_two = fold(send_x, rest, True)
    send_x, rest = run(
        functools.partial(earlier_section_kernel, False, 0.25),
        [*one, rest_two, folded_two],
        [576, 768],
        pull_scratch + (384,),
    )
    rest_one, folded_one = fold(send_x, rest, False)
    send_x, rest = run(
        functools.partial(earlier_section_kernel, True, 1.0),
        [*zero, rest_one, folded_one],
        [576, 768],
        pull_scratch + (384,),
    )
    rest_zero, folded_zero = fold(send_x, rest, True)
    grad_state, grad_eddy = run(
        end_kernel,
        [adjoint, rest_two, folded_two, rest_zero, folded_zero],
        [320, 64],
        [320],
    )
    return grad_state, grad_eddy


def on_device(state, eddy, adjoint):
    grad_state, grad_eddy = pipeline(
        state.reshape(320, 128), eddy.reshape(64, 128), adjoint.reshape(320, 128)
    )
    return grad_state.reshape(5, 8, 8, 128), grad_eddy.reshape(8, 8, 128)


def solution(mesh):
    placed = (P(None, "gx", "gy", None), P("gx", "gy", None), P(None, "gx", "gy", None))
    return jax.shard_map(
        on_device,
        mesh=mesh,
        in_specs=placed,
        out_specs=(P(None, "gx", "gy", None), P("gx", "gy", None)),
        check_vma=False,
    )
```

```python
import functools

import jax
import jax.numpy as jnp
from jax import lax
from jax.experimental import pallas as pl
from jax.experimental.pallas import tpu as pltpu
from jax.sharding import PartitionSpec as P

HEAT_RATIO = 1.4
MOLECULAR_DRAG = 0.05
PRANDTL = 0.72
TIME_STEP = 0.04
SMOOTH_EPS = 1e-06
CONDUCTION = HEAT_RATIO / ((HEAT_RATIO - 1.0) * PRANDTL)
SMALL = 0.75 * SMOOTH_EPS

PITCH = 16
PLANE = 14 * PITCH


def frame(left):
    return (2, 6, 0) if left else (0, 0, 8)


def get(ref, start, stride=1, count=8):
    if stride == 1:
        return ref[pl.ds(start, count), :]
    return ref[pl.ds(start, count, stride=stride), :]


def put(ref, start, value, stride=1, count=8):
    if stride == 1:
        ref[pl.ds(start, count), :] = value
    else:
        ref[pl.ds(start, count, stride=stride), :] = value


def add(ref, start, value, stride=1, count=8):
    put(ref, start, get(ref, start, stride, count) + value, stride, count)


def ahead(value, offset):
    return pltpu.roll(value, (-offset) % 128, 1)


def quick_inverse(value):
    return pl.reciprocal(value, approx=True)


def loop(count, body, together=1):
    def step(i, carry):
        for k in range(together):
            body(i * together + k)
        return carry

    lax.fori_loop(0, count // together, step, 0)


class Slope:
    def __init__(self, value):
        self.value = value
        self.kept = {}

    def times(self, factor):
        if factor == 1.0:
            return self.value
        if factor not in self.kept:
            self.kept[factor] = factor * self.value
        return self.kept[factor]

    def square(self):
        if 0 not in self.kept:
            self.kept[0] = self.value * self.value + SMALL
        return self.kept[0]


def weno_parts(d1, d2, d3, d4):
    i1 = quick_inverse(d1.square() + d2.value * (d2.times(2.5) - d1.times(2.75)))
    i2 = quick_inverse(d2.square() + d3.value * (d3.value - d2.times(1.25)))
    i3 = quick_inverse(d4.square() + d3.value * (d3.times(2.5) - d4.times(2.75)))
    w1, w2, w3 = i1 * i1, 6.0 * (i2 * i2), 3.0 * (i3 * i3)
    m1 = d2.times(2.5) - d1.value
    m2 = d2.times(0.5) + d3.value
    m3 = d3.times(2.0) - d4.times(0.5)
    inverse = quick_inverse(w1 + w2 + w3)
    mean = (w1 * m1 + w2 * m2 + w3 * m3) * inverse
    return (i1, i2, i3), (w1, w2, w3), (m1, m2, m3), inverse, mean


def weno_rise(d1, d2, d3, d4):
    return weno_parts(d1, d2, d3, d4)[4]


def weno_pull(d1, d2, d3, d4, third):
    (i1, i2, i3), (w1, w2, w3), (m1, m2, m3), inverse, mean = weno_parts(d1, d2, d3, d4)
    scaled = third * inverse
    e1, e2, e3 = w1 * scaled, w2 * scaled, w3 * scaled
    g1 = (e1 * i1) * (mean - m1)
    g2 = (e2 * i2) * (mean - m2)
    g3 = (e3 * i3) * (mean - m3)
    c1 = g1 * (d1.times(4.0) - d2.times(5.5)) - e1
    c2 = g1 * (d2.times(10.0) - d1.times(5.5)) + g2 * (d2.times(4.0) - d3.times(2.5))
    c2 = c2 + (2.5 * e1 + 0.5 * e2)
    c3 = g2 * (d3.times(4.0) - d2.times(2.5)) + g3 * (d3.times(10.0) - d4.times(5.5))
    c3 = c3 + (e2 + 2.0 * e3)
    c4 = g3 * (d4.times(4.0) - d3.times(5.5)) - 0.5 * e3
    return c1, c2, c3, c4


def split_flux(cells, speed, push, direction):
    fluxes = [cells[1 + direction]]
    for j in range(3):
        momentum_flux = cells[1 + j] * speed
        fluxes.append(momentum_flux + push if j == direction else momentum_flux)
    fluxes.append((cells[4] + push) * speed)
    plus, minus = [], []
    for flux, cell in zip(fluxes, cells):
        half, double = 0.5 * flux, 2.0 * cell
        plus.append(half + double)
        minus.append(half - double)
    return plus, minus


def pull_flux(cells, velocity, push, inverse_rho, direction, cot, out):
    speed = velocity[direction]
    speed_cot = cot[4] * (cells[4] + push)
    for j in range(3):
        speed_cot = speed_cot + cot[1 + j] * cells[1 + j]
        out[1 + j] = out[1 + j] + cot[1 + j] * speed
    through = cot[4] * speed
    out[4] = out[4] + through
    pull_push(out, velocity, cot[1 + direction] + through)
    speed_cot = speed_cot * inverse_rho
    out[1 + direction] = out[1 + direction] + cot[0] + speed_cot
    out[0] = out[0] - speed_cot * speed


def pull_push(out, velocity, push_cot):
    scaled = 0.4 * push_cot
    out[4] = out[4] + scaled
    square = velocity[0] * velocity[0] + velocity[1] * velocity[1] + velocity[2] * velocity[2]
    out[0] = out[0] + 0.5 * (scaled * square)
    for j in range(3):
        out[1 + j] = out[1 + j] - scaled * velocity[j]


def fill_prim(padded, prim):
    def body(i):
        row = i * 32
        cells = [get(padded, c * PLANE + row, count=32) for c in range(6)]
        inverse = 1.0 / cells[0]
        velocity = [cells[1 + j] * inverse for j in range(3)]
        kinetic = 0.5 * (
            cells[1] * velocity[0] + cells[2] * velocity[1] + cells[3] * velocity[2]
        )
        push = (HEAT_RATIO - 1.0) * (cells[4] - kinetic)
        thermal = push * inverse
        molecular = MOLECULAR_DRAG * jnp.exp(0.7 * jnp.log(thermal))
        values = velocity + [thermal, molecular + cells[5], push, inverse, molecular]
        for k, value in enumerate(values):
            put(prim, k * PLANE + row, value, count=32)

    loop(7, lambda i: body(pl.multiple_of(i, 1)))


def line_layout(direction, front):
    if direction == 0:
        return lambda lead: lead * PITCH + (front + 3), 1
    return lambda lead: lead + (3 * PITCH + front), PITCH


def fill_split(padded, prim, split, direction, front):
    place, stride = line_layout(direction, front)

    def body(lead):
        row = place(lead)
        cells = [get(padded, c * PLANE + row, stride) for c in range(5)]
        speed = get(prim, direction * PLANE + row, stride)
        push = get(prim, 5 * PLANE + row, stride)
        plus, minus = split_flux(cells, speed, push, direction)
        for c in range(5):
            put(split, (c * 14 + lead) * 8, plus[c])
            put(split, ((5 + c) * 14 + lead) * 8, minus[c])

    for lead in range(14):
        body(lead)


def line_slopes(split, c):
    plus = [get(split, pl.multiple_of((c * 14 + k) * 8, 8)) for k in range(14)]
    minus = [get(split, pl.multiple_of(((5 + c) * 14 + k) * 8, 8)) for k in range(14)]
    plus_slopes = [Slope(plus[k + 1] - plus[k]) for k in range(13)]
    minus_slopes = [Slope(minus[k + 1] - minus[k]) for k in range(13)]
    return plus, minus, plus_slopes, minus_slopes


def line_rate(padded, prim, split, rate, direction, front, first):
    fill_split(padded, prim, split, direction, front)

    def body(c):
        plus, minus, ps, ms = line_slopes(split, c)
        low = None
        for f in range(9):
            rise = weno_rise(*ps[f : f + 4]) - weno_rise(ms[f + 4], ms[f + 3], ms[f + 2], ms[f + 1])
            face = (plus[f + 2] + minus[f + 3]) + (1.0 / 3.0) * rise
            if f:
                row, stride = (c * 64 + (f - 1) * 8, 1) if direction == 0 else (c * 64 + f - 1, 8)
                value = low - face
                if not first:
                    value = value + get(rate, row, stride)
                put(rate, row, value, stride)
            low = face

    loop(5, body)


def line_pull(padded, prim, split, split_cot, cot, grad, direction, front):
    place, stride = line_layout(direction, front)
    fill_split(padded, prim, split, direction, front)

    def body(c):
        _, _, ps, ms = line_slopes(split, c)
        own = [get(cot, c * PLANE + place(lead), stride) for lead in range(2, 12)]
        plus_cot, minus_cot = [None] * 14, [None] * 14

        def gather(table, lead, value):
            table[lead] = value if table[lead] is None else table[lead] + value

        for f in range(9):
            face = own[f + 1] - own[f]
            third = (1.0 / 3.0) * face
            c1, c2, c3, c4 = weno_pull(*ps[f : f + 4], third)
            for k, value in enumerate((-c1, c1 - c2, (face + c2) - c3, c3 - c4, c4)):
                gather(plus_cot, f + k, value)
            c1, c2, c3, c4 = weno_pull(ms[f + 4], ms[f + 3], ms[f + 2], ms[f + 1], -third)
            for k, value in enumerate((-c4, c4 - c3, (face + c3) - c2, c2 - c1, c1)):
                gather(minus_cot, f + 1 + k, value)
            done = range(f, f + 1) if f < 8 else range(8, 14)
            for lead in done:
                p, m = plus_cot[lead], minus_cot[lead]
                if p is None:
                    total, gap = m, -m
                elif m is None:
                    total, gap = p, p
                else:
                    total, gap = p + m, p - m
                put(split_cot, pl.multiple_of((c * 14 + lead) * 8, 8), 0.5 * total)
                put(split_cot, pl.multiple_of(((5 + c) * 14 + lead) * 8, 8), 2.0 * gap)

    loop(5, body)
    for lead in range(14):
        row = place(lead)
        cells = [get(padded, c * PLANE + row, stride) for c in range(5)]
        velocity = [get(prim, c * PLANE + row, stride) for c in range(3)]
        push = get(prim, 5 * PLANE + row, stride)
        inverse = get(prim, 6 * PLANE + row, stride)
        flux_cot = [get(split_cot, (c * 14 + lead) * 8) for c in range(5)]
        out = [get(split_cot, ((5 + c) * 14 + lead) * 8) for c in range(5)]
        pull_flux(cells, velocity, push, inverse, direction, flux_cot, out)
        for c in range(5):
            add(grad, c * PLANE + row, out[c], stride)


def column_rate(padded, prim, rate, front):
    def body(o):
        row = (o + 3) * PITCH + (front + 3)
        cells = [get(padded, c * PLANE + row) for c in range(5)]
        plus, minus = split_flux(cells, get(prim, 2 * PLANE + row), get(prim, 5 * PLANE + row), 2)
        changes = []
        for c in range(5):
            dp = ahead(plus[c], 1) - plus[c]
            next_minus = ahead(minus[c], 1)
            dm = next_minus - minus[c]
            rise = weno_rise(*[Slope(v) for v in (ahead(dp, -2), ahead(dp, -1), dp, ahead(dp, 1))])
            rise = rise - weno_rise(
                *[Slope(v) for v in (ahead(dm, 2), ahead(dm, 1), dm, ahead(dm, -1))]
            )
            face = (plus[c] + next_minus) + (1.0 / 3.0) * rise
            changes.append(ahead(face, -1) - face)
        for c in range(5):
            add(rate, pl.multiple_of((c * 8 + o) * 8, 8), changes[c])

    loop(8, body)


def column_pull(padded, prim, cot, grad, front):
    def body(o):
        row = (o + 3) * PITCH + (front + 3)
        cells = [get(padded, c * PLANE + row) for c in range(5)]
        velocity = [get(prim, c * PLANE + row) for c in range(3)]
        push = get(prim, 5 * PLANE + row)
        inverse = get(prim, 6 * PLANE + row)
        plus, minus = split_flux(cells, velocity[2], push, 2)
        flux_cot, out = [], []
        for c in range(5):
            own = get(cot, c * PLANE + row)
            face = ahead(own, 1) - own
            third = (1.0 / 3.0) * face
            dp = ahead(plus[c], 1) - plus[c]
            c1, c2, c3, c4 = weno_pull(
                *[Slope(v) for v in (ahead(dp, -2), ahead(dp, -1), dp, ahead(dp, 1))], third
            )
            total = (c3 + ahead(c1, 2)) + (ahead(c2, 1) + ahead(c4, -1))
            p = face + (ahead(total, -1) - total)
            dm = ahead(minus[c], 1) - minus[c]
            c1, c2, c3, c4 = weno_pull(
                *[Slope(v) for v in (ahead(dm, 2), ahead(dm, 1), dm, ahead(dm, -1))], -third
            )
            total = (c3 + ahead(c1, -2)) + (ahead(c2, -1) + ahead(c4, 1))
            m = ahead(face + total, -1) - total
            flux_cot.append(0.5 * (p + m))
            out.append(2.0 * (p - m))
        pull_flux(cells, velocity, push, inverse, 2, flux_cot, out)
        for c in range(5):
            add(grad, c * PLANE + row, out[c])

    loop(8, body)


def slopes(prim, row, stride, count):
    fields = [get(prim, j * PLANE + row, stride) for j in range(count)]
    table = [[], [], []]
    for j in range(count):
        start = j * PLANE + row
        table[0].append(
            0.5 * (get(prim, start + PITCH, stride) - get(prim, start - PITCH, stride))
        )
        table[1].append(0.5 * (get(prim, start + 1, stride) - get(prim, start - 1, stride)))
        table[2].append(0.5 * (ahead(fields[j], 1) - ahead(fields[j], -1)))
    return fields, table


def strain(table, k, j):
    return table[k][j] + table[j][k]


def viscous_fluxes(prim, row, stride, directions):
    fields, table = slopes(prim, row, stride, 4)
    drag = get(prim, 4 * PLANE + row, stride)
    spread = (2.0 / 3.0) * (table[0][0] + table[1][1] + table[2][2])
    out = {}
    for k in directions:
        stress = []
        for j in range(3):
            shape = strain(table, k, j)
            stress.append(drag * (shape - spread if j == k else shape))
        power = (
            fields[0] * stress[0]
            + fields[1] * stress[1]
            + fields[2] * stress[2]
            + CONDUCTION * (drag * table[k][3])
        )
        out[k] = stress + [power]
    return out


def viscous_rate(prim, flux_x, flux_y, rate, front):
    def store(ref, row, stride, values):
        for c in range(4):
            put(ref, c * PLANE + row, values[c], stride)

    for edge in (2, 11):
        row = edge * PITCH + (front + 3)
        store(flux_x, row, 1, viscous_fluxes(prim, row, 1, (0,))[0])
        row = 3 * PITCH + (front + edge)
        store(flux_y, row, PITCH, viscous_fluxes(prim, row, PITCH, (1,))[1])

    def body(o):
        row = (o + 3) * PITCH + (front + 3)
        values = viscous_fluxes(prim, row, 1, (0, 1, 2))
        changes = [0.5 * (ahead(value, 1) - ahead(value, -1)) for value in values[2]]
        store(flux_x, row, 1, values[0])
        store(flux_y, row, 1, values[1])
        for c in range(4):
            add(rate, pl.multiple_of(((1 + c) * 8 + o) * 8, 8), changes[c])

    loop(8, body, 2)

    for o in range(8):
        row = (o + 3) * PITCH + (front + 3)
        for c in range(4):
            start = c * PLANE + row
            change = (get(flux_x, start + PITCH) - get(flux_x, start - PITCH)) + (
                get(flux_y, start + 1) - get(flux_y, start - 1)
            )
            add(rate, ((1 + c) * 8 + o) * 8, 0.5 * change)


def total_of(terms):
    out = terms[0]
    for term in terms[1:]:
        out = out + term
    return out


def viscous_pull_at(prim, cot, prim_cot, row, stride, directions):
    fields, table = slopes(prim, row, stride, 4)
    drag = get(prim, 4 * PLANE + row, stride)
    spread = (2.0 / 3.0) * (table[0][0] + table[1][1] + table[2][2])
    field_cot = [[], [], []]
    drag_cot, spread_cot = [], []
    slope_cot = [[[] for _ in range(4)] for _ in range(3)]
    for k in directions:
        flux_cot = []
        for c in range(4):
            start = (1 + c) * PLANE + row
            if k == 2:
                own = get(cot, start, stride)
                flux_cot.append(0.5 * (ahead(own, -1) - ahead(own, 1)))
            else:
                step = PITCH if k == 0 else 1
                flux_cot.append(
                    0.5 * (get(cot, start - step, stride) - get(cot, start + step, stride))
                )
        power = flux_cot[3]
        heat = CONDUCTION * power
        drag_cot.append(heat * table[k][3])
        slope_cot[k][3].append(heat * drag)
        for j in range(3):
            shape = strain(table, k, j)
            if j == k:
                shape = shape - spread
            stress_cot = flux_cot[j] + fields[j] * power
            field_cot[j].append(power * (drag * shape))
            drag_cot.append(stress_cot * shape)
            scaled = drag * stress_cot
            slope_cot[k][j].append(scaled)
            slope_cot[j][k].append(scaled)
            if j == k:
                spread_cot.append(scaled)
    spread_total = (2.0 / 3.0) * total_of(spread_cot)
    for j in range(3):
        slope_cot[j][j].append(-spread_total)
    put(prim_cot, 4 * PLANE + row, total_of(drag_cot), stride)
    for j in range(4):
        here = list(field_cot[j]) if j < 3 else []
        if slope_cot[2][j]:
            value = total_of(slope_cot[2][j])
            here.append(0.5 * (ahead(value, -1) - ahead(value, 1)))
        if here:
            put(prim_cot, j * PLANE + row, total_of(here), stride)
        for k in range(2):
            if slope_cot[k][j]:
                put(
                    prim_cot,
                    (5 + 4 * k + j) * PLANE + row,
                    0.5 * total_of(slope_cot[k][j]),
                    stride,
                )


def viscous_pull(prim, cot, prim_cot, grad, front):
    clear_rows(prim_cot, 13 * PLANE)
    for edge in (2, 11):
        row = edge * PITCH + (front + 3)
        viscous_pull_at(prim, cot, prim_cot, row, 1, (0,))
        row = 3 * PITCH + (front + edge)
        viscous_pull_at(prim, cot, prim_cot, row, PITCH, (1,))

    def body(o):
        row = (o + 3) * PITCH + (front + 3)
        viscous_pull_at(prim, cot, prim_cot, row, 1, (0, 1, 2))

    loop(8, body)

    def finish(i):
        row = i * 16 + 16
        velocity = [get(prim, j * PLANE + row, count=16) for j in range(3)]
        thermal = get(prim, 3 * PLANE + row, count=16)
        inverse = get(prim, 6 * PLANE + row, count=16)
        molecular = get(prim, 7 * PLANE + row, count=16)
        field_cot = []
        for j in range(4):
            start = j * PLANE + row
            along = (5 + j) * PLANE + row
            across = (9 + j) * PLANE + row
            field_cot.append(
                get(prim_cot, start, count=16)
                + (get(prim_cot, along - PITCH, count=16) - get(prim_cot, along + PITCH, count=16))
                + (get(prim_cot, across - 1, count=16) - get(prim_cot, across + 1, count=16))
            )
        drag_cot = get(prim_cot, 4 * PLANE + row, count=16)
        thermal_cot = field_cot[3] + 0.7 * (drag_cot * molecular) / thermal
        out = [get(grad, c * PLANE + row, count=16) for c in range(6)]
        push_cot = thermal_cot * inverse
        out[0] = out[0] - push_cot * thermal
        pull_push(out, velocity, push_cot)
        for j in range(3):
            scaled = field_cot[j] * inverse
            out[1 + j] = out[1 + j] + scaled
            out[0] = out[0] - scaled * velocity[j]
        out[5] = out[5] + drag_cot
        for c in range(6):
            put(grad, c * PLANE + row, out[c], count=16)

    loop(12, finish, 2)


def clear_rows(ref, rows):
    for row in range(0, rows, 32):
        put(ref, row, jnp.zeros((32, 128), jnp.float32), count=32)


X_ROWS = 72


def x_pieces(left):
    pieces, place = [], 0
    for x in range(6):
        near = x >= 3 if left else x < 3
        first, count = (0, 14) if near else (2, 10)
        pieces.append((place, x, first, count))
        place += count
    return pieces


def assemble(padded, own, from_y, from_x, left, components=range(6)):
    front, first, outer = frame(left)
    for c in components:
        for x in range(8):
            row = c * PLANE + (first + x) * PITCH + front
            put(padded, row + first, get(own, (c * 8 + x) * 8))
            put(padded, row + outer, get(from_y, (c * 8 + x) * 6, count=6), count=6)
        for place, x, cell, count in x_pieces(left):
            row = c * PLANE + (outer + x) * PITCH + front + cell
            put(padded, row, get(from_x, c * X_ROWS + place, count=count), count=count)


def start_kernel(state, eddy, own, send_y):
    for i in range(40):
        put(own, i * 8, get(state, i * 8))
    for i in range(8):
        put(own, 320 + i * 8, get(eddy, i * 8))
    for i in range(48):
        put(send_y, i * 6, get(own, i * 8 + 2, count=6), count=6)


def side_kernel(left, components, own, from_y, *refs):
    adjoint = refs[0] if len(refs) > 2 else None
    send_x, line = refs[-2:]
    front, first, outer = frame(left)
    begin = 2 if left else 0
    for c in range(components):
        for x in range(6):
            source = c * 8 + begin + x
            row = (c * 6 + x) * PITCH + front
            put(line, row + first, get(own, source * 8))
            put(line, row + outer, get(from_y, source * 6, count=6), count=6)
        for place, x, cell, count in x_pieces(left):
            value = get(line, (c * 6 + x) * PITCH + front + cell, count=count)
            put(send_x, c * X_ROWS + place, value, count=count)
    if adjoint is not None:
        for c in range(5):
            for x in range(3):
                source = c * 8 + 5 + x
                row = 5 * X_ROWS + (c * 3 + x) * 8
                put(send_x, row, get(from_y, 240 + source * 3, count=3), count=3)
                put(send_x, row + 3, get(adjoint, source * 8, count=5), count=5)


def section_kernel(left, keep, weight, *refs):
    own, from_y, from_x = refs[:3]
    base, adjoint = refs[3:5] if keep else (None, None)
    out, send_y, padded, prim, split, rate, flux_x, flux_y = refs[-8:]
    front, first, outer = frame(left)
    assemble(padded, own, from_y, from_x, left)
    fill_prim(padded, prim)
    line_rate(padded, prim, split, rate, 0, front, True)
    line_rate(padded, prim, split, rate, 1, front, False)
    column_rate(padded, prim, rate, front)
    viscous_rate(prim, flux_x, flux_y, rate, front)
    for x in range(8):
        row = (x + 3) * PITCH + (front + 3)
        for c in range(5):
            place = (c * 8 + x) * 8
            value = weight * get(padded, c * PLANE + row) + (weight * TIME_STEP) * get(rate, place)
            if keep:
                value = value + keep * get(base, place)
            put(out, place, value)
        put(out, (40 + x) * 8, get(padded, 5 * PLANE + row))
    begin = 0 if left else 2
    for i in range(40 if keep else 48):
        put(send_y, i * 6, get(out, i * 8 + begin, count=6), count=6)
    if keep:
        for i in range(40):
            put(send_y, 240 + i * 3, get(adjoint, i * 8 + 5, count=3), count=3)


def pull_section(left, padded, prim, split, split_cot, cot, prim_cot, grad):
    front, first, outer = frame(left)
    fill_prim(padded, prim)
    viscous_pull(prim, cot, prim_cot, grad, front)
    line_pull(padded, prim, split, split_cot, cot, grad, 1, front)
    line_pull(padded, prim, split, split_cot, cot, grad, 0, front)
    column_pull(padded, prim, cot, grad, front)


def hand_back(left, components, grad, send_x, rest):
    front, first, outer = frame(left)
    for c in range(components):
        for place, x, cell, count in x_pieces(left):
            row = c * PLANE + (outer + x) * PITCH + front + cell
            put(send_x, c * X_ROWS + place, get(grad, row, count=count), count=count)
        row = c * PLANE + first * PITCH
        put(rest, c * 128, get(grad, row, count=128), count=128)


def last_section_kernel(own, from_y, from_x, zero_y, zero_x, adjoint, send_x, rest, drag_part, *scratch):
    padded, prim, split, split_cot, cot, prim_cot, grad = scratch
    front, first, outer = frame(True)
    scale = 2.0 / 3.0
    assemble(padded, own, from_y, from_x, True, range(5))
    assemble(padded, own, zero_y, zero_x, True, (5,))
    clear_rows(cot, 5 * PLANE)
    clear_rows(grad, 6 * PLANE)
    for c in range(5):
        for x in range(5):
            row = c * PLANE + (6 + x) * PITCH + front
            put(cot, row + 3, get(from_y, 240 + (c * 8 + x) * 3, count=3), count=3)
            put(cot, row + 6, get(adjoint, (c * 8 + x) * 8, count=5), count=5)
        for x in range(3):
            row = c * PLANE + (3 + x) * PITCH + front
            put(cot, row + 3, get(from_x, 5 * X_ROWS + (c * 3 + x) * 8))
    for c in range(5):
        for x in range(8):
            row = c * PLANE + (3 + x) * PITCH + (front + 3)
            value = scale * get(cot, row)
            put(grad, row, value)
            put(cot, row, TIME_STEP * value)
    pull_section(True, padded, prim, split, split_cot, cot, prim_cot, grad)
    hand_back(True, 5, grad, send_x, rest)
    put(drag_part, 0, get(grad, 5 * PLANE, count=PLANE), count=PLANE)


def earlier_section_kernel(left, scale, own, from_y, from_x, rest_in, folded_y, drag_in, *refs):
    send_x, rest = refs[:2]
    padded, prim, split, split_cot, cot, prim_cot, grad, folded = refs[2:]
    front, first, outer = frame(left)
    assemble(padded, own, from_y, from_x, left)
    clear_rows(cot, 5 * PLANE)
    clear_rows(grad, 5 * PLANE)
    if left:
        put(grad, 5 * PLANE, get(drag_in, 0, count=PLANE), count=PLANE)
    else:
        put(grad, 5 * PLANE, jnp.zeros((PLANE, 128), jnp.float32), count=PLANE)
    components = 6 if left else 5
    begin = 0 if left else 2
    for i in range(8 * components):
        put(folded, i * 8, get(rest_in, i * 8))
        row = i * 8 + begin
        add(folded, row, get(folded_y, i * 6, count=6), count=6)
    for c in range(components):
        for x in range(8):
            row = c * PLANE + (3 + x) * PITCH + (front + 3)
            value = get(folded, (c * 8 + x) * 8)
            if c < 5:
                value = scale * value
                put(cot, row, TIME_STEP * value)
                put(grad, row, value)
            else:
                add(grad, row, value)
    pull_section(left, padded, prim, split, split_cot, cot, prim_cot, grad)
    hand_back(left, 6, grad, send_x, rest)


def fold_kernel(left, components, rest_in, from_x, rest, send_y, work):
    front, first, outer = frame(left)
    begin = 2 if left else 0
    put(work, 0, get(rest_in, 0, count=components * 128), count=components * 128)
    for c in range(components):
        for place, x, cell, count in x_pieces(left):
            row = (c * 8 + begin + x) * PITCH + front + cell
            add(work, row, get(from_x, c * X_ROWS + place, count=count), count=count)
    for i in range(8 * components):
        put(rest, i * 8, get(work, i * PITCH + front + first))
        put(send_y, i * 6, get(work, i * PITCH + front + outer, count=6), count=6)


def end_kernel(adjoint, rest_two, folded_two, rest_zero, folded_zero, grad_state, grad_eddy, work):
    for i in range(40):
        put(work, i * 8, get(rest_two, i * 8))
        row = i * 8 + 2
        add(work, row, get(folded_two, i * 6, count=6), count=6)
    for i in range(40):
        value = (1.0 / 3.0) * get(adjoint, i * 8) + 0.75 * get(work, i * 8)
        put(grad_state, i * 8, value + get(rest_zero, i * 8))
        row = i * 8 + 2
        add(grad_state, row, get(folded_zero, i * 6, count=6), count=6)
    for i in range(8):
        put(grad_eddy, i * 8, get(rest_zero, 320 + i * 8))
        row = i * 8 + 2
        add(grad_eddy, row, get(folded_zero, (40 + i) * 6, count=6), count=6)


def run(kernel, operands, outs, scratch=()):
    return pl.pallas_call(
        kernel,
        out_shape=[jax.ShapeDtypeStruct((rows, 128), jnp.float32) for rows in outs],
        in_specs=[pl.BlockSpec(memory_space=pltpu.VMEM)] * len(operands),
        out_specs=[pl.BlockSpec(memory_space=pltpu.VMEM)] * len(outs),
        scratch_shapes=[pltpu.VMEM((rows, 128), jnp.float32) for rows in scratch],
        compiler_params=pltpu.CompilerParams(vmem_limit_bytes=24 * 1024 * 1024),
    )(*operands)


def shifted(values, axis, up):
    count = lax.axis_size(axis)
    step = 1 if up else count - 1
    return lax.ppermute(values, axis, [(i, (i + step) % count) for i in range(count)])


def pipeline(state, eddy, adjoint):
    section_scratch = (6 * PLANE, 8 * PLANE, 1120, 320, 4 * PLANE, 4 * PLANE)
    pull_scratch = (6 * PLANE, 8 * PLANE, 1120, 1120, 5 * PLANE, 13 * PLANE, 6 * PLANE)

    def surround(own, send_y, left, components=6, more=()):
        from_y = shifted(send_y, "gy", left)
        rows = components * X_ROWS + 120 * len(more)
        (send_x,) = run(
            functools.partial(side_kernel, left, components),
            [own, from_y, *more],
            [rows],
            [components * 6 * PITCH],
        )
        return own, from_y, shifted(send_x, "gx", left)

    def fold(send_x, rest, left, components=6):
        from_x = shifted(send_x, "gx", not left)
        rest, send_y = run(
            functools.partial(fold_kernel, left, components),
            [rest, from_x],
            [64 * components, 48 * components],
            [128 * components],
        )
        return rest, shifted(send_y, "gy", not left)

    own, send_y = run(start_kernel, [state, eddy], [384, 288])
    zero = surround(own, send_y, True)
    own, send_y = run(
        functools.partial(section_kernel, True, 0.0, 1.0), list(zero), [384, 288], section_scratch
    )
    one = surround(own, send_y, False)
    own, send_y = run(
        functools.partial(section_kernel, False, 0.75, 0.25),
        [*one, state, adjoint],
        [384, 360],
        section_scratch,
    )
    two = surround(own, send_y, True, 5, (adjoint,))
    send_x, rest, drag_part = run(
        last_section_kernel,
        [*two, zero[1], zero[2], adjoint],
        [5 * X_ROWS, 5 * 128, PLANE],
        pull_scratch,
    )
    rest_two, folded_two = fold(send_x, rest, True, 5)
    send_x, rest = run(
        functools.partial(earlier_section_kernel, False, 0.25),
        [*one, rest_two, folded_two, drag_part],
        [6 * X_ROWS, 6 * 128],
        pull_scratch + (384,),
    )
    rest_one, folded_one = fold(send_x, rest, False)
    send_x, rest = run(
        functools.partial(earlier_section_kernel, True, 1.0),
        [*zero, rest_one, folded_one, drag_part],
        [6 * X_ROWS, 6 * 128],
        pull_scratch + (384,),
    )
    rest_zero, folded_zero = fold(send_x, rest, True)
    return run(
        end_kernel,
        [adjoint, rest_two, folded_two, rest_zero, folded_zero],
        [320, 64],
        [320],
    )


def on_device(state, eddy, adjoint):
    grad_state, grad_eddy = pipeline(
        state.reshape(320, 128), eddy.reshape(64, 128), adjoint.reshape(320, 128)
    )
    return grad_state.reshape(5, 8, 8, 128), grad_eddy.reshape(8, 8, 128)


def solution(mesh):
    placed = (P(None, "gx", "gy", None), P("gx", "gy", None), P(None, "gx", "gy", None))
    return jax.shard_map(
        on_device,
        mesh=mesh,
        in_specs=placed,
        out_specs=(P(None, "gx", "gy", None), P("gx", "gy", None)),
        check_vma=False,
    )
```

```python
import functools

import jax
import jax.numpy as jnp
from jax import lax
from jax.experimental import pallas as pl
from jax.experimental.pallas import tpu as pltpu
from jax.sharding import PartitionSpec as P

HEAT_RATIO = 1.4
MOLECULAR_DRAG = 0.05
PRANDTL = 0.72
TIME_STEP = 0.04
SMOOTH_EPS = 1e-06
CONDUCTION = HEAT_RATIO / ((HEAT_RATIO - 1.0) * PRANDTL)
SMALL = 0.75 * SMOOTH_EPS

PITCH = 16
PLANE = 14 * PITCH


def frame(left):
    return (2, 6, 0) if left else (0, 0, 8)


def get(ref, start, stride=1, count=8):
    if stride == 1:
        return ref[pl.ds(start, count), :]
    return ref[pl.ds(start, count, stride=stride), :]


def put(ref, start, value, stride=1, count=8):
    if stride == 1:
        ref[pl.ds(start, count), :] = value
    else:
        ref[pl.ds(start, count, stride=stride), :] = value


def add(ref, start, value, stride=1, count=8):
    put(ref, start, get(ref, start, stride, count) + value, stride, count)


def ahead(value, offset):
    return pltpu.roll(value, (-offset) % 128, 1)


def quick_inverse(value):
    return pl.reciprocal(value, approx=True)


def loop(count, body, together=1):
    def step(i, carry):
        for k in range(together):
            body(i * together + k)
        return carry

    lax.fori_loop(0, count // together, step, 0)


class Slope:
    def __init__(self, value):
        self.value = value
        self.kept = {}

    def times(self, factor):
        if factor == 1.0:
            return self.value
        if factor not in self.kept:
            self.kept[factor] = factor * self.value
        return self.kept[factor]

    def square(self):
        if 0 not in self.kept:
            self.kept[0] = self.value * self.value + SMALL
        return self.kept[0]


def weno_parts(d1, d2, d3, d4):
    i1 = quick_inverse(d1.square() + d2.value * (d2.times(2.5) - d1.times(2.75)))
    i2 = quick_inverse(d2.square() + d3.value * (d3.value - d2.times(1.25)))
    i3 = quick_inverse(d4.square() + d3.value * (d3.times(2.5) - d4.times(2.75)))
    w1, w2, w3 = i1 * i1, 6.0 * (i2 * i2), 3.0 * (i3 * i3)
    m1 = d2.times(2.5) - d1.value
    m2 = d2.times(0.5) + d3.value
    m3 = d3.times(2.0) - d4.times(0.5)
    inverse = quick_inverse(w1 + w2 + w3)
    mean = (w1 * m1 + w2 * m2 + w3 * m3) * inverse
    return (i1, i2, i3), (w1, w2, w3), (m1, m2, m3), inverse, mean


def weno_rise(d1, d2, d3, d4):
    return weno_parts(d1, d2, d3, d4)[4]


def weno_pull(d1, d2, d3, d4, third=None):
    (i1, i2, i3), (w1, w2, w3), (m1, m2, m3), inverse, mean = weno_parts(d1, d2, d3, d4)
    scaled = inverse if third is None else third * inverse
    e1, e2, e3 = w1 * scaled, w2 * scaled, w3 * scaled
    g1 = (e1 * i1) * (mean - m1)
    g2 = (e2 * i2) * (mean - m2)
    g3 = (e3 * i3) * (mean - m3)
    c1 = g1 * (d1.times(4.0) - d2.times(5.5)) - e1
    c2 = g1 * (d2.times(10.0) - d1.times(5.5)) + g2 * (d2.times(4.0) - d3.times(2.5))
    c2 = c2 + (2.5 * e1 + 0.5 * e2)
    c3 = g2 * (d3.times(4.0) - d2.times(2.5)) + g3 * (d3.times(10.0) - d4.times(5.5))
    c3 = c3 + (e2 + 2.0 * e3)
    c4 = g3 * (d4.times(4.0) - d3.times(5.5)) - 0.5 * e3
    return c1, c2, c3, c4


def split_flux(cells, speed, push, direction):
    fluxes = [cells[1 + direction]]
    for j in range(3):
        momentum_flux = cells[1 + j] * speed
        fluxes.append(momentum_flux + push if j == direction else momentum_flux)
    fluxes.append((cells[4] + push) * speed)
    plus, minus = [], []
    for flux, cell in zip(fluxes, cells):
        half, double = 0.5 * flux, 2.0 * cell
        plus.append(half + double)
        minus.append(half - double)
    return plus, minus


def pull_flux(cells, velocity, push, inverse_rho, direction, cot, out):
    speed = velocity[direction]
    speed_cot = cot[4] * (cells[4] + push)
    for j in range(3):
        speed_cot = speed_cot + cot[1 + j] * cells[1 + j]
        out[1 + j] = out[1 + j] + cot[1 + j] * speed
    through = cot[4] * speed
    out[4] = out[4] + through
    pull_push(out, velocity, cot[1 + direction] + through)
    speed_cot = speed_cot * inverse_rho
    out[1 + direction] = out[1 + direction] + cot[0] + speed_cot
    out[0] = out[0] - speed_cot * speed


def pull_push(out, velocity, push_cot):
    scaled = 0.4 * push_cot
    out[4] = out[4] + scaled
    square = velocity[0] * velocity[0] + velocity[1] * velocity[1] + velocity[2] * velocity[2]
    out[0] = out[0] + 0.5 * (scaled * square)
    for j in range(3):
        out[1 + j] = out[1 + j] - scaled * velocity[j]


def fill_prim(padded, prim):
    def body(i):
        row = i * 32
        cells = [get(padded, c * PLANE + row, count=32) for c in range(6)]
        inverse = 1.0 / cells[0]
        velocity = [cells[1 + j] * inverse for j in range(3)]
        kinetic = 0.5 * (
            cells[1] * velocity[0] + cells[2] * velocity[1] + cells[3] * velocity[2]
        )
        push = (HEAT_RATIO - 1.0) * (cells[4] - kinetic)
        thermal = push * inverse
        molecular = MOLECULAR_DRAG * jnp.exp(0.7 * jnp.log(thermal))
        values = velocity + [thermal, molecular + cells[5], push, inverse, molecular]
        for k, value in enumerate(values):
            put(prim, k * PLANE + row, value, count=32)

    loop(7, lambda i: body(pl.multiple_of(i, 1)))


def line_layout(direction, front):
    if direction == 0:
        return lambda lead: lead * PITCH + (front + 3), 1
    return lambda lead: lead + (3 * PITCH + front), PITCH


def fill_split(padded, prim, split, direction, front):
    place, stride = line_layout(direction, front)

    def body(lead):
        row = place(lead)
        cells = [get(padded, c * PLANE + row, stride) for c in range(5)]
        speed = get(prim, direction * PLANE + row, stride)
        push = get(prim, 5 * PLANE + row, stride)
        plus, minus = split_flux(cells, speed, push, direction)
        for c in range(5):
            put(split, (c * 14 + lead) * 8, plus[c])
            put(split, ((5 + c) * 14 + lead) * 8, minus[c])

    for lead in range(14):
        body(lead)


def line_slopes(split, c):
    plus = [get(split, pl.multiple_of((c * 14 + k) * 8, 8)) for k in range(14)]
    minus = [get(split, pl.multiple_of(((5 + c) * 14 + k) * 8, 8)) for k in range(14)]
    plus_slopes = [Slope(plus[k + 1] - plus[k]) for k in range(13)]
    minus_slopes = [Slope(minus[k + 1] - minus[k]) for k in range(13)]
    return plus, minus, plus_slopes, minus_slopes


def line_rate(padded, prim, split, rate, direction, front, first):
    fill_split(padded, prim, split, direction, front)

    def body(c):
        plus, minus, ps, ms = line_slopes(split, c)
        low = None
        for f in range(9):
            rise = weno_rise(*ps[f : f + 4]) - weno_rise(ms[f + 4], ms[f + 3], ms[f + 2], ms[f + 1])
            face = (plus[f + 2] + minus[f + 3]) + (1.0 / 3.0) * rise
            if f:
                row, stride = (c * 64 + (f - 1) * 8, 1) if direction == 0 else (c * 64 + f - 1, 8)
                value = low - face
                if not first:
                    value = value + get(rate, row, stride)
                put(rate, row, value, stride)
            low = face

    loop(5, body)


def line_tangent(padded, prim, split, tangent, direction, front):
    fill_split(padded, prim, split, direction, front)

    def body(c):
        _, _, ps, ms = line_slopes(split, c)
        for f in range(9):
            plus = weno_pull(*ps[f : f + 4])
            minus = weno_pull(ms[f + 4], ms[f + 3], ms[f + 2], ms[f + 1])
            for k, value in enumerate(plus + minus):
                put(tangent, pl.multiple_of((c * 9 + f) * 64, 8) + k * 8, value)

    loop(5, body)


def line_pull(padded, prim, split, split_cot, cot, grad, direction, front, tangent=None):
    place, stride = line_layout(direction, front)
    if tangent is None:
        fill_split(padded, prim, split, direction, front)

    def body(c):
        if tangent is None:
            _, _, ps, ms = line_slopes(split, c)
        own = [get(cot, c * PLANE + place(lead), stride) for lead in range(2, 12)]
        plus_cot, minus_cot = [None] * 14, [None] * 14

        def gather(table, lead, value):
            table[lead] = value if table[lead] is None else table[lead] + value

        for f in range(9):
            face = own[f + 1] - own[f]
            third = (1.0 / 3.0) * face
            if tangent is None:
                plus = weno_pull(*ps[f : f + 4], third)
                minus = weno_pull(ms[f + 4], ms[f + 3], ms[f + 2], ms[f + 1], -third)
            else:
                first = pl.multiple_of((c * 9 + f) * 64, 8)
                plus = [third * get(tangent, first + k * 8) for k in range(4)]
                minus = [-third * get(tangent, first + k * 8) for k in range(4, 8)]
            c1, c2, c3, c4 = plus
            for k, value in enumerate((-c1, c1 - c2, (face + c2) - c3, c3 - c4, c4)):
                gather(plus_cot, f + k, value)
            c1, c2, c3, c4 = minus
            for k, value in enumerate((-c4, c4 - c3, (face + c3) - c2, c2 - c1, c1)):
                gather(minus_cot, f + 1 + k, value)
            done = range(f, f + 1) if f < 8 else range(8, 14)
            for lead in done:
                p, m = plus_cot[lead], minus_cot[lead]
                if p is None:
                    total, gap = m, -m
                elif m is None:
                    total, gap = p, p
                else:
                    total, gap = p + m, p - m
                put(split_cot, pl.multiple_of((c * 14 + lead) * 8, 8), 0.5 * total)
                put(split_cot, pl.multiple_of(((5 + c) * 14 + lead) * 8, 8), 2.0 * gap)

    loop(5, body)
    for lead in range(14):
        row = place(lead)
        cells = [get(padded, c * PLANE + row, stride) for c in range(5)]
        velocity = [get(prim, c * PLANE + row, stride) for c in range(3)]
        push = get(prim, 5 * PLANE + row, stride)
        inverse = get(prim, 6 * PLANE + row, stride)
        flux_cot = [get(split_cot, (c * 14 + lead) * 8) for c in range(5)]
        out = [get(split_cot, ((5 + c) * 14 + lead) * 8) for c in range(5)]
        pull_flux(cells, velocity, push, inverse, direction, flux_cot, out)
        for c in range(5):
            add(grad, c * PLANE + row, out[c], stride)


def column_rate(padded, prim, rate, front):
    def body(o):
        row = (o + 3) * PITCH + (front + 3)
        cells = [get(padded, c * PLANE + row) for c in range(5)]
        plus, minus = split_flux(cells, get(prim, 2 * PLANE + row), get(prim, 5 * PLANE + row), 2)
        changes = []
        for c in range(5):
            dp = ahead(plus[c], 1) - plus[c]
            next_minus = ahead(minus[c], 1)
            dm = next_minus - minus[c]
            rise = weno_rise(*[Slope(v) for v in (ahead(dp, -2), ahead(dp, -1), dp, ahead(dp, 1))])
            rise = rise - weno_rise(
                *[Slope(v) for v in (ahead(dm, 2), ahead(dm, 1), dm, ahead(dm, -1))]
            )
            face = (plus[c] + next_minus) + (1.0 / 3.0) * rise
            changes.append(ahead(face, -1) - face)
        for c in range(5):
            add(rate, pl.multiple_of((c * 8 + o) * 8, 8), changes[c])

    loop(8, body, 4)


def column_slopes(plus, minus):
    dp = ahead(plus, 1) - plus
    dm = ahead(minus, 1) - minus
    return (
        [Slope(value) for value in (ahead(dp, -2), ahead(dp, -1), dp, ahead(dp, 1))],
        [Slope(value) for value in (ahead(dm, 2), ahead(dm, 1), dm, ahead(dm, -1))],
    )


def column_tangent(padded, prim, tangent, front):
    def body(o):
        row = (o + 3) * PITCH + (front + 3)
        cells = [get(padded, c * PLANE + row) for c in range(5)]
        plus, minus = split_flux(cells, get(prim, 2 * PLANE + row), get(prim, 5 * PLANE + row), 2)
        for c in range(5):
            ps, ms = column_slopes(plus[c], minus[c])
            for k, value in enumerate(weno_pull(*ps) + weno_pull(*ms)):
                put(tangent, pl.multiple_of((c * 8 + o) * 64, 8) + k * 8, value)

    loop(8, body, 4)


def column_cot(cells, velocity, push, inverse, cot, factors=None):
    if factors is None:
        plus, minus = split_flux(cells, velocity[2], push, 2)
    flux_cot, out = [], []
    for c in range(5):
        face = ahead(cot[c], 1) - cot[c]
        third = (1.0 / 3.0) * face
        if factors is None:
            ps, ms = column_slopes(plus[c], minus[c])
            plus_parts, minus_parts = weno_pull(*ps, third), weno_pull(*ms, -third)
        else:
            plus_parts = [third * value for value in factors[c][:4]]
            minus_parts = [-third * value for value in factors[c][4:]]
        c1, c2, c3, c4 = plus_parts
        total = (c3 + ahead(c1, 2)) + (ahead(c2, 1) + ahead(c4, -1))
        p = face + (ahead(total, -1) - total)
        c1, c2, c3, c4 = minus_parts
        total = (c3 + ahead(c1, -2)) + (ahead(c2, -1) + ahead(c4, 1))
        m = ahead(face + total, -1) - total
        flux_cot.append(0.5 * (p + m))
        out.append(2.0 * (p - m))
    pull_flux(cells, velocity, push, inverse, 2, flux_cot, out)
    return out


def column_pull(padded, prim, cot, grad, front, tangent):
    def body(o):
        row = (o + 3) * PITCH + (front + 3)
        cells = [get(padded, c * PLANE + row) for c in range(5)]
        velocity = [get(prim, c * PLANE + row) for c in range(3)]
        push = get(prim, 5 * PLANE + row)
        inverse = get(prim, 6 * PLANE + row)
        own = [get(cot, c * PLANE + row) for c in range(5)]
        factors = []
        for c in range(5):
            first = pl.multiple_of((c * 8 + o) * 64, 8)
            factors.append([get(tangent, first + k * 8) for k in range(8)])
        out = column_cot(cells, velocity, push, inverse, own, factors)
        for c in range(5):
            add(grad, c * PLANE + row, out[c])

    loop(8, body, 4)


def slopes(prim, row, stride, count):
    fields = [get(prim, j * PLANE + row, stride) for j in range(count)]
    table = [[], [], []]
    for j in range(count):
        start = j * PLANE + row
        table[0].append(
            0.5 * (get(prim, start + PITCH, stride) - get(prim, start - PITCH, stride))
        )
        table[1].append(0.5 * (get(prim, start + 1, stride) - get(prim, start - 1, stride)))
        table[2].append(0.5 * (ahead(fields[j], 1) - ahead(fields[j], -1)))
    return fields, table


def strain(table, k, j):
    return table[k][j] + table[j][k]


def viscous_fluxes(prim, row, stride, directions):
    fields, table = slopes(prim, row, stride, 4)
    drag = get(prim, 4 * PLANE + row, stride)
    spread = (2.0 / 3.0) * (table[0][0] + table[1][1] + table[2][2])
    out = {}
    for k in directions:
        stress = []
        for j in range(3):
            shape = strain(table, k, j)
            stress.append(drag * (shape - spread if j == k else shape))
        power = (
            fields[0] * stress[0]
            + fields[1] * stress[1]
            + fields[2] * stress[2]
            + CONDUCTION * (drag * table[k][3])
        )
        out[k] = stress + [power]
    return out


def viscous_rate(prim, flux_x, flux_y, rate, front):
    def store(ref, row, stride, values):
        for c in range(4):
            put(ref, c * PLANE + row, values[c], stride)

    for edge in (2, 11):
        row = edge * PITCH + (front + 3)
        store(flux_x, row, 1, viscous_fluxes(prim, row, 1, (0,))[0])
        row = 3 * PITCH + (front + edge)
        store(flux_y, row, PITCH, viscous_fluxes(prim, row, PITCH, (1,))[1])

    def body(o):
        row = (o + 3) * PITCH + (front + 3)
        values = viscous_fluxes(prim, row, 1, (0, 1, 2))
        changes = [0.5 * (ahead(value, 1) - ahead(value, -1)) for value in values[2]]
        store(flux_x, row, 1, values[0])
        store(flux_y, row, 1, values[1])
        for c in range(4):
            add(rate, pl.multiple_of(((1 + c) * 8 + o) * 8, 8), changes[c])

    loop(8, body, 2)

    for o in range(8):
        row = (o + 3) * PITCH + (front + 3)
        for c in range(4):
            start = c * PLANE + row
            change = (get(flux_x, start + PITCH) - get(flux_x, start - PITCH)) + (
                get(flux_y, start + 1) - get(flux_y, start - 1)
            )
            add(rate, ((1 + c) * 8 + o) * 8, 0.5 * change)


def total_of(terms):
    out = terms[0]
    for term in terms[1:]:
        out = out + term
    return out


def viscous_pull_at(prim, cot, prim_cot, row, stride, directions):
    fields, table = slopes(prim, row, stride, 4)
    drag = get(prim, 4 * PLANE + row, stride)
    spread = (2.0 / 3.0) * (table[0][0] + table[1][1] + table[2][2])
    field_cot = [[], [], []]
    drag_cot, spread_cot = [], []
    slope_cot = [[[] for _ in range(4)] for _ in range(3)]
    for k in directions:
        flux_cot = []
        for c in range(4):
            start = (1 + c) * PLANE + row
            if k == 2:
                own = get(cot, start, stride)
                flux_cot.append(0.5 * (ahead(own, -1) - ahead(own, 1)))
            else:
                step = PITCH if k == 0 else 1
                flux_cot.append(
                    0.5 * (get(cot, start - step, stride) - get(cot, start + step, stride))
                )
        power = flux_cot[3]
        heat = CONDUCTION * power
        drag_cot.append(heat * table[k][3])
        slope_cot[k][3].append(heat * drag)
        for j in range(3):
            shape = strain(table, k, j)
            if j == k:
                shape = shape - spread
            stress_cot = flux_cot[j] + fields[j] * power
            field_cot[j].append(power * (drag * shape))
            drag_cot.append(stress_cot * shape)
            scaled = drag * stress_cot
            slope_cot[k][j].append(scaled)
            slope_cot[j][k].append(scaled)
            if j == k:
                spread_cot.append(scaled)
    spread_total = (2.0 / 3.0) * total_of(spread_cot)
    for j in range(3):
        slope_cot[j][j].append(-spread_total)
    put(prim_cot, 4 * PLANE + row, total_of(drag_cot), stride)
    for j in range(4):
        here = list(field_cot[j]) if j < 3 else []
        if slope_cot[2][j]:
            value = total_of(slope_cot[2][j])
            here.append(0.5 * (ahead(value, -1) - ahead(value, 1)))
        if here:
            put(prim_cot, j * PLANE + row, total_of(here), stride)
        for k in range(2):
            if slope_cot[k][j]:
                put(
                    prim_cot,
                    (5 + 4 * k + j) * PLANE + row,
                    0.5 * total_of(slope_cot[k][j]),
                    stride,
                )


def viscous_pull(prim, cot, prim_cot, grad, front):
    clear_rows(prim_cot, 13 * PLANE)
    for edge in (2, 11):
        row = edge * PITCH + (front + 3)
        viscous_pull_at(prim, cot, prim_cot, row, 1, (0,))
        row = 3 * PITCH + (front + edge)
        viscous_pull_at(prim, cot, prim_cot, row, PITCH, (1,))

    def body(o):
        row = (o + 3) * PITCH + (front + 3)
        viscous_pull_at(prim, cot, prim_cot, row, 1, (0, 1, 2))

    loop(8, body)

    def finish(i):
        row = i * 16 + 16
        velocity = [get(prim, j * PLANE + row, count=16) for j in range(3)]
        thermal = get(prim, 3 * PLANE + row, count=16)
        inverse = get(prim, 6 * PLANE + row, count=16)
        molecular = get(prim, 7 * PLANE + row, count=16)
        field_cot = []
        for j in range(4):
            start = j * PLANE + row
            along = (5 + j) * PLANE + row
            across = (9 + j) * PLANE + row
            field_cot.append(
                get(prim_cot, start, count=16)
                + (get(prim_cot, along - PITCH, count=16) - get(prim_cot, along + PITCH, count=16))
                + (get(prim_cot, across - 1, count=16) - get(prim_cot, across + 1, count=16))
            )
        drag_cot = get(prim_cot, 4 * PLANE + row, count=16)
        thermal_cot = field_cot[3] + 0.7 * (drag_cot * molecular) / thermal
        out = [get(grad, c * PLANE + row, count=16) for c in range(6)]
        push_cot = thermal_cot * inverse
        out[0] = out[0] - push_cot * thermal
        pull_push(out, velocity, push_cot)
        for j in range(3):
            scaled = field_cot[j] * inverse
            out[1 + j] = out[1 + j] + scaled
            out[0] = out[0] - scaled * velocity[j]
        out[5] = out[5] + drag_cot
        for c in range(6):
            put(grad, c * PLANE + row, out[c], count=16)

    loop(12, finish, 2)


def clear_rows(ref, rows):
    for row in range(0, rows, 32):
        put(ref, row, jnp.zeros((32, 128), jnp.float32), count=32)


X_ROWS = 72


def x_pieces(left):
    pieces, place = [], 0
    for x in range(6):
        near = x >= 3 if left else x < 3
        first, count = (0, 14) if near else (2, 10)
        pieces.append((place, x, first, count))
        place += count
    return pieces


def assemble(padded, own, from_y, from_x, left, components=range(6)):
    front, first, outer = frame(left)
    for c in components:
        for x in range(8):
            row = c * PLANE + (first + x) * PITCH + front
            put(padded, row + first, get(own, (c * 8 + x) * 8))
            put(padded, row + outer, get(from_y, (c * 8 + x) * 6, count=6), count=6)
        for place, x, cell, count in x_pieces(left):
            row = c * PLANE + (outer + x) * PITCH + front + cell
            put(padded, row, get(from_x, c * X_ROWS + place, count=count), count=count)


def start_kernel(state, eddy, own, send_y):
    for i in range(40):
        put(own, i * 8, get(state, i * 8))
    for i in range(8):
        put(own, 320 + i * 8, get(eddy, i * 8))
    for i in range(48):
        put(send_y, i * 6, get(own, i * 8 + 2, count=6), count=6)


def side_kernel(left, components, own, from_y, *refs):
    adjoint = refs[0] if len(refs) > 2 else None
    send_x, line = refs[-2:]
    front, first, outer = frame(left)
    begin = 2 if left else 0
    for c in range(components):
        for x in range(6):
            source = c * 8 + begin + x
            row = (c * 6 + x) * PITCH + front
            put(line, row + first, get(own, source * 8))
            put(line, row + outer, get(from_y, source * 6, count=6), count=6)
        for place, x, cell, count in x_pieces(left):
            value = get(line, (c * 6 + x) * PITCH + front + cell, count=count)
            put(send_x, c * X_ROWS + place, value, count=count)
    if adjoint is not None:
        for c in range(5):
            for x in range(3):
                source = c * 8 + 5 + x
                row = 5 * X_ROWS + (c * 3 + x) * 8
                put(send_x, row, get(from_y, 240 + source * 3, count=3), count=3)
                put(send_x, row + 3, get(adjoint, source * 8, count=5), count=5)


def section_kernel(left, keep, weight, *refs):
    own, from_y, from_x = refs[:3]
    base, adjoint = refs[3:5] if keep else (None, None)
    out, send_y, padded, prim, split, rate, flux_x, flux_y = refs[-8:]
    front, first, outer = frame(left)
    assemble(padded, own, from_y, from_x, left)
    fill_prim(padded, prim)
    line_rate(padded, prim, split, rate, 0, front, True)
    line_rate(padded, prim, split, rate, 1, front, False)
    column_rate(padded, prim, rate, front)
    viscous_rate(prim, flux_x, flux_y, rate, front)
    for x in range(8):
        row = (x + 3) * PITCH + (front + 3)
        for c in range(5):
            place = (c * 8 + x) * 8
            value = weight * get(padded, c * PLANE + row) + (weight * TIME_STEP) * get(rate, place)
            if keep:
                value = value + keep * get(base, place)
            put(out, place, value)
        put(out, (40 + x) * 8, get(padded, 5 * PLANE + row))
    begin = 0 if left else 2
    for i in range(40 if keep else 48):
        put(send_y, i * 6, get(out, i * 8 + begin, count=6), count=6)
    if keep:
        for i in range(40):
            put(send_y, 240 + i * 3, get(adjoint, i * 8 + 5, count=3), count=3)


def tangent_kernel(left, own, from_y, from_x, padded, prim, tangent, split):
    front = frame(left)[0]
    assemble(padded, own, from_y, from_x, left)
    fill_prim(padded, prim)
    line_tangent(padded, prim, split, tangent, 0, front)


def line_tangent_kernel(left, padded, prim, tangent, split):
    line_tangent(padded, prim, split, tangent, 1, frame(left)[0])


def column_tangent_kernel(left, padded, prim, tangent):
    column_tangent(padded, prim, tangent, frame(left)[0])


def own_column_kernel(own, adjoint, part):
    def body(x):
        rows = [pl.multiple_of((c * 8 + x) * 8, 8) for c in range(5)]
        cells = [get(own, row) for row in rows]
        inverse = 1.0 / cells[0]
        velocity = [cells[1 + j] * inverse for j in range(3)]
        kinetic = 0.5 * (
            cells[1] * velocity[0] + cells[2] * velocity[1] + cells[3] * velocity[2]
        )
        push = (HEAT_RATIO - 1.0) * (cells[4] - kinetic)
        cot = [(2.0 / 3.0 * TIME_STEP) * get(adjoint, row) for row in rows]
        out = column_cot(cells, velocity, push, inverse, cot)
        for row, value in zip(rows, out):
            put(part, row, value)

    loop(8, body, 4)


def hand_back(left, components, grad, send_x, rest):
    front, first, outer = frame(left)
    for c in range(components):
        for place, x, cell, count in x_pieces(left):
            row = c * PLANE + (outer + x) * PITCH + front + cell
            put(send_x, c * X_ROWS + place, get(grad, row, count=count), count=count)
        row = c * PLANE + first * PITCH
        put(rest, c * 128, get(grad, row, count=128), count=128)


def last_section_kernel(own, from_y, from_x, zero_y, zero_x, adjoint, send_x, rest, drag_part, *scratch):
    padded, prim, split, split_cot, cot, prim_cot, grad = scratch
    front, first, outer = frame(True)
    scale = 2.0 / 3.0
    assemble(padded, own, from_y, from_x, True, range(5))
    assemble(padded, own, zero_y, zero_x, True, (5,))
    clear_rows(cot, 5 * PLANE)
    clear_rows(grad, 6 * PLANE)
    for c in range(5):
        for x in range(5):
            row = c * PLANE + (6 + x) * PITCH + front
            put(cot, row + 3, get(from_y, 240 + (c * 8 + x) * 3, count=3), count=3)
            put(cot, row + 6, get(adjoint, (c * 8 + x) * 8, count=5), count=5)
        for x in range(3):
            row = c * PLANE + (3 + x) * PITCH + front
            put(cot, row + 3, get(from_x, 5 * X_ROWS + (c * 3 + x) * 8))
    for c in range(5):
        for x in range(8):
            row = c * PLANE + (3 + x) * PITCH + (front + 3)
            value = scale * get(cot, row)
            put(grad, row, value)
            put(cot, row, TIME_STEP * value)
    fill_prim(padded, prim)
    viscous_pull(prim, cot, prim_cot, grad, front)
    line_pull(padded, prim, split, split_cot, cot, grad, 1, front)
    line_pull(padded, prim, split, split_cot, cot, grad, 0, front)
    hand_back(True, 5, grad, send_x, rest)
    put(drag_part, 0, get(grad, 5 * PLANE, count=PLANE), count=PLANE)


def earlier_section_kernel(left, scale, padded, prim, along_x, along_y, along_z, *refs):
    rest_in, folded_y, drag_in, send_x, rest, split_cot, cot, prim_cot, grad, folded = refs
    front, first, outer = frame(left)
    clear_rows(cot, 5 * PLANE)
    clear_rows(grad, 5 * PLANE)
    if left:
        put(grad, 5 * PLANE, get(drag_in, 0, count=PLANE), count=PLANE)
    else:
        put(grad, 5 * PLANE, jnp.zeros((PLANE, 128), jnp.float32), count=PLANE)
    components = 6 if left else 5
    begin = 0 if left else 2
    for i in range(8 * components):
        put(folded, i * 8, get(rest_in, i * 8))
        row = i * 8 + begin
        add(folded, row, get(folded_y, i * 6, count=6), count=6)
    for c in range(components):
        for x in range(8):
            row = c * PLANE + (3 + x) * PITCH + (front + 3)
            value = get(folded, (c * 8 + x) * 8)
            if c < 5:
                value = scale * value
                put(cot, row, TIME_STEP * value)
                put(grad, row, value)
            else:
                add(grad, row, value)
    viscous_pull(prim, cot, prim_cot, grad, front)
    line_pull(padded, prim, None, split_cot, cot, grad, 1, front, along_y)
    line_pull(padded, prim, None, split_cot, cot, grad, 0, front, along_x)
    column_pull(padded, prim, cot, grad, front, along_z)
    hand_back(left, 6, grad, send_x, rest)


def fold_kernel(left, components, rest_in, from_x, *refs):
    part = refs[0] if len(refs) > 3 else None
    rest, send_y, work = refs[-3:]
    front, first, outer = frame(left)
    begin = 2 if left else 0
    put(work, 0, get(rest_in, 0, count=components * 128), count=components * 128)
    for c in range(components):
        for place, x, cell, count in x_pieces(left):
            row = (c * 8 + begin + x) * PITCH + front + cell
            add(work, row, get(from_x, c * X_ROWS + place, count=count), count=count)
    for i in range(8 * components):
        value = get(work, i * PITCH + front + first)
        put(rest, i * 8, value if part is None else value + get(part, i * 8))
        put(send_y, i * 6, get(work, i * PITCH + front + outer, count=6), count=6)


def end_kernel(adjoint, rest_two, folded_two, rest_zero, folded_zero, grad_state, grad_eddy, work):
    for i in range(40):
        put(work, i * 8, get(rest_two, i * 8))
        row = i * 8 + 2
        add(work, row, get(folded_two, i * 6, count=6), count=6)
    for i in range(40):
        value = (1.0 / 3.0) * get(adjoint, i * 8) + 0.75 * get(work, i * 8)
        put(grad_state, i * 8, value + get(rest_zero, i * 8))
        row = i * 8 + 2
        add(grad_state, row, get(folded_zero, i * 6, count=6), count=6)
    for i in range(8):
        put(grad_eddy, i * 8, get(rest_zero, 320 + i * 8))
        row = i * 8 + 2
        add(grad_eddy, row, get(folded_zero, (40 + i) * 6, count=6), count=6)


def run(kernel, operands, outs, scratch=(), work=0):
    cost = pl.CostEstimate(flops=work, bytes_accessed=4 * work, transcendentals=0) if work else None
    return pl.pallas_call(
        kernel,
        out_shape=[jax.ShapeDtypeStruct((rows, 128), jnp.float32) for rows in outs],
        in_specs=[pl.BlockSpec(memory_space=pltpu.VMEM)] * len(operands),
        out_specs=[pl.BlockSpec(memory_space=pltpu.VMEM)] * len(outs),
        scratch_shapes=[pltpu.VMEM((rows, 128), jnp.float32) for rows in scratch],
        compiler_params=pltpu.CompilerParams(vmem_limit_bytes=20 * 1024 * 1024),
        cost_estimate=cost,
    )(*operands)


def shifted(values, axis, up):
    count = lax.axis_size(axis)
    step = 1 if up else count - 1
    return lax.ppermute(values, axis, [(i, (i + step) % count) for i in range(count)])


def together(*values):
    return lax.optimization_barrier(values)


def shifted_beside(values, axis, up, kernel, operands, outs, scratch=()):
    values, *operands = together(values, *operands)
    moved = shifted(values, axis, up)
    moved, *results = together(moved, *run(kernel, operands, outs, scratch, 2_000_000))
    return moved, results


def pipeline(state, eddy, adjoint):
    section_scratch = (6 * PLANE, 8 * PLANE, 1120, 320, 4 * PLANE, 4 * PLANE)
    last_scratch = (6 * PLANE, 8 * PLANE, 1120, 1120, 5 * PLANE, 13 * PLANE, 6 * PLANE)
    earlier_scratch = (1120, 5 * PLANE, 13 * PLANE, 6 * PLANE, 384)
    first_tangent = [6 * PLANE, 8 * PLANE, 2880]

    def sides(own, from_y, left, components=6, more=()):
        (send_x,) = run(
            functools.partial(side_kernel, left, components),
            [own, from_y, *more],
            [components * X_ROWS + 120 * len(more)],
            [components * 6 * PITCH],
        )
        return send_x

    def fold(rest, from_x, left, components=6, more=()):
        return run(
            functools.partial(fold_kernel, left, components),
            [rest, from_x, *more],
            [64 * components, 48 * components],
            [128 * components],
        )

    own, send_y = run(start_kernel, [state, eddy], [384, 288])
    zero_y = shifted(send_y, "gy", True)
    zero_x = shifted(sides(own, zero_y, True), "gx", True)
    zero = own, zero_y, zero_x
    own, send_y = run(
        functools.partial(section_kernel, True, 0.0, 1.0), list(zero), [384, 288], section_scratch
    )
    one_y, (zero_cells, zero_prim, zero_along_x) = shifted_beside(
        send_y, "gy", False, functools.partial(tangent_kernel, True), zero, first_tangent, [1120]
    )
    one_x, (zero_along_y,) = shifted_beside(
        sides(own, one_y, False),
        "gx",
        False,
        functools.partial(line_tangent_kernel, True),
        [zero_cells, zero_prim],
        [2880],
        [1120],
    )
    one = own, one_y, one_x
    own, send_y = run(
        functools.partial(section_kernel, False, 0.75, 0.25),
        [*one, state, adjoint],
        [384, 360],
        section_scratch,
    )
    two_y, (column_part,) = shifted_beside(
        send_y, "gy", True, own_column_kernel, [own, adjoint], [320]
    )
    two_x, (one_cells, one_prim, one_along_x) = shifted_beside(
        sides(own, two_y, True, 5, (adjoint,)),
        "gx",
        True,
        functools.partial(tangent_kernel, False),
        one,
        first_tangent,
        [1120],
    )
    send_x, rest, drag_part = run(
        last_section_kernel,
        [own, two_y, two_x, zero_y, zero_x, adjoint],
        [5 * X_ROWS, 5 * 128, PLANE],
        last_scratch,
    )
    from_x, (one_along_y,) = shifted_beside(
        send_x,
        "gx",
        False,
        functools.partial(line_tangent_kernel, False),
        [one_cells, one_prim],
        [2880],
        [1120],
    )
    rest_two, send_y = fold(rest, from_x, True, 5, (column_part,))
    folded_two, (one_along_z,) = shifted_beside(
        send_y,
        "gy",
        False,
        functools.partial(column_tangent_kernel, False),
        [one_cells, one_prim],
        [2560],
    )
    send_x, rest = run(
        functools.partial(earlier_section_kernel, False, 0.25),
        [
            one_cells,
            one_prim,
            one_along_x,
            one_along_y,
            one_along_z,
            rest_two,
            folded_two,
            drag_part,
        ],
        [6 * X_ROWS, 6 * 128],
        earlier_scratch,
    )
    from_x, (zero_along_z,) = shifted_beside(
        send_x,
        "gx",
        True,
        functools.partial(column_tangent_kernel, True),
        [zero_cells, zero_prim],
        [2560],
    )
    rest_one, send_y = fold(rest, from_x, False)
    folded_one = shifted(send_y, "gy", True)
    send_x, rest = run(
        functools.partial(earlier_section_kernel, True, 1.0),
        [
            zero_cells,
            zero_prim,
            zero_along_x,
            zero_along_y,
            zero_along_z,
            rest_one,
            folded_one,
            drag_part,
        ],
        [6 * X_ROWS, 6 * 128],
        earlier_scratch,
    )
    rest_zero, send_y = fold(rest, shifted(send_x, "gx", False), True)
    folded_zero = shifted(send_y, "gy", False)
    return run(
        end_kernel,
        [adjoint, rest_two, folded_two, rest_zero, folded_zero],
        [320, 64],
        [320],
    )


def on_device(state, eddy, adjoint):
    grad_state, grad_eddy = pipeline(
        state.reshape(320, 128), eddy.reshape(64, 128), adjoint.reshape(320, 128)
    )
    return grad_state.reshape(5, 8, 8, 128), grad_eddy.reshape(8, 8, 128)


def solution(mesh):
    placed = (P(None, "gx", "gy", None), P("gx", "gy", None), P(None, "gx", "gy", None))
    return jax.shard_map(
        on_device,
        mesh=mesh,
        in_specs=placed,
        out_specs=(P(None, "gx", "gy", None), P("gx", "gy", None)),
        check_vma=False,
    )
```

```python
import functools

import jax
import jax.numpy as jnp
from jax import lax
from jax.experimental import pallas as pl
from jax.experimental.pallas import tpu as pltpu
from jax.sharding import PartitionSpec as P

HEAT_RATIO = 1.4
MOLECULAR_DRAG = 0.05
PRANDTL = 0.72
TIME_STEP = 0.04
SMOOTH_EPS = 1e-06
CONDUCTION = HEAT_RATIO / ((HEAT_RATIO - 1.0) * PRANDTL)
SMALL = 0.75 * SMOOTH_EPS

PITCH = 16
PLANE = 14 * PITCH


def frame(left):
    return (2, 6, 0) if left else (0, 0, 8)


def get(ref, start, stride=1, count=8):
    if stride == 1:
        return ref[pl.ds(start, count), :]
    return ref[pl.ds(start, count, stride=stride), :]


def put(ref, start, value, stride=1, count=8):
    if stride == 1:
        ref[pl.ds(start, count), :] = value
    else:
        ref[pl.ds(start, count, stride=stride), :] = value


def add(ref, start, value, stride=1, count=8):
    put(ref, start, get(ref, start, stride, count) + value, stride, count)


def ahead(value, offset):
    return pltpu.roll(value, (-offset) % 128, 1)


def quick_inverse(value):
    return pl.reciprocal(value, approx=True)


def loop(count, body, together=1):
    def step(i, carry):
        for k in range(together):
            body(i * together + k)
        return carry

    lax.fori_loop(0, count // together, step, 0)


class Slope:
    def __init__(self, value):
        self.value = value
        self.kept = {}

    def times(self, factor):
        if factor == 1.0:
            return self.value
        if factor not in self.kept:
            self.kept[factor] = factor * self.value
        return self.kept[factor]

    def square(self):
        if 0 not in self.kept:
            self.kept[0] = self.value * self.value + SMALL
        return self.kept[0]


def weno_parts(d1, d2, d3, d4):
    i1 = quick_inverse(d1.square() + d2.value * (d2.times(2.5) - d1.times(2.75)))
    i2 = quick_inverse(d2.square() + d3.value * (d3.value - d2.times(1.25)))
    i3 = quick_inverse(d4.square() + d3.value * (d3.times(2.5) - d4.times(2.75)))
    w1, w2, w3 = i1 * i1, 6.0 * (i2 * i2), 3.0 * (i3 * i3)
    m1 = d2.times(2.5) - d1.value
    m2 = d2.times(0.5) + d3.value
    m3 = d3.times(2.0) - d4.times(0.5)
    inverse = quick_inverse(w1 + w2 + w3)
    mean = (w1 * m1 + w2 * m2 + w3 * m3) * inverse
    return (i1, i2, i3), (w1, w2, w3), (m1, m2, m3), inverse, mean


def weno_rise(d1, d2, d3, d4):
    return weno_parts(d1, d2, d3, d4)[4]


def weno_pull(d1, d2, d3, d4, third=None):
    (i1, i2, i3), (w1, w2, w3), (m1, m2, m3), inverse, mean = weno_parts(d1, d2, d3, d4)
    scaled = inverse if third is None else third * inverse
    e1, e2, e3 = w1 * scaled, w2 * scaled, w3 * scaled
    g1 = (e1 * i1) * (mean - m1)
    g2 = (e2 * i2) * (mean - m2)
    g3 = (e3 * i3) * (mean - m3)
    c1 = g1 * (d1.times(4.0) - d2.times(5.5)) - e1
    c2 = g1 * (d2.times(10.0) - d1.times(5.5)) + g2 * (d2.times(4.0) - d3.times(2.5))
    c2 = c2 + (2.5 * e1 + 0.5 * e2)
    c3 = g2 * (d3.times(4.0) - d2.times(2.5)) + g3 * (d3.times(10.0) - d4.times(5.5))
    c3 = c3 + (e2 + 2.0 * e3)
    c4 = g3 * (d4.times(4.0) - d3.times(5.5)) - 0.5 * e3
    return c1, c2, c3, c4


def split_flux(cells, speed, push, direction):
    fluxes = [cells[1 + direction]]
    for j in range(3):
        momentum_flux = cells[1 + j] * speed
        fluxes.append(momentum_flux + push if j == direction else momentum_flux)
    fluxes.append((cells[4] + push) * speed)
    plus, minus = [], []
    for flux, cell in zip(fluxes, cells):
        half, double = 0.5 * flux, 2.0 * cell
        plus.append(half + double)
        minus.append(half - double)
    return plus, minus


def pull_flux(cells, velocity, push, inverse_rho, direction, cot, out):
    speed = velocity[direction]
    speed_cot = cot[4] * (cells[4] + push)
    for j in range(3):
        speed_cot = speed_cot + cot[1 + j] * cells[1 + j]
        out[1 + j] = out[1 + j] + cot[1 + j] * speed
    through = cot[4] * speed
    out[4] = out[4] + through
    pull_push(out, velocity, cot[1 + direction] + through)
    speed_cot = speed_cot * inverse_rho
    out[1 + direction] = out[1 + direction] + cot[0] + speed_cot
    out[0] = out[0] - speed_cot * speed


def pull_push(out, velocity, push_cot):
    scaled = 0.4 * push_cot
    out[4] = out[4] + scaled
    square = velocity[0] * velocity[0] + velocity[1] * velocity[1] + velocity[2] * velocity[2]
    out[0] = out[0] + 0.5 * (scaled * square)
    for j in range(3):
        out[1 + j] = out[1 + j] - scaled * velocity[j]


def fill_prim(padded, prim):
    def body(i):
        row = i * 32
        cells = [get(padded, c * PLANE + row, count=32) for c in range(6)]
        inverse = 1.0 / cells[0]
        velocity = [cells[1 + j] * inverse for j in range(3)]
        kinetic = 0.5 * (
            cells[1] * velocity[0] + cells[2] * velocity[1] + cells[3] * velocity[2]
        )
        push = (HEAT_RATIO - 1.0) * (cells[4] - kinetic)
        thermal = push * inverse
        molecular = MOLECULAR_DRAG * jnp.exp(0.7 * jnp.log(thermal))
        values = velocity + [thermal, molecular + cells[5], push, inverse, molecular]
        for k, value in enumerate(values):
            put(prim, k * PLANE + row, value, count=32)

    loop(7, lambda i: body(pl.multiple_of(i, 1)))


def line_layout(direction, front):
    if direction == 0:
        return lambda lead: lead * PITCH + (front + 3), 1
    return lambda lead: lead + (3 * PITCH + front), PITCH


def fill_split(padded, prim, split, direction, front):
    place, stride = line_layout(direction, front)

    def body(lead):
        row = place(lead)
        cells = [get(padded, c * PLANE + row, stride) for c in range(5)]
        speed = get(prim, direction * PLANE + row, stride)
        push = get(prim, 5 * PLANE + row, stride)
        plus, minus = split_flux(cells, speed, push, direction)
        for c in range(5):
            put(split, (c * 14 + lead) * 8, plus[c])
            put(split, ((5 + c) * 14 + lead) * 8, minus[c])

    for lead in range(14):
        body(lead)


def line_slopes(split, c):
    plus = [get(split, pl.multiple_of((c * 14 + k) * 8, 8)) for k in range(14)]
    minus = [get(split, pl.multiple_of(((5 + c) * 14 + k) * 8, 8)) for k in range(14)]
    plus_slopes = [Slope(plus[k + 1] - plus[k]) for k in range(13)]
    minus_slopes = [Slope(minus[k + 1] - minus[k]) for k in range(13)]
    return plus, minus, plus_slopes, minus_slopes


def line_rate(padded, prim, split, rate, direction, front, first):
    fill_split(padded, prim, split, direction, front)

    def body(c):
        plus, minus, ps, ms = line_slopes(split, c)
        low = None
        for f in range(9):
            rise = weno_rise(*ps[f : f + 4]) - weno_rise(ms[f + 4], ms[f + 3], ms[f + 2], ms[f + 1])
            face = (plus[f + 2] + minus[f + 3]) + (1.0 / 3.0) * rise
            if f:
                row, stride = (c * 64 + (f - 1) * 8, 1) if direction == 0 else (c * 64 + f - 1, 8)
                value = low - face
                if not first:
                    value = value + get(rate, row, stride)
                put(rate, row, value, stride)
            low = face

    loop(5, body, 5)


def line_tangent(padded, prim, split, tangent, direction, front):
    fill_split(padded, prim, split, direction, front)

    def body(c):
        _, _, ps, ms = line_slopes(split, c)
        for f in range(9):
            plus = weno_pull(*ps[f : f + 4])
            minus = weno_pull(ms[f + 4], ms[f + 3], ms[f + 2], ms[f + 1])
            for k, value in enumerate(plus + minus):
                put(tangent, pl.multiple_of((c * 9 + f) * 64, 8) + k * 8, value)

    loop(5, body)


def line_pull(padded, prim, split, split_cot, cot, grad, direction, front, tangent=None):
    place, stride = line_layout(direction, front)
    if tangent is None:
        fill_split(padded, prim, split, direction, front)

    def body(c):
        if tangent is None:
            _, _, ps, ms = line_slopes(split, c)
        own = [get(cot, c * PLANE + place(lead), stride) for lead in range(2, 12)]
        plus_cot, minus_cot = [None] * 14, [None] * 14

        def gather(table, lead, value):
            table[lead] = value if table[lead] is None else table[lead] + value

        for f in range(9):
            face = own[f + 1] - own[f]
            third = (1.0 / 3.0) * face
            if tangent is None:
                plus = weno_pull(*ps[f : f + 4], third)
                minus = weno_pull(ms[f + 4], ms[f + 3], ms[f + 2], ms[f + 1], -third)
            else:
                first = pl.multiple_of((c * 9 + f) * 64, 8)
                plus = [third * get(tangent, first + k * 8) for k in range(4)]
                minus = [-third * get(tangent, first + k * 8) for k in range(4, 8)]
            c1, c2, c3, c4 = plus
            for k, value in enumerate((-c1, c1 - c2, (face + c2) - c3, c3 - c4, c4)):
                gather(plus_cot, f + k, value)
            c1, c2, c3, c4 = minus
            for k, value in enumerate((-c4, c4 - c3, (face + c3) - c2, c2 - c1, c1)):
                gather(minus_cot, f + 1 + k, value)
            done = range(f, f + 1) if f < 8 else range(8, 14)
            for lead in done:
                p, m = plus_cot[lead], minus_cot[lead]
                if p is None:
                    total, gap = m, -m
                elif m is None:
                    total, gap = p, p
                else:
                    total, gap = p + m, p - m
                put(split_cot, pl.multiple_of((c * 14 + lead) * 8, 8), 0.5 * total)
                put(split_cot, pl.multiple_of(((5 + c) * 14 + lead) * 8, 8), 2.0 * gap)

    loop(5, body)
    for lead in range(14):
        row = place(lead)
        cells = [get(padded, c * PLANE + row, stride) for c in range(5)]
        velocity = [get(prim, c * PLANE + row, stride) for c in range(3)]
        push = get(prim, 5 * PLANE + row, stride)
        inverse = get(prim, 6 * PLANE + row, stride)
        flux_cot = [get(split_cot, (c * 14 + lead) * 8) for c in range(5)]
        out = [get(split_cot, ((5 + c) * 14 + lead) * 8) for c in range(5)]
        pull_flux(cells, velocity, push, inverse, direction, flux_cot, out)
        for c in range(5):
            add(grad, c * PLANE + row, out[c], stride)


def column_rate(padded, prim, rate, front):
    def body(o):
        row = (o + 3) * PITCH + (front + 3)
        cells = [get(padded, c * PLANE + row) for c in range(5)]
        plus, minus = split_flux(cells, get(prim, 2 * PLANE + row), get(prim, 5 * PLANE + row), 2)
        changes = []
        for c in range(5):
            dp = ahead(plus[c], 1) - plus[c]
            next_minus = ahead(minus[c], 1)
            dm = next_minus - minus[c]
            rise = weno_rise(*[Slope(v) for v in (ahead(dp, -2), ahead(dp, -1), dp, ahead(dp, 1))])
            rise = rise - weno_rise(
                *[Slope(v) for v in (ahead(dm, 2), ahead(dm, 1), dm, ahead(dm, -1))]
            )
            face = (plus[c] + next_minus) + (1.0 / 3.0) * rise
            changes.append(ahead(face, -1) - face)
        for c in range(5):
            add(rate, pl.multiple_of((c * 8 + o) * 8, 8), changes[c])

    loop(8, body, 4)


def column_slopes(plus, minus):
    dp = ahead(plus, 1) - plus
    dm = ahead(minus, 1) - minus
    return (
        [Slope(value) for value in (ahead(dp, -2), ahead(dp, -1), dp, ahead(dp, 1))],
        [Slope(value) for value in (ahead(dm, 2), ahead(dm, 1), dm, ahead(dm, -1))],
    )


def column_tangent(padded, prim, tangent, front):
    def body(o):
        row = (o + 3) * PITCH + (front + 3)
        cells = [get(padded, c * PLANE + row) for c in range(5)]
        plus, minus = split_flux(cells, get(prim, 2 * PLANE + row), get(prim, 5 * PLANE + row), 2)
        for c in range(5):
            ps, ms = column_slopes(plus[c], minus[c])
            for k, value in enumerate(weno_pull(*ps) + weno_pull(*ms)):
                put(tangent, pl.multiple_of((c * 8 + o) * 64, 8) + k * 8, value)

    loop(8, body, 4)


def column_cot(cells, velocity, push, inverse, cot, factors=None):
    if factors is None:
        plus, minus = split_flux(cells, velocity[2], push, 2)
    flux_cot, out = [], []
    for c in range(5):
        face = ahead(cot[c], 1) - cot[c]
        third = (1.0 / 3.0) * face
        if factors is None:
            ps, ms = column_slopes(plus[c], minus[c])
            plus_parts, minus_parts = weno_pull(*ps, third), weno_pull(*ms, -third)
        else:
            plus_parts = [third * value for value in factors[c][:4]]
            minus_parts = [-third * value for value in factors[c][4:]]
        c1, c2, c3, c4 = plus_parts
        total = (c3 + ahead(c1, 2)) + (ahead(c2, 1) + ahead(c4, -1))
        p = face + (ahead(total, -1) - total)
        c1, c2, c3, c4 = minus_parts
        total = (c3 + ahead(c1, -2)) + (ahead(c2, -1) + ahead(c4, 1))
        m = ahead(face + total, -1) - total
        flux_cot.append(0.5 * (p + m))
        out.append(2.0 * (p - m))
    pull_flux(cells, velocity, push, inverse, 2, flux_cot, out)
    return out


def column_pull(padded, prim, cot, grad, front, tangent):
    def body(o):
        row = (o + 3) * PITCH + (front + 3)
        cells = [get(padded, c * PLANE + row) for c in range(5)]
        velocity = [get(prim, c * PLANE + row) for c in range(3)]
        push = get(prim, 5 * PLANE + row)
        inverse = get(prim, 6 * PLANE + row)
        own = [get(cot, c * PLANE + row) for c in range(5)]
        factors = []
        for c in range(5):
            first = pl.multiple_of((c * 8 + o) * 64, 8)
            factors.append([get(tangent, first + k * 8) for k in range(8)])
        out = column_cot(cells, velocity, push, inverse, own, factors)
        for c in range(5):
            add(grad, c * PLANE + row, out[c])

    loop(8, body, 4)


def slopes(prim, row, stride, count):
    fields = [get(prim, j * PLANE + row, stride) for j in range(count)]
    table = [[], [], []]
    for j in range(count):
        start = j * PLANE + row
        table[0].append(
            0.5 * (get(prim, start + PITCH, stride) - get(prim, start - PITCH, stride))
        )
        table[1].append(0.5 * (get(prim, start + 1, stride) - get(prim, start - 1, stride)))
        table[2].append(0.5 * (ahead(fields[j], 1) - ahead(fields[j], -1)))
    return fields, table


def strain(table, k, j):
    return table[k][j] + table[j][k]


def viscous_fluxes(prim, row, stride, directions):
    fields, table = slopes(prim, row, stride, 4)
    drag = get(prim, 4 * PLANE + row, stride)
    spread = (2.0 / 3.0) * (table[0][0] + table[1][1] + table[2][2])
    out = {}
    for k in directions:
        stress = []
        for j in range(3):
            shape = strain(table, k, j)
            stress.append(drag * (shape - spread if j == k else shape))
        power = (
            fields[0] * stress[0]
            + fields[1] * stress[1]
            + fields[2] * stress[2]
            + CONDUCTION * (drag * table[k][3])
        )
        out[k] = stress + [power]
    return out


def viscous_rate(prim, flux_x, flux_y, rate, front):
    def store(ref, row, stride, values):
        for c in range(4):
            put(ref, c * PLANE + row, values[c], stride)

    for edge in (2, 11):
        row = edge * PITCH + (front + 3)
        store(flux_x, row, 1, viscous_fluxes(prim, row, 1, (0,))[0])
        row = 3 * PITCH + (front + edge)
        store(flux_y, row, PITCH, viscous_fluxes(prim, row, PITCH, (1,))[1])

    def body(o):
        row = (o + 3) * PITCH + (front + 3)
        values = viscous_fluxes(prim, row, 1, (0, 1, 2))
        changes = [0.5 * (ahead(value, 1) - ahead(value, -1)) for value in values[2]]
        store(flux_x, row, 1, values[0])
        store(flux_y, row, 1, values[1])
        for c in range(4):
            add(rate, pl.multiple_of(((1 + c) * 8 + o) * 8, 8), changes[c])

    loop(8, body, 8)

    for o in range(8):
        row = (o + 3) * PITCH + (front + 3)
        for c in range(4):
            start = c * PLANE + row
            change = (get(flux_x, start + PITCH) - get(flux_x, start - PITCH)) + (
                get(flux_y, start + 1) - get(flux_y, start - 1)
            )
            add(rate, ((1 + c) * 8 + o) * 8, 0.5 * change)


def total_of(terms):
    out = terms[0]
    for term in terms[1:]:
        out = out + term
    return out


def viscous_pull_at(prim, cot, prim_cot, row, stride, directions):
    fields, table = slopes(prim, row, stride, 4)
    drag = get(prim, 4 * PLANE + row, stride)
    spread = (2.0 / 3.0) * (table[0][0] + table[1][1] + table[2][2])
    field_cot = [[], [], []]
    drag_cot, spread_cot = [], []
    slope_cot = [[[] for _ in range(4)] for _ in range(3)]
    for k in directions:
        flux_cot = []
        for c in range(4):
            start = (1 + c) * PLANE + row
            if k == 2:
                own = get(cot, start, stride)
                flux_cot.append(0.5 * (ahead(own, -1) - ahead(own, 1)))
            else:
                step = PITCH if k == 0 else 1
                flux_cot.append(
                    0.5 * (get(cot, start - step, stride) - get(cot, start + step, stride))
                )
        power = flux_cot[3]
        heat = CONDUCTION * power
        drag_cot.append(heat * table[k][3])
        slope_cot[k][3].append(heat * drag)
        for j in range(3):
            shape = strain(table, k, j)
            if j == k:
                shape = shape - spread
            stress_cot = flux_cot[j] + fields[j] * power
            field_cot[j].append(power * (drag * shape))
            drag_cot.append(stress_cot * shape)
            scaled = drag * stress_cot
            slope_cot[k][j].append(scaled)
            slope_cot[j][k].append(scaled)
            if j == k:
                spread_cot.append(scaled)
    spread_total = (2.0 / 3.0) * total_of(spread_cot)
    for j in range(3):
        slope_cot[j][j].append(-spread_total)
    put(prim_cot, 4 * PLANE + row, total_of(drag_cot), stride)
    for j in range(4):
        here = list(field_cot[j]) if j < 3 else []
        if slope_cot[2][j]:
            value = total_of(slope_cot[2][j])
            here.append(0.5 * (ahead(value, -1) - ahead(value, 1)))
        if here:
            put(prim_cot, j * PLANE + row, total_of(here), stride)
        for k in range(2):
            if slope_cot[k][j]:
                put(
                    prim_cot,
                    (5 + 4 * k + j) * PLANE + row,
                    0.5 * total_of(slope_cot[k][j]),
                    stride,
                )


def viscous_pull(prim, cot, prim_cot, grad, front):
    clear_rows(prim_cot, 13 * PLANE)
    for edge in (2, 11):
        row = edge * PITCH + (front + 3)
        viscous_pull_at(prim, cot, prim_cot, row, 1, (0,))
        row = 3 * PITCH + (front + edge)
        viscous_pull_at(prim, cot, prim_cot, row, PITCH, (1,))

    def body(o):
        row = (o + 3) * PITCH + (front + 3)
        viscous_pull_at(prim, cot, prim_cot, row, 1, (0, 1, 2))

    loop(8, body, 4)

    def finish(i):
        row = i * 16 + 16
        velocity = [get(prim, j * PLANE + row, count=16) for j in range(3)]
        thermal = get(prim, 3 * PLANE + row, count=16)
        inverse = get(prim, 6 * PLANE + row, count=16)
        molecular = get(prim, 7 * PLANE + row, count=16)
        field_cot = []
        for j in range(4):
            start = j * PLANE + row
            along = (5 + j) * PLANE + row
            across = (9 + j) * PLANE + row
            field_cot.append(
                get(prim_cot, start, count=16)
                + (get(prim_cot, along - PITCH, count=16) - get(prim_cot, along + PITCH, count=16))
                + (get(prim_cot, across - 1, count=16) - get(prim_cot, across + 1, count=16))
            )
        drag_cot = get(prim_cot, 4 * PLANE + row, count=16)
        thermal_cot = field_cot[3] + 0.7 * (drag_cot * molecular) / thermal
        out = [get(grad, c * PLANE + row, count=16) for c in range(6)]
        push_cot = thermal_cot * inverse
        out[0] = out[0] - push_cot * thermal
        pull_push(out, velocity, push_cot)
        for j in range(3):
            scaled = field_cot[j] * inverse
            out[1 + j] = out[1 + j] + scaled
            out[0] = out[0] - scaled * velocity[j]
        out[5] = out[5] + drag_cot
        for c in range(6):
            put(grad, c * PLANE + row, out[c], count=16)

    loop(12, finish, 4)


def clear_rows(ref, rows):
    clear_rows_from(ref, 0, rows)


def clear_rows_from(ref, first, rows):
    for row in range(first, first + rows, 32):
        put(ref, row, jnp.zeros((32, 128), jnp.float32), count=32)


X_ROWS = 68
X_MORE = 5 * X_ROWS
Y_MORE = 5 * 48


def x_pieces(left):
    pieces, place = [], 0
    for x in range(6):
        distance = 5 - x if left else x
        first, count = (0, 14) if distance < 3 else (2, 10) if distance == 3 else (3, 8)
        pieces.append((place, x, first, count))
        place += count
    return pieces


def assemble(padded, own, from_y, from_x, left):
    front, first, outer = frame(left)
    for c in range(5):
        for x in range(8):
            row = c * PLANE + (first + x) * PITCH + front
            put(padded, row + first, get(own, (c * 8 + x) * 8))
            put(padded, row + outer, get(from_y, (c * 8 + x) * 6, count=6), count=6)
        for place, x, cell, count in x_pieces(left):
            row = c * PLANE + (outer + x) * PITCH + front + cell
            put(padded, row, get(from_x, c * X_ROWS + place, count=count), count=count)


def assemble_eddy_left(padded, eddy, zero_y, zero_x):
    front = frame(True)[0]
    for x in range(8):
        row = 5 * PLANE + (6 + x) * PITCH + front
        put(padded, row + 6, get(eddy, x * 8))
        put(padded, row + 2, get(zero_y, Y_MORE + x * 4, count=4), count=4)
    for x in range(4):
        row = 5 * PLANE + (2 + x) * PITCH + front + 2
        put(padded, row, get(zero_x, X_MORE + x * 12, count=12), count=12)


def assemble_eddy_right(padded, eddy, zero_y, zero_x, one_y, one_x):
    base = 5 * PLANE
    for x in range(8):
        row = base + (3 + x) * PITCH
        put(padded, row + 3, get(eddy, x * 8))
        put(padded, row + 2, get(zero_y, Y_MORE + x * 4 + 3, count=1), count=1)
        put(padded, row + 11, get(one_y, Y_MORE + x, count=1), count=1)
    put(padded, base + 2 * PITCH + 3, get(zero_x, X_MORE + 3 * 12 + 4))
    put(padded, base + 11 * PITCH + 3, get(one_x, X_MORE))


def start_kernel(state, eddy, send_y):
    for i in range(40):
        put(send_y, i * 6, get(state, i * 8 + 2, count=6), count=6)
    for x in range(8):
        put(send_y, Y_MORE + x * 4, get(eddy, x * 8 + 4, count=4), count=4)


def side_kernel(left, own, from_y, more, send_x, line):
    front, first, outer = frame(left)
    begin = 2 if left else 0
    for c in range(5):
        for x in range(6):
            source = c * 8 + begin + x
            row = (c * 6 + x) * PITCH + front
            put(line, row + first, get(own, source * 8))
            put(line, row + outer, get(from_y, source * 6, count=6), count=6)
        for place, x, cell, count in x_pieces(left):
            value = get(line, (c * 6 + x) * PITCH + front + cell, count=count)
            put(send_x, c * X_ROWS + place, value, count=count)
    if more.shape[0] == 320:
        for c in range(5):
            for x in range(3):
                source = c * 8 + 5 + x
                row = X_MORE + (c * 3 + x) * 8
                put(send_x, row, get(from_y, Y_MORE + source * 3, count=3), count=3)
                put(send_x, row + 3, get(more, source * 8, count=5), count=5)
    elif left:
        for x in range(4):
            row = X_MORE + x * 12
            put(send_x, row, get(from_y, Y_MORE + (4 + x) * 4, count=4), count=4)
            put(send_x, row + 4, get(more, (4 + x) * 8))
    else:
        put(send_x, X_MORE, get(more, 0))


def section_body(left, keep, weight, base, out, padded, prim, split, rate, flux_x, flux_y):
    front = frame(left)[0]
    fill_prim(padded, prim)
    line_rate(padded, prim, split, rate, 0, front, True)
    line_rate(padded, prim, split, rate, 1, front, False)
    column_rate(padded, prim, rate, front)
    viscous_rate(prim, flux_x, flux_y, rate, front)
    for x in range(8):
        row = (x + 3) * PITCH + (front + 3)
        for c in range(5):
            place = (c * 8 + x) * 8
            value = weight * get(padded, c * PLANE + row) + (weight * TIME_STEP) * get(rate, place)
            if keep:
                value = value + keep * get(base, place)
            put(out, place, value)


def first_section_kernel(state, zero_y, zero_x, eddy, out, send_y, padded, *scratch):
    assemble(padded, state, zero_y, zero_x, True)
    assemble_eddy_left(padded, eddy, zero_y, zero_x)
    section_body(True, 0.0, 1.0, None, out, padded, *scratch)
    for i in range(40):
        put(send_y, i * 6, get(out, i * 8, count=6), count=6)
    for x in range(8):
        put(send_y, Y_MORE + x, get(eddy, x * 8, count=1), count=1)


def second_section_kernel(
    own, one_y, one_x, zero_y, zero_x, eddy, state, adjoint, out, send_y, padded, *scratch
):
    assemble(padded, own, one_y, one_x, False)
    assemble_eddy_right(padded, eddy, zero_y, zero_x, one_y, one_x)
    section_body(False, 0.75, 0.25, state, out, padded, *scratch)
    for i in range(40):
        put(send_y, i * 6, get(out, i * 8 + 2, count=6), count=6)
        put(send_y, Y_MORE + i * 3, get(adjoint, i * 8 + 5, count=3), count=3)


def first_tangent_kernel(state, zero_y, zero_x, eddy, padded, prim, tangent, split):
    assemble(padded, state, zero_y, zero_x, True)
    assemble_eddy_left(padded, eddy, zero_y, zero_x)
    fill_prim(padded, prim)
    line_tangent(padded, prim, split, tangent, 0, frame(True)[0])


def second_tangent_kernel(own, one_y, one_x, zero_y, zero_x, eddy, padded, prim, tangent, split):
    assemble(padded, own, one_y, one_x, False)
    assemble_eddy_right(padded, eddy, zero_y, zero_x, one_y, one_x)
    fill_prim(padded, prim)
    line_tangent(padded, prim, split, tangent, 0, frame(False)[0])


def line_tangent_kernel(left, padded, prim, tangent, split):
    line_tangent(padded, prim, split, tangent, 1, frame(left)[0])


def column_tangent_kernel(left, padded, prim, tangent):
    column_tangent(padded, prim, tangent, frame(left)[0])


def own_column_kernel(own, adjoint, part):
    def body(x):
        rows = [pl.multiple_of((c * 8 + x) * 8, 8) for c in range(5)]
        cells = [get(own, row) for row in rows]
        inverse = 1.0 / cells[0]
        velocity = [cells[1 + j] * inverse for j in range(3)]
        kinetic = 0.5 * (
            cells[1] * velocity[0] + cells[2] * velocity[1] + cells[3] * velocity[2]
        )
        push = (HEAT_RATIO - 1.0) * (cells[4] - kinetic)
        cot = [(2.0 / 3.0 * TIME_STEP) * get(adjoint, row) for row in rows]
        out = column_cot(cells, velocity, push, inverse, cot)
        for row, value in zip(rows, out):
            put(part, row, value)

    loop(8, body, 4)


def hand_back(left, grad, send_x, rest):
    front, first, outer = frame(left)
    for c in range(5):
        for place, x, cell, count in x_pieces(left):
            row = c * PLANE + (outer + x) * PITCH + front + cell
            put(send_x, c * X_ROWS + place, get(grad, row, count=count), count=count)
        row = c * PLANE + first * PITCH
        put(rest, c * 128, get(grad, row, count=128), count=128)


def last_section_kernel(
    own, from_y, from_x, zero_y, zero_x, eddy, adjoint, send_x, rest, drag_part, *scratch
):
    padded, prim, split, split_cot, cot, prim_cot, grad = scratch
    front = frame(True)[0]
    scale = 2.0 / 3.0
    assemble(padded, own, from_y, from_x, True)
    assemble_eddy_left(padded, eddy, zero_y, zero_x)
    clear_rows(cot, 5 * PLANE)
    clear_rows(grad, 6 * PLANE)
    for c in range(5):
        for x in range(5):
            row = c * PLANE + (6 + x) * PITCH + front
            put(cot, row + 3, get(from_y, Y_MORE + (c * 8 + x) * 3, count=3), count=3)
            put(cot, row + 6, get(adjoint, (c * 8 + x) * 8, count=5), count=5)
        for x in range(3):
            row = c * PLANE + (3 + x) * PITCH + front
            put(cot, row + 3, get(from_x, X_MORE + (c * 3 + x) * 8))
    for c in range(5):
        for x in range(8):
            row = c * PLANE + (3 + x) * PITCH + (front + 3)
            value = scale * get(cot, row)
            put(grad, row, value)
            put(cot, row, TIME_STEP * value)
    fill_prim(padded, prim)
    viscous_pull(prim, cot, prim_cot, grad, front)
    line_pull(padded, prim, split, split_cot, cot, grad, 1, front)
    line_pull(padded, prim, split, split_cot, cot, grad, 0, front)
    hand_back(True, grad, send_x, rest)
    put(drag_part, 0, get(grad, 5 * PLANE, count=PLANE), count=PLANE)


def earlier_section(left, scale, cells, tangents, rest_in, folded_y, scratch):
    padded, prim = cells
    along_x, along_y, along_z = tangents
    split_cot, cot, prim_cot, grad, folded = scratch
    front = frame(left)[0]
    clear_rows(cot, 5 * PLANE)
    clear_rows(grad, 5 * PLANE)
    begin = 0 if left else 2
    for i in range(40):
        put(folded, i * 8, get(rest_in, i * 8))
        add(folded, i * 8 + begin, get(folded_y, i * 6, count=6), count=6)
    for c in range(5):
        for x in range(8):
            row = c * PLANE + (3 + x) * PITCH + (front + 3)
            value = scale * get(folded, (c * 8 + x) * 8)
            put(cot, row, TIME_STEP * value)
            put(grad, row, value)
    viscous_pull(prim, cot, prim_cot, grad, front)
    line_pull(padded, prim, None, split_cot, cot, grad, 1, front, along_y)
    line_pull(padded, prim, None, split_cot, cot, grad, 0, front, along_x)
    column_pull(padded, prim, cot, grad, front, along_z)


def second_pull_kernel(
    padded, prim, along_x, along_y, along_z, rest_in, folded_y, send_x, rest, drag_part, *scratch
):
    grad = scratch[3]
    clear_rows_from(grad, 5 * PLANE, PLANE)
    earlier_section(
        False, 0.25, (padded, prim), (along_x, along_y, along_z), rest_in, folded_y, scratch
    )
    hand_back(False, grad, send_x, rest)
    put(send_x, X_MORE, get(grad, 5 * PLANE + 11 * PITCH + 3))
    put(drag_part, 0, get(grad, 5 * PLANE, count=PLANE), count=PLANE)


def first_pull_kernel(
    padded, prim, along_x, along_y, along_z, rest_in, folded_y, folded_x, drag_two, drag_one, *refs
):
    send_x, rest = refs[:2]
    scratch = refs[2:]
    grad = scratch[3]
    front = frame(True)[0]
    put(grad, 5 * PLANE, get(drag_two, 0, count=PLANE), count=PLANE)
    for x in range(9):
        row = 5 * PLANE + (5 + x) * PITCH + front + 5
        add(grad, row, get(drag_one, (2 + x) * PITCH + 2, count=9), count=9)
    add(grad, 5 * PLANE + 6 * PITCH + front + 6, get(folded_x, X_MORE))
    for x in range(8):
        row = 5 * PLANE + (6 + x) * PITCH + front + 6
        add(grad, row, get(folded_y, Y_MORE + x, count=1), count=1)
    earlier_section(
        True, 1.0, (padded, prim), (along_x, along_y, along_z), rest_in, folded_y, scratch
    )
    hand_back(True, grad, send_x, rest)
    for x in range(4):
        row = 5 * PLANE + (2 + x) * PITCH + front + 2
        put(send_x, X_MORE + x * 12, get(grad, row, count=12), count=12)
    put(rest, 640, get(grad, 5 * PLANE + 6 * PITCH, count=128), count=128)


def fold_rows(left, rest_in, from_x, rest, send_y, work):
    front, first, outer = frame(left)
    begin = 2 if left else 0
    put(work, 0, get(rest_in, 0, count=640), count=640)
    for c in range(5):
        for place, x, cell, count in x_pieces(left):
            row = (c * 8 + begin + x) * PITCH + front + cell
            add(work, row, get(from_x, c * X_ROWS + place, count=count), count=count)
    for i in range(40):
        put(rest, i * 8, get(work, i * PITCH + front + first))
        put(send_y, i * 6, get(work, i * PITCH + front + outer, count=6), count=6)


def last_fold_kernel(rest_in, from_x, column_part, rest, send_y, work):
    fold_rows(True, rest_in, from_x, rest, send_y, work)
    for i in range(40):
        add(rest, i * 8, get(column_part, i * 8))


def second_fold_kernel(rest_in, from_x, drag_part, rest, send_y, work):
    fold_rows(False, rest_in, from_x, rest, send_y, work)
    for x in range(8):
        put(send_y, Y_MORE + x, get(drag_part, (3 + x) * PITCH + 11, count=1), count=1)


def first_fold_kernel(rest_in, from_x, rest, send_y, work):
    fold_rows(True, rest_in, from_x, rest, send_y, work)
    put(work, 640, get(rest_in, 640, count=128), count=128)
    front = frame(True)[0]
    for x in range(4):
        row = 640 + (4 + x) * PITCH + front + 2
        add(work, row, get(from_x, X_MORE + x * 12, count=12), count=12)
    for x in range(8):
        put(rest, 320 + x * 8, get(work, 640 + x * PITCH + front + 6))
        row = 640 + x * PITCH + front + 2
        put(send_y, Y_MORE + x * 4, get(work, row, count=4), count=4)


def end_kernel(adjoint, rest_two, folded_two, rest_zero, folded_zero, grad_state, grad_eddy, work):
    for i in range(40):
        put(work, i * 8, get(rest_two, i * 8))
        add(work, i * 8 + 2, get(folded_two, i * 6, count=6), count=6)
    for i in range(40):
        value = (1.0 / 3.0) * get(adjoint, i * 8) + 0.75 * get(work, i * 8)
        put(grad_state, i * 8, value + get(rest_zero, i * 8))
        add(grad_state, i * 8 + 2, get(folded_zero, i * 6, count=6), count=6)
    for i in range(8):
        put(grad_eddy, i * 8, get(rest_zero, 320 + i * 8))
        add(grad_eddy, i * 8 + 4, get(folded_zero, Y_MORE + i * 4, count=4), count=4)


def run(kernel, operands, outs, scratch=(), work=0):
    cost = pl.CostEstimate(flops=work, bytes_accessed=4 * work, transcendentals=0) if work else None
    return pl.pallas_call(
        kernel,
        out_shape=[jax.ShapeDtypeStruct((rows, 128), jnp.float32) for rows in outs],
        in_specs=[pl.BlockSpec(memory_space=pltpu.VMEM)] * len(operands),
        out_specs=[pl.BlockSpec(memory_space=pltpu.VMEM)] * len(outs),
        scratch_shapes=[pltpu.VMEM((rows, 128), jnp.float32) for rows in scratch],
        compiler_params=pltpu.CompilerParams(vmem_limit_bytes=20 * 1024 * 1024),
        cost_estimate=cost,
    )(*operands)


def shifted(values, axis, up):
    count = lax.axis_size(axis)
    step = 1 if up else count - 1
    return lax.ppermute(values, axis, [(i, (i + step) % count) for i in range(count)])


def together(*values):
    return lax.optimization_barrier(values)


def shifted_beside(values, axis, up, kernel, operands, outs, scratch=()):
    values, *operands = together(values, *operands)
    moved = shifted(values, axis, up)
    moved, *results = together(moved, *run(kernel, operands, outs, scratch, 2_000_000))
    return moved, results


def pipeline(state, eddy, adjoint):
    section_scratch = (6 * PLANE, 8 * PLANE, 1120, 320, 4 * PLANE, 4 * PLANE)
    last_scratch = (6 * PLANE, 8 * PLANE, 1120, 1120, 5 * PLANE, 13 * PLANE, 6 * PLANE)
    earlier_scratch = (1120, 5 * PLANE, 13 * PLANE, 6 * PLANE, 320)
    first_tangent = [6 * PLANE, 8 * PLANE, 2880]

    def sides(own, from_y, more, left, rows):
        (send_x,) = run(
            functools.partial(side_kernel, left),
            [own, from_y, more],
            [X_MORE + rows],
            [5 * 6 * PITCH],
        )
        return send_x

    (send_y,) = run(start_kernel, [state, eddy], [Y_MORE + 32])
    zero_y = shifted(send_y, "gy", True)
    zero_x = shifted(sides(state, zero_y, eddy, True, 48), "gx", True)
    zero = [state, zero_y, zero_x, eddy]
    one, send_y = run(first_section_kernel, zero, [320, Y_MORE + 8], section_scratch)

    one_y, (zero_cells, zero_prim, zero_along_x) = shifted_beside(
        send_y, "gy", False, first_tangent_kernel, zero, first_tangent, [1120]
    )
    one_x, (zero_along_y,) = shifted_beside(
        sides(one, one_y, eddy, False, 8),
        "gx",
        False,
        functools.partial(line_tangent_kernel, True),
        [zero_cells, zero_prim],
        [2880],
        [1120],
    )
    one_all = [one, one_y, one_x, zero_y, zero_x, eddy]
    two, send_y = run(
        second_section_kernel, [*one_all, state, adjoint], [320, Y_MORE + 120], section_scratch
    )

    two_y, (column_part,) = shifted_beside(
        send_y, "gy", True, own_column_kernel, [two, adjoint], [320]
    )
    two_x, (one_cells, one_prim, one_along_x) = shifted_beside(
        sides(two, two_y, adjoint, True, 120),
        "gx",
        True,
        second_tangent_kernel,
        one_all,
        first_tangent,
        [1120],
    )
    send_x, rest, drag_two = run(
        last_section_kernel,
        [two, two_y, two_x, zero_y, zero_x, eddy, adjoint],
        [X_MORE, 640, PLANE],
        last_scratch,
    )
    from_x, (one_along_y,) = shifted_beside(
        send_x,
        "gx",
        False,
        functools.partial(line_tangent_kernel, False),
        [one_cells, one_prim],
        [2880],
        [1120],
    )
    rest_two, send_y = run(last_fold_kernel, [rest, from_x, column_part], [320, Y_MORE], [640])
    folded_two, (one_along_z,) = shifted_beside(
        send_y,
        "gy",
        False,
        functools.partial(column_tangent_kernel, False),
        [one_cells, one_prim],
        [2560],
    )

    one_tangents = [one_along_x, one_along_y, one_along_z]
    send_x, rest, drag_one = run(
        second_pull_kernel,
        [one_cells, one_prim, *one_tangents, rest_two, folded_two],
        [X_MORE + 8, 640, PLANE],
        earlier_scratch,
    )
    from_x, (zero_along_z,) = shifted_beside(
        send_x,
        "gx",
        True,
        functools.partial(column_tangent_kernel, True),
        [zero_cells, zero_prim],
        [2560],
    )
    rest_one, send_y = run(second_fold_kernel, [rest, from_x, drag_one], [320, Y_MORE + 8], [640])
    folded_one = shifted(send_y, "gy", True)

    zero_tangents = [zero_along_x, zero_along_y, zero_along_z]
    send_x, rest = run(
        first_pull_kernel,
        [zero_cells, zero_prim, *zero_tangents, rest_one, folded_one, from_x, drag_two, drag_one],
        [X_MORE + 48, 768],
        earlier_scratch,
    )
    from_x = shifted(send_x, "gx", False)
    rest_zero, send_y = run(first_fold_kernel, [rest, from_x], [384, Y_MORE + 32], [768])
    folded_zero = shifted(send_y, "gy", False)
    return run(
        end_kernel,
        [adjoint, rest_two, folded_two, rest_zero, folded_zero],
        [320, 64],
        [320],
    )


def on_device(state, eddy, adjoint):
    grad_state, grad_eddy = pipeline(
        state.reshape(320, 128), eddy.reshape(64, 128), adjoint.reshape(320, 128)
    )
    return grad_state.reshape(5, 8, 8, 128), grad_eddy.reshape(8, 8, 128)


def solution(mesh):
    placed = (P(None, "gx", "gy", None), P("gx", "gy", None), P(None, "gx", "gy", None))
    return jax.shard_map(
        on_device,
        mesh=mesh,
        in_specs=placed,
        out_specs=(P(None, "gx", "gy", None), P("gx", "gy", None)),
        check_vma=False,
    )
```

```python
import collections
import functools

import jax
import jax.numpy as jnp
from jax import lax
from jax.experimental import pallas as pl
from jax.experimental.pallas import tpu as pltpu
from jax.sharding import PartitionSpec as P

HEAT_RATIO = 1.4
MOLECULAR_DRAG = 0.05
PRANDTL = 0.72
TIME_STEP = 0.04
SMOOTH_EPS = 1e-06
CONDUCTION = HEAT_RATIO / ((HEAT_RATIO - 1.0) * PRANDTL)
SMALL = 0.75 * SMOOTH_EPS

PITCH = 16
PLANE = 14 * PITCH


def frame(left):
    return (2, 6, 0) if left else (0, 0, 8)


Grid = collections.namedtuple("Grid", ["pitch", "plane", "leads", "x_start", "y_start"])


def narrow(front):
    return Grid(PITCH, PLANE, 14, front + 3, 3 * PITCH + front)


WIDE = Grid(24, 18 * 24, 18, 8, 5 * 24 + 3)


NARROW = narrow(0)


def wide_row(x, y):
    return (x + 5) * 24 + 8 + y


def get(ref, start, stride=1, count=8):
    if stride == 1:
        return ref[pl.ds(start, count), :]
    return ref[pl.ds(start, count, stride=stride), :]


def put(ref, start, value, stride=1, count=8):
    if stride == 1:
        ref[pl.ds(start, count), :] = value
    else:
        ref[pl.ds(start, count, stride=stride), :] = value


def add(ref, start, value, stride=1, count=8):
    put(ref, start, get(ref, start, stride, count) + value, stride, count)


def ahead(value, offset):
    return pltpu.roll(value, (-offset) % 128, 1)


def quick_inverse(value):
    return pl.reciprocal(value, approx=True)


def loop(count, body, together=1):
    def step(i, carry):
        for k in range(together):
            body(i * together + k)
        return carry

    lax.fori_loop(0, count // together, step, 0)


class Slope:
    def __init__(self, value):
        self.value = value
        self.kept = {}

    def times(self, factor):
        if factor == 1.0:
            return self.value
        if factor not in self.kept:
            self.kept[factor] = factor * self.value
        return self.kept[factor]

    def square(self):
        if 0 not in self.kept:
            self.kept[0] = self.value * self.value + SMALL
        return self.kept[0]


def weno_parts(d1, d2, d3, d4):
    i1 = quick_inverse(d1.square() + d2.value * (d2.times(2.5) - d1.times(2.75)))
    i2 = quick_inverse(d2.square() + d3.value * (d3.value - d2.times(1.25)))
    i3 = quick_inverse(d4.square() + d3.value * (d3.times(2.5) - d4.times(2.75)))
    w1, w2, w3 = i1 * i1, 6.0 * (i2 * i2), 3.0 * (i3 * i3)
    m1 = d2.times(2.5) - d1.value
    m2 = d2.times(0.5) + d3.value
    m3 = d3.times(2.0) - d4.times(0.5)
    inverse = quick_inverse(w1 + w2 + w3)
    mean = (w1 * m1 + w2 * m2 + w3 * m3) * inverse
    return (i1, i2, i3), (w1, w2, w3), (m1, m2, m3), inverse, mean


def weno_rise(d1, d2, d3, d4):
    return weno_parts(d1, d2, d3, d4)[4]


def weno_pull(d1, d2, d3, d4, third=None):
    (i1, i2, i3), (w1, w2, w3), (m1, m2, m3), inverse, mean = weno_parts(d1, d2, d3, d4)
    scaled = inverse if third is None else third * inverse
    e1, e2, e3 = w1 * scaled, w2 * scaled, w3 * scaled
    g1 = (e1 * i1) * (mean - m1)
    g2 = (e2 * i2) * (mean - m2)
    g3 = (e3 * i3) * (mean - m3)
    c1 = g1 * (d1.times(4.0) - d2.times(5.5)) - e1
    c2 = g1 * (d2.times(10.0) - d1.times(5.5)) + g2 * (d2.times(4.0) - d3.times(2.5))
    c2 = c2 + (2.5 * e1 + 0.5 * e2)
    c3 = g2 * (d3.times(4.0) - d2.times(2.5)) + g3 * (d3.times(10.0) - d4.times(5.5))
    c3 = c3 + (e2 + 2.0 * e3)
    c4 = g3 * (d4.times(4.0) - d3.times(5.5)) - 0.5 * e3
    return c1, c2, c3, c4


def split_flux(cells, speed, push, direction):
    fluxes = [cells[1 + direction]]
    for j in range(3):
        momentum_flux = cells[1 + j] * speed
        fluxes.append(momentum_flux + push if j == direction else momentum_flux)
    fluxes.append((cells[4] + push) * speed)
    plus, minus = [], []
    for flux, cell in zip(fluxes, cells):
        half, double = 0.5 * flux, 2.0 * cell
        plus.append(half + double)
        minus.append(half - double)
    return plus, minus


def pull_flux(cells, velocity, push, inverse_rho, direction, cot, out):
    speed = velocity[direction]
    speed_cot = cot[4] * (cells[4] + push)
    for j in range(3):
        speed_cot = speed_cot + cot[1 + j] * cells[1 + j]
        out[1 + j] = out[1 + j] + cot[1 + j] * speed
    through = cot[4] * speed
    out[4] = out[4] + through
    pull_push(out, velocity, cot[1 + direction] + through)
    speed_cot = speed_cot * inverse_rho
    out[1 + direction] = out[1 + direction] + cot[0] + speed_cot
    out[0] = out[0] - speed_cot * speed


def pull_push(out, velocity, push_cot):
    scaled = 0.4 * push_cot
    out[4] = out[4] + scaled
    square = velocity[0] * velocity[0] + velocity[1] * velocity[1] + velocity[2] * velocity[2]
    out[0] = out[0] + 0.5 * (scaled * square)
    for j in range(3):
        out[1 + j] = out[1 + j] - scaled * velocity[j]


def fill_prim(padded, prim, plane=PLANE, count=32):
    def body(i):
        row = i * count
        cells = [get(padded, c * plane + row, count=count) for c in range(6)]
        inverse = 1.0 / cells[0]
        velocity = [cells[1 + j] * inverse for j in range(3)]
        kinetic = 0.5 * (
            cells[1] * velocity[0] + cells[2] * velocity[1] + cells[3] * velocity[2]
        )
        push = (HEAT_RATIO - 1.0) * (cells[4] - kinetic)
        thermal = push * inverse
        molecular = MOLECULAR_DRAG * jnp.exp(0.7 * jnp.log(thermal))
        values = velocity + [thermal, molecular + cells[5], push, inverse, molecular]
        for k, value in enumerate(values):
            put(prim, k * plane + row, value, count=count)

    loop(plane // count, body)


def line_layout(direction, g):
    if direction == 0:
        return lambda lead: lead * g.pitch + g.x_start, 1
    return lambda lead: lead + g.y_start, g.pitch


def fill_split(padded, prim, split, direction, g):
    place, stride = line_layout(direction, g)
    for lead in range(g.leads):
        row = place(lead)
        cells = [get(padded, c * g.plane + row, stride) for c in range(5)]
        speed = get(prim, direction * g.plane + row, stride)
        push = get(prim, 5 * g.plane + row, stride)
        plus, minus = split_flux(cells, speed, push, direction)
        for c in range(5):
            put(split, (c * g.leads + lead) * 8, plus[c])
            put(split, ((5 + c) * g.leads + lead) * 8, minus[c])


def line_slopes(split, c, leads):
    plus = [get(split, pl.multiple_of((c * leads + k) * 8, 8)) for k in range(leads)]
    minus = [get(split, pl.multiple_of(((5 + c) * leads + k) * 8, 8)) for k in range(leads)]
    plus_slopes = [Slope(plus[k + 1] - plus[k]) for k in range(leads - 1)]
    minus_slopes = [Slope(minus[k + 1] - minus[k]) for k in range(leads - 1)]
    return plus, minus, plus_slopes, minus_slopes


def line_rate(padded, prim, split, rate, direction, front, first):
    fill_split(padded, prim, split, direction, narrow(front))

    def body(c):
        plus, minus, ps, ms = line_slopes(split, c, 14)
        low = None
        for f in range(9):
            rise = weno_rise(*ps[f : f + 4]) - weno_rise(ms[f + 4], ms[f + 3], ms[f + 2], ms[f + 1])
            face = (plus[f + 2] + minus[f + 3]) + (1.0 / 3.0) * rise
            if f:
                row, stride = (c * 64 + (f - 1) * 8, 1) if direction == 0 else (c * 64 + f - 1, 8)
                value = low - face
                if not first:
                    value = value + get(rate, row, stride)
                put(rate, row, value, stride)
            low = face

    loop(5, body, 5)


def line_tangent(padded, prim, split, tangent, direction, front):
    fill_split(padded, prim, split, direction, narrow(front))

    def body(c):
        _, _, ps, ms = line_slopes(split, c, 14)
        for f in range(9):
            plus = weno_pull(*ps[f : f + 4])
            minus = weno_pull(ms[f + 4], ms[f + 3], ms[f + 2], ms[f + 1])
            for k, value in enumerate(plus + minus):
                put(tangent, pl.multiple_of((c * 9 + f) * 64, 8) + k * 8, value)

    loop(5, body)


def line_pull(padded, prim, split, split_cot, cot, grad, direction, g, kept, tangent=None):
    place, stride = line_layout(direction, g)
    leads, faces = g.leads, g.leads - 5
    if tangent is None:
        fill_split(padded, prim, split, direction, g)

    def body(c):
        if tangent is None:
            _, _, ps, ms = line_slopes(split, c, leads)
        own = [get(cot, c * g.plane + place(lead), stride) for lead in range(2, leads - 2)]
        plus_cot, minus_cot = [None] * leads, [None] * leads

        def gather(table, lead, value):
            if lead in kept:
                table[lead] = value if table[lead] is None else table[lead] + value

        for f in range(faces):
            face = own[f + 1] - own[f]
            third = (1.0 / 3.0) * face
            if tangent is None:
                plus = weno_pull(*ps[f : f + 4], third)
                minus = weno_pull(ms[f + 4], ms[f + 3], ms[f + 2], ms[f + 1], -third)
            else:
                first = pl.multiple_of((c * 9 + f) * 64, 8)
                plus = [third * get(tangent, first + k * 8) for k in range(4)]
                minus = [-third * get(tangent, first + k * 8) for k in range(4, 8)]
            c1, c2, c3, c4 = plus
            for k, value in enumerate((-c1, c1 - c2, (face + c2) - c3, c3 - c4, c4)):
                gather(plus_cot, f + k, value)
            c1, c2, c3, c4 = minus
            for k, value in enumerate((-c4, c4 - c3, (face + c3) - c2, c2 - c1, c1)):
                gather(minus_cot, f + 1 + k, value)
            for lead in range(f, f + 1 if f < faces - 1 else leads):
                if lead not in kept:
                    continue
                p, m = plus_cot[lead], minus_cot[lead]
                if p is None:
                    total, gap = m, -m
                elif m is None:
                    total, gap = p, p
                else:
                    total, gap = p + m, p - m
                put(split_cot, pl.multiple_of((c * leads + lead) * 8, 8), 0.5 * total)
                put(split_cot, pl.multiple_of(((5 + c) * leads + lead) * 8, 8), 2.0 * gap)

    loop(5, body)
    for lead in kept:
        row = place(lead)
        cells = [get(padded, c * g.plane + row, stride) for c in range(5)]
        velocity = [get(prim, c * g.plane + row, stride) for c in range(3)]
        push = get(prim, 5 * g.plane + row, stride)
        inverse = get(prim, 6 * g.plane + row, stride)
        flux_cot = [get(split_cot, (c * leads + lead) * 8) for c in range(5)]
        out = [get(split_cot, ((5 + c) * leads + lead) * 8) for c in range(5)]
        pull_flux(cells, velocity, push, inverse, direction, flux_cot, out)
        for c in range(5):
            add(grad, c * g.plane + row, out[c], stride)


def column_change(cells, speed, push):
    plus, minus = split_flux(cells, speed, push, 2)
    changes = []
    for c in range(5):
        next_minus = ahead(minus[c], 1)
        dp, dm = ahead(plus[c], 1) - plus[c], next_minus - minus[c]
        rise = weno_rise(*[Slope(v) for v in (ahead(dp, -2), ahead(dp, -1), dp, ahead(dp, 1))])
        rise = rise - weno_rise(
            *[Slope(v) for v in (ahead(dm, 2), ahead(dm, 1), dm, ahead(dm, -1))]
        )
        face = (plus[c] + next_minus) + (1.0 / 3.0) * rise
        changes.append(ahead(face, -1) - face)
    return changes


def column_rate(padded, prim, rate, front, rows):
    for o in rows:
        row = (o + 3) * PITCH + (front + 3)
        cells = [get(padded, c * PLANE + row) for c in range(5)]
        changes = column_change(cells, get(prim, 2 * PLANE + row), get(prim, 5 * PLANE + row))
        for c in range(5):
            add(rate, (c * 8 + o) * 8, changes[c])


def early_column_kernel(left, own, from_y, column, line):
    for i in range(5):
        x = i if left else 3 + i
        for c in range(5):
            source, row = c * 8 + x, c * 16
            if left:
                put(line, row, get(from_y, source * 6 + 3, count=3), count=3)
                put(line, row + 3, get(own, source * 8, count=5), count=5)
            else:
                put(line, row, get(own, source * 8 + 3, count=5), count=5)
                put(line, row + 5, get(from_y, source * 6, count=3), count=3)
        cells = [get(line, c * 16) for c in range(5)]
        inverse = 1.0 / cells[0]
        velocity = [cells[1 + j] * inverse for j in range(3)]
        kinetic = 0.5 * (
            cells[1] * velocity[0] + cells[2] * velocity[1] + cells[3] * velocity[2]
        )
        push = (HEAT_RATIO - 1.0) * (cells[4] - kinetic)
        changes = column_change(cells, velocity[2], push)
        for c in range(5):
            put(column, (c * 5 + i) * 8, changes[c])


def column_slopes(plus, minus):
    dp = ahead(plus, 1) - plus
    dm = ahead(minus, 1) - minus
    return (
        [Slope(value) for value in (ahead(dp, -2), ahead(dp, -1), dp, ahead(dp, 1))],
        [Slope(value) for value in (ahead(dm, 2), ahead(dm, 1), dm, ahead(dm, -1))],
    )


def column_tangent(padded, prim, tangent, front):
    def body(o):
        row = (o + 3) * PITCH + (front + 3)
        cells = [get(padded, c * PLANE + row) for c in range(5)]
        plus, minus = split_flux(cells, get(prim, 2 * PLANE + row), get(prim, 5 * PLANE + row), 2)
        for c in range(5):
            ps, ms = column_slopes(plus[c], minus[c])
            for k, value in enumerate(weno_pull(*ps) + weno_pull(*ms)):
                put(tangent, pl.multiple_of((c * 8 + o) * 64, 8) + k * 8, value)

    loop(8, body, 4)


def column_cot(cells, velocity, push, inverse, cot, factors=None):
    if factors is None:
        plus, minus = split_flux(cells, velocity[2], push, 2)
    flux_cot, out = [], []
    for c in range(5):
        face = ahead(cot[c], 1) - cot[c]
        third = (1.0 / 3.0) * face
        if factors is None:
            ps, ms = column_slopes(plus[c], minus[c])
            plus_parts, minus_parts = weno_pull(*ps, third), weno_pull(*ms, -third)
        else:
            plus_parts = [third * value for value in factors[c][:4]]
            minus_parts = [-third * value for value in factors[c][4:]]
        c1, c2, c3, c4 = plus_parts
        total = (c3 + ahead(c1, 2)) + (ahead(c2, 1) + ahead(c4, -1))
        p = face + (ahead(total, -1) - total)
        c1, c2, c3, c4 = minus_parts
        total = (c3 + ahead(c1, -2)) + (ahead(c2, -1) + ahead(c4, 1))
        m = ahead(face + total, -1) - total
        flux_cot.append(0.5 * (p + m))
        out.append(2.0 * (p - m))
    pull_flux(cells, velocity, push, inverse, 2, flux_cot, out)
    return out


def column_pull(padded, prim, cot, grad, front, tangent):
    def body(o):
        row = (o + 3) * PITCH + (front + 3)
        cells = [get(padded, c * PLANE + row) for c in range(5)]
        velocity = [get(prim, c * PLANE + row) for c in range(3)]
        push = get(prim, 5 * PLANE + row)
        inverse = get(prim, 6 * PLANE + row)
        own = [get(cot, c * PLANE + row) for c in range(5)]
        factors = []
        for c in range(5):
            first = pl.multiple_of((c * 8 + o) * 64, 8)
            factors.append([get(tangent, first + k * 8) for k in range(8)])
        out = column_cot(cells, velocity, push, inverse, own, factors)
        for c in range(5):
            add(grad, c * PLANE + row, out[c])

    loop(8, body, 4)


def slopes(prim, row, stride, count, g):
    fields = [get(prim, j * g.plane + row, stride) for j in range(count)]
    table = [[], [], []]
    for j in range(count):
        start = j * g.plane + row
        table[0].append(
            0.5 * (get(prim, start + g.pitch, stride) - get(prim, start - g.pitch, stride))
        )
        table[1].append(0.5 * (get(prim, start + 1, stride) - get(prim, start - 1, stride)))
        table[2].append(0.5 * (ahead(fields[j], 1) - ahead(fields[j], -1)))
    return fields, table


def strain(table, k, j):
    return table[k][j] + table[j][k]


def viscous_fluxes(prim, row, stride, directions):
    fields, table = slopes(prim, row, stride, 4, NARROW)
    drag = get(prim, 4 * PLANE + row, stride)
    spread = (2.0 / 3.0) * (table[0][0] + table[1][1] + table[2][2])
    out = {}
    for k in directions:
        stress = []
        for j in range(3):
            shape = strain(table, k, j)
            stress.append(drag * (shape - spread if j == k else shape))
        power = (
            fields[0] * stress[0]
            + fields[1] * stress[1]
            + fields[2] * stress[2]
            + CONDUCTION * (drag * table[k][3])
        )
        out[k] = stress + [power]
    return out


def viscous_rate(prim, flux_x, flux_y, rate, front):
    def store(ref, row, stride, values):
        for c in range(4):
            put(ref, c * PLANE + row, values[c], stride)

    for edge in (2, 11):
        row = edge * PITCH + (front + 3)
        store(flux_x, row, 1, viscous_fluxes(prim, row, 1, (0,))[0])
        row = 3 * PITCH + (front + edge)
        store(flux_y, row, PITCH, viscous_fluxes(prim, row, PITCH, (1,))[1])

    def body(o):
        row = (o + 3) * PITCH + (front + 3)
        values = viscous_fluxes(prim, row, 1, (0, 1, 2))
        changes = [0.5 * (ahead(value, 1) - ahead(value, -1)) for value in values[2]]
        store(flux_x, row, 1, values[0])
        store(flux_y, row, 1, values[1])
        for c in range(4):
            add(rate, pl.multiple_of(((1 + c) * 8 + o) * 8, 8), changes[c])

    loop(8, body, 8)

    for o in range(8):
        row = (o + 3) * PITCH + (front + 3)
        for c in range(4):
            start = c * PLANE + row
            change = (get(flux_x, start + PITCH) - get(flux_x, start - PITCH)) + (
                get(flux_y, start + 1) - get(flux_y, start - 1)
            )
            add(rate, ((1 + c) * 8 + o) * 8, 0.5 * change)


def total_of(terms):
    out = terms[0]
    for term in terms[1:]:
        out = out + term
    return out


def viscous_pull_at(prim, cot, prim_cot, row, stride, directions, g=NARROW):
    fields, table = slopes(prim, row, stride, 4, g)
    drag = get(prim, 4 * g.plane + row, stride)
    spread = (2.0 / 3.0) * (table[0][0] + table[1][1] + table[2][2])
    field_cot = [[], [], []]
    drag_cot, spread_cot = [], []
    slope_cot = [[[] for _ in range(4)] for _ in range(3)]
    for k in directions:
        flux_cot = []
        for c in range(4):
            start = (1 + c) * g.plane + row
            if k == 2:
                own = get(cot, start, stride)
                flux_cot.append(0.5 * (ahead(own, -1) - ahead(own, 1)))
            else:
                step = g.pitch if k == 0 else 1
                flux_cot.append(
                    0.5 * (get(cot, start - step, stride) - get(cot, start + step, stride))
                )
        power = flux_cot[3]
        heat = CONDUCTION * power
        drag_cot.append(heat * table[k][3])
        slope_cot[k][3].append(heat * drag)
        for j in range(3):
            shape = strain(table, k, j)
            if j == k:
                shape = shape - spread
            stress_cot = flux_cot[j] + fields[j] * power
            field_cot[j].append(power * (drag * shape))
            drag_cot.append(stress_cot * shape)
            scaled = drag * stress_cot
            slope_cot[k][j].append(scaled)
            slope_cot[j][k].append(scaled)
            if j == k:
                spread_cot.append(scaled)
    spread_total = (2.0 / 3.0) * total_of(spread_cot)
    for j in range(3):
        slope_cot[j][j].append(-spread_total)
    put(prim_cot, 4 * g.plane + row, total_of(drag_cot), stride)
    for j in range(4):
        here = list(field_cot[j]) if j < 3 else []
        if slope_cot[2][j]:
            value = total_of(slope_cot[2][j])
            here.append(0.5 * (ahead(value, -1) - ahead(value, 1)))
        if here:
            put(prim_cot, j * g.plane + row, total_of(here), stride)
        for k in range(2):
            if slope_cot[k][j]:
                put(
                    prim_cot,
                    (5 + 4 * k + j) * g.plane + row,
                    0.5 * total_of(slope_cot[k][j]),
                    stride,
                )


def viscous_finish(prim, prim_cot, row, count, g, out):
    velocity = [get(prim, j * g.plane + row, count=count) for j in range(3)]
    thermal = get(prim, 3 * g.plane + row, count=count)
    inverse = get(prim, 6 * g.plane + row, count=count)
    molecular = get(prim, 7 * g.plane + row, count=count)
    field_cot = []
    for j in range(4):
        along = (5 + j) * g.plane + row
        across = (9 + j) * g.plane + row
        field_cot.append(
            get(prim_cot, j * g.plane + row, count=count)
            + (
                get(prim_cot, along - g.pitch, count=count)
                - get(prim_cot, along + g.pitch, count=count)
            )
            + (get(prim_cot, across - 1, count=count) - get(prim_cot, across + 1, count=count))
        )
    drag_cot = get(prim_cot, 4 * g.plane + row, count=count)
    thermal_cot = field_cot[3] + 0.7 * (drag_cot * molecular) / thermal
    push_cot = thermal_cot * inverse
    out[0] = out[0] - push_cot * thermal
    pull_push(out, velocity, push_cot)
    for j in range(3):
        scaled = field_cot[j] * inverse
        out[1 + j] = out[1 + j] + scaled
        out[0] = out[0] - scaled * velocity[j]
    return drag_cot


def viscous_pull(prim, cot, prim_cot, grad, front):
    clear_rows(prim_cot, 13 * PLANE)
    for edge in (2, 11):
        row = edge * PITCH + (front + 3)
        viscous_pull_at(prim, cot, prim_cot, row, 1, (0,))
        row = 3 * PITCH + (front + edge)
        viscous_pull_at(prim, cot, prim_cot, row, PITCH, (1,))

    def body(o):
        row = (o + 3) * PITCH + (front + 3)
        viscous_pull_at(prim, cot, prim_cot, row, 1, (0, 1, 2))

    loop(8, body, 4)

    def finish(i):
        row = i * 16 + 16
        out = [get(grad, c * PLANE + row, count=16) for c in range(6)]
        out[5] = out[5] + viscous_finish(prim, prim_cot, row, 16, NARROW, out)
        for c in range(6):
            put(grad, c * PLANE + row, out[c], count=16)

    loop(12, finish, 4)


def wide_viscous_pull(prim, cot, prim_cot, grad, drag_part):
    def body(x):
        viscous_pull_at(prim, cot, prim_cot, wide_row(x, 0), 1, (0, 1, 2), WIDE)

    for x in (-1, 8):
        body(x)
    for y in (-1, 8):
        viscous_pull_at(prim, cot, prim_cot, wide_row(0, y), 24, (0, 1, 2), WIDE)
    loop(8, body, 4)

    def finish(x):
        row = wide_row(x, 0)
        out = [get(grad, c * WIDE.plane + row) for c in range(5)]
        drag_cot = viscous_finish(prim, prim_cot, row, 8, WIDE, out)
        put(drag_part, pl.multiple_of(x * 8, 8), drag_cot)
        for c in range(5):
            put(grad, c * WIDE.plane + row, out[c])

    loop(8, finish, 4)


def clear_rows(ref, rows):
    clear_rows_from(ref, 0, rows)


def clear_rows_from(ref, first, rows):
    for row in range(first, first + rows, 32):
        put(ref, row, jnp.zeros((32, 128), jnp.float32), count=32)


X_ROWS = 68
X_MORE = 5 * X_ROWS
Y_MORE = 5 * 48


def x_pieces(left):
    pieces, place = [], 0
    for x in range(6):
        distance = 5 - x if left else x
        first, count = (0, 14) if distance < 3 else (2, 10) if distance == 3 else (3, 8)
        pieces.append((place, x, first, count))
        place += count
    return pieces


def assemble(padded, own, from_y, from_x, left):
    front, first, outer = frame(left)
    for c in range(5):
        for x in range(8):
            row = c * PLANE + (first + x) * PITCH + front
            put(padded, row + first, get(own, (c * 8 + x) * 8))
            put(padded, row + outer, get(from_y, (c * 8 + x) * 6, count=6), count=6)
        for place, x, cell, count in x_pieces(left):
            row = c * PLANE + (outer + x) * PITCH + front + cell
            put(padded, row, get(from_x, c * X_ROWS + place, count=count), count=count)


def assemble_eddy_left(padded, eddy, zero_y, zero_x):
    front = frame(True)[0]
    for x in range(8):
        row = 5 * PLANE + (6 + x) * PITCH + front
        put(padded, row + 6, get(eddy, x * 8))
        put(padded, row + 2, get(zero_y, Y_MORE + x * 4, count=4), count=4)
    for x in range(4):
        row = 5 * PLANE + (2 + x) * PITCH + front + 2
        put(padded, row, get(zero_x, X_MORE + x * 12, count=12), count=12)


def assemble_eddy_right(padded, eddy, zero_y, zero_x, one_y, one_x):
    base = 5 * PLANE
    for x in range(8):
        row = base + (3 + x) * PITCH
        put(padded, row + 3, get(eddy, x * 8))
        put(padded, row + 2, get(zero_y, Y_MORE + x * 4 + 3, count=1), count=1)
        put(padded, row + 11, get(one_y, Y_MORE + x, count=1), count=1)
    put(padded, base + 2 * PITCH + 3, get(zero_x, X_MORE + 3 * 12 + 4))
    put(padded, base + 11 * PITCH + 3, get(one_x, X_MORE))


def start_kernel(state, eddy, send_y):
    for i in range(40):
        put(send_y, i * 6, get(state, i * 8 + 2, count=6), count=6)
    for x in range(8):
        put(send_y, Y_MORE + x * 4, get(eddy, x * 8 + 4, count=4), count=4)


def side_kernel(left, own, from_y, more, send_x, line):
    front, first, outer = frame(left)
    begin = 2 if left else 0
    for c in range(5):
        for x in range(6):
            source = c * 8 + begin + x
            row = (c * 6 + x) * PITCH + front
            put(line, row + first, get(own, source * 8))
            put(line, row + outer, get(from_y, source * 6, count=6), count=6)
        for place, x, cell, count in x_pieces(left):
            value = get(line, (c * 6 + x) * PITCH + front + cell, count=count)
            put(send_x, c * X_ROWS + place, value, count=count)
    if left:
        for x in range(4):
            row = X_MORE + x * 12
            put(send_x, row, get(from_y, Y_MORE + (4 + x) * 4, count=4), count=4)
            put(send_x, row + 4, get(more, (4 + x) * 8))
    else:
        put(send_x, X_MORE, get(more, 0))


def section_body(left, keep, weight, base, column, out, padded, prim, split, rate, flux_x, flux_y):
    front = frame(left)[0]
    fill_prim(padded, prim)
    line_rate(padded, prim, split, rate, 0, front, True)
    line_rate(padded, prim, split, rate, 1, front, False)
    column_rate(padded, prim, rate, front, range(3) if left else range(5, 8))
    early = 3 if left else 0
    for c in range(5):
        add(rate, (c * 8 + early) * 8, get(column, c * 40, count=40), count=40)
    viscous_rate(prim, flux_x, flux_y, rate, front)
    for x in range(8):
        row = (x + 3) * PITCH + (front + 3)
        for c in range(5):
            place = (c * 8 + x) * 8
            value = weight * get(padded, c * PLANE + row) + (weight * TIME_STEP) * get(rate, place)
            if keep:
                value = value + keep * get(base, place)
            put(out, place, value)


def first_section_kernel(state, zero_y, zero_x, eddy, column, out, send_y, padded, *scratch):
    assemble(padded, state, zero_y, zero_x, True)
    assemble_eddy_left(padded, eddy, zero_y, zero_x)
    section_body(True, 0.0, 1.0, None, column, out, padded, *scratch)
    for i in range(40):
        put(send_y, i * 6, get(out, i * 8, count=6), count=6)
    for x in range(8):
        put(send_y, Y_MORE + x, get(eddy, x * 8, count=1), count=1)


def second_section_kernel(
    own, one_y, one_x, zero_y, zero_x, eddy, state, adjoint, column, out, *refs
):
    send_up, send_down, padded, *scratch = refs
    assemble(padded, own, one_y, one_x, False)
    assemble_eddy_right(padded, eddy, zero_y, zero_x, one_y, one_x)
    section_body(False, 0.75, 0.25, state, column, out, padded, *scratch)
    for i in range(40):
        put(send_up, i * 5, get(out, i * 8 + 3, count=5), count=5)
        put(send_up, 200 + i * 3, get(adjoint, i * 8 + 5, count=3), count=3)
        put(send_down, i * 5, get(out, i * 8, count=5), count=5)
        put(send_down, 200 + i * 3, get(adjoint, i * 8, count=3), count=3)


def first_tangent_kernel(state, zero_y, zero_x, eddy, padded, prim, tangent, split):
    assemble(padded, state, zero_y, zero_x, True)
    assemble_eddy_left(padded, eddy, zero_y, zero_x)
    fill_prim(padded, prim)
    line_tangent(padded, prim, split, tangent, 0, frame(True)[0])


def second_tangent_kernel(own, one_y, one_x, zero_y, zero_x, eddy, padded, prim, tangent, split):
    assemble(padded, own, one_y, one_x, False)
    assemble_eddy_right(padded, eddy, zero_y, zero_x, one_y, one_x)
    fill_prim(padded, prim)
    line_tangent(padded, prim, split, tangent, 0, frame(False)[0])


def line_tangent_kernel(left, padded, prim, tangent, split):
    line_tangent(padded, prim, split, tangent, 1, frame(left)[0])


def first_line_and_column_kernel(padded, prim, own, from_y, tangent, column, split, line):
    line_tangent_kernel(True, padded, prim, tangent, split)
    early_column_kernel(False, own, from_y, column, line)


def column_tangent_kernel(left, padded, prim, tangent):
    column_tangent(padded, prim, tangent, frame(left)[0])


def own_column_kernel(own, adjoint, part):
    def body(x):
        rows = [pl.multiple_of((c * 8 + x) * 8, 8) for c in range(5)]
        cells = [get(own, row) for row in rows]
        inverse = 1.0 / cells[0]
        velocity = [cells[1 + j] * inverse for j in range(3)]
        kinetic = 0.5 * (
            cells[1] * velocity[0] + cells[2] * velocity[1] + cells[3] * velocity[2]
        )
        push = (HEAT_RATIO - 1.0) * (cells[4] - kinetic)
        cot = [(2.0 / 3.0 * TIME_STEP) * get(adjoint, row) for row in rows]
        out = column_cot(cells, velocity, push, inverse, cot)
        for row, value in zip(rows, out):
            put(part, row, value)

    loop(8, body, 4)


def hand_back(left, grad, send_x, rest):
    front, first, outer = frame(left)
    for c in range(5):
        for place, x, cell, count in x_pieces(left):
            row = c * PLANE + (outer + x) * PITCH + front + cell
            put(send_x, c * X_ROWS + place, get(grad, row, count=count), count=count)
        row = c * PLANE + first * PITCH
        put(rest, c * 128, get(grad, row, count=128), count=128)


def wide_side_kernel(own, low_y, high_y, adjoint, send_up, send_down):
    for send, first, layer, near in ((send_up, 3, 5, 7), (send_down, 0, 0, 0)):
        for c in range(5):
            put(send, c * 40, get(own, (c * 8 + first) * 8, count=40), count=40)
            put(send, 200 + c * 24, get(adjoint, (c * 8 + layer) * 8, count=24), count=24)
            corner = c * 8 + near
            put(send, 320 + c * 4, get(low_y, corner * 5 + 4, count=1), count=1)
            put(send, 321 + c * 4, get(high_y, corner * 5, count=1), count=1)
            put(send, 322 + c * 4, get(low_y, 202 + corner * 3, count=1), count=1)
            put(send, 323 + c * 4, get(high_y, 200 + corner * 3, count=1), count=1)


def wide_assemble(padded, cot, own, low_y, high_y, low_x, high_x, adjoint, edges):
    zero_y, zero_x, one_y, one_x, eddy = edges
    for c in range(5):
        base = c * WIDE.plane
        for x in range(8):
            row, source = base + wide_row(x, 0), c * 8 + x
            put(padded, row, get(own, source * 8))
            put(padded, row - 5, get(low_y, source * 5, count=5), count=5)
            put(padded, row + 8, get(high_y, source * 5, count=5), count=5)
            put(cot, row, get(adjoint, source * 8))
            put(cot, row - 3, get(low_y, 200 + source * 3, count=3), count=3)
            put(cot, row + 8, get(high_y, 200 + source * 3, count=3), count=3)
        for r in range(5):
            put(padded, base + wide_row(r - 5, 0), get(low_x, (c * 5 + r) * 8))
            put(padded, base + wide_row(r + 8, 0), get(high_x, (c * 5 + r) * 8))
        for r in range(3):
            put(cot, base + wide_row(r - 3, 0), get(low_x, 200 + (c * 3 + r) * 8))
            put(cot, base + wide_row(r + 8, 0), get(high_x, 200 + (c * 3 + r) * 8))
        for x, source in ((-1, low_x), (8, high_x)):
            for k, (ref, y) in enumerate(((padded, -1), (padded, 8), (cot, -1), (cot, 8))):
                row = base + wide_row(x, y)
                put(ref, row, get(source, 320 + c * 4 + k, count=1), count=1)
    base = 5 * WIDE.plane
    for x in range(8):
        put(padded, base + wide_row(x, 0), get(eddy, x * 8))
        put(padded, base + wide_row(x, -1), get(zero_y, Y_MORE + x * 4 + 3, count=1), count=1)
        put(padded, base + wide_row(x, 8), get(one_y, Y_MORE + x, count=1), count=1)
    put(padded, base + wide_row(-1, 0), get(zero_x, X_MORE + 3 * 12 + 4))
    put(padded, base + wide_row(8, 0), get(one_x, X_MORE))


def last_section_kernel(
    own, low_y, high_y, low_x, high_x, zero_y, zero_x, one_y, one_x, eddy, adjoint, column_part, *refs
):
    adjoint_two, drag_part, padded, prim, split, split_cot, cot, prim_cot, grad = refs
    scale = 2.0 / 3.0
    edges = zero_y, zero_x, one_y, one_x, eddy
    wide_assemble(padded, cot, own, low_y, high_y, low_x, high_x, adjoint, edges)
    fill_prim(padded, prim, WIDE.plane, 48)
    for c in range(5):
        for x in range(8):
            put(grad, c * WIDE.plane + wide_row(x, 0), jnp.zeros((8, 128), jnp.float32))
    wide_viscous_pull(prim, cot, prim_cot, grad, drag_part)
    kept = range(5, 13)
    line_pull(padded, prim, split, split_cot, cot, grad, 1, WIDE, kept)
    line_pull(padded, prim, split, split_cot, cot, grad, 0, WIDE, kept)
    for c in range(5):
        for x in range(8):
            row, place = c * WIDE.plane + wide_row(x, 0), (c * 8 + x) * 8
            value = scale * get(adjoint, place) + (scale * TIME_STEP) * get(grad, row)
            put(adjoint_two, place, value + get(column_part, place))
    for x in range(8):
        put(drag_part, x * 8, (scale * TIME_STEP) * get(drag_part, x * 8))


def earlier_section(left, scale, cells, tangents, rest_in, folded_y, scratch):
    padded, prim = cells
    along_x, along_y, along_z = tangents
    split_cot, cot, prim_cot, grad, folded = scratch
    front = frame(left)[0]
    clear_rows(cot, 5 * PLANE)
    clear_rows(grad, 5 * PLANE)
    begin = 0 if left else 2
    for i in range(40):
        put(folded, i * 8, get(rest_in, i * 8))
        if folded_y is not None:
            add(folded, i * 8 + begin, get(folded_y, i * 6, count=6), count=6)
    for c in range(5):
        for x in range(8):
            row = c * PLANE + (3 + x) * PITCH + (front + 3)
            value = scale * get(folded, (c * 8 + x) * 8)
            put(cot, row, TIME_STEP * value)
            put(grad, row, value)
    viscous_pull(prim, cot, prim_cot, grad, front)
    g = narrow(front)
    line_pull(padded, prim, None, split_cot, cot, grad, 1, g, range(14), along_y)
    line_pull(padded, prim, None, split_cot, cot, grad, 0, g, range(14), along_x)
    column_pull(padded, prim, cot, grad, front, along_z)


def second_pull_kernel(
    padded, prim, along_x, along_y, along_z, adjoint_two, send_x, rest, drag_part, *scratch
):
    grad = scratch[3]
    clear_rows_from(grad, 5 * PLANE, PLANE)
    earlier_section(
        False, 0.25, (padded, prim), (along_x, along_y, along_z), adjoint_two, None, scratch
    )
    hand_back(False, grad, send_x, rest)
    put(send_x, X_MORE, get(grad, 5 * PLANE + 11 * PITCH + 3))
    put(drag_part, 0, get(grad, 5 * PLANE, count=PLANE), count=PLANE)


def first_pull_kernel(
    padded, prim, along_x, along_y, along_z, rest_in, folded_y, folded_x, drag_two, drag_one, *refs
):
    send_x, rest = refs[:2]
    scratch = refs[2:]
    grad = scratch[3]
    front = frame(True)[0]
    clear_rows_from(grad, 5 * PLANE, PLANE)
    for x in range(8):
        put(grad, 5 * PLANE + (6 + x) * PITCH + front + 6, get(drag_two, x * 8))
    for x in range(9):
        row = 5 * PLANE + (5 + x) * PITCH + front + 5
        add(grad, row, get(drag_one, (2 + x) * PITCH + 2, count=9), count=9)
    add(grad, 5 * PLANE + 6 * PITCH + front + 6, get(folded_x, X_MORE))
    for x in range(8):
        row = 5 * PLANE + (6 + x) * PITCH + front + 6
        add(grad, row, get(folded_y, Y_MORE + x, count=1), count=1)
    earlier_section(
        True, 1.0, (padded, prim), (along_x, along_y, along_z), rest_in, folded_y, scratch
    )
    hand_back(True, grad, send_x, rest)
    for x in range(4):
        row = 5 * PLANE + (2 + x) * PITCH + front + 2
        put(send_x, X_MORE + x * 12, get(grad, row, count=12), count=12)
    put(rest, 640, get(grad, 5 * PLANE + 6 * PITCH, count=128), count=128)


def fold_rows(left, rest_in, from_x, rest, send_y, work):
    front, first, outer = frame(left)
    begin = 2 if left else 0
    put(work, 0, get(rest_in, 0, count=640), count=640)
    for c in range(5):
        for place, x, cell, count in x_pieces(left):
            row = (c * 8 + begin + x) * PITCH + front + cell
            add(work, row, get(from_x, c * X_ROWS + place, count=count), count=count)
    for i in range(40):
        put(rest, i * 8, get(work, i * PITCH + front + first))
        put(send_y, i * 6, get(work, i * PITCH + front + outer, count=6), count=6)


def second_fold_kernel(rest_in, from_x, drag_part, rest, send_y, work):
    fold_rows(False, rest_in, from_x, rest, send_y, work)
    for x in range(8):
        put(send_y, Y_MORE + x, get(drag_part, (3 + x) * PITCH + 11, count=1), count=1)


def first_fold_kernel(rest_in, from_x, rest, send_y, work):
    fold_rows(True, rest_in, from_x, rest, send_y, work)
    put(work, 640, get(rest_in, 640, count=128), count=128)
    front = frame(True)[0]
    for x in range(4):
        row = 640 + (4 + x) * PITCH + front + 2
        add(work, row, get(from_x, X_MORE + x * 12, count=12), count=12)
    for x in range(8):
        put(rest, 320 + x * 8, get(work, 640 + x * PITCH + front + 6))
        row = 640 + x * PITCH + front + 2
        put(send_y, Y_MORE + x * 4, get(work, row, count=4), count=4)


def end_kernel(adjoint, adjoint_two, rest_zero, folded_zero, grad_state, grad_eddy):
    for i in range(40):
        value = (1.0 / 3.0) * get(adjoint, i * 8) + 0.75 * get(adjoint_two, i * 8)
        put(grad_state, i * 8, value + get(rest_zero, i * 8))
        add(grad_state, i * 8 + 2, get(folded_zero, i * 6, count=6), count=6)
    for i in range(8):
        put(grad_eddy, i * 8, get(rest_zero, 320 + i * 8))
        add(grad_eddy, i * 8 + 4, get(folded_zero, Y_MORE + i * 4, count=4), count=4)


def run(kernel, operands, outs, scratch=(), work=0):
    cost = pl.CostEstimate(flops=work, bytes_accessed=4 * work, transcendentals=0) if work else None
    return pl.pallas_call(
        kernel,
        out_shape=[jax.ShapeDtypeStruct((rows, 128), jnp.float32) for rows in outs],
        in_specs=[pl.BlockSpec(memory_space=pltpu.VMEM)] * len(operands),
        out_specs=[pl.BlockSpec(memory_space=pltpu.VMEM)] * len(outs),
        scratch_shapes=[pltpu.VMEM((rows, 128), jnp.float32) for rows in scratch],
        compiler_params=pltpu.CompilerParams(vmem_limit_bytes=20 * 1024 * 1024),
        cost_estimate=cost,
    )(*operands)


def shifted(values, axis, up):
    count = lax.axis_size(axis)
    step = 1 if up else count - 1
    return lax.ppermute(values, axis, [(i, (i + step) % count) for i in range(count)])


def together(*values):
    return lax.optimization_barrier(values)


def shifted_beside(values, axis, up, kernel, operands, outs, scratch=()):
    values, *operands = together(values, *operands)
    moved = shifted(values, axis, up)
    moved, *results = together(moved, *run(kernel, operands, outs, scratch, 2_000_000))
    return moved, results


def shifted_both_beside(up, down, axis, first_job, second_job):
    kernel, given, outs, scratch = first_job
    up, *given = together(up, *given)
    low = shifted(up, axis, True)
    first = run(kernel, given, outs, scratch, 2_000_000)
    kernel, given, outs, scratch = second_job
    down, *rest = together(down, *first, *given)
    first, given = rest[: len(first)], rest[len(first) :]
    high = shifted(down, axis, False)
    second = run(kernel, given, outs, scratch, 2_000_000)
    low, high, *rest = together(low, high, *first, *second)
    return low, high, rest[: len(first)], rest[len(first) :]


def pipeline(state, eddy, adjoint):
    section_scratch = (6 * PLANE, 8 * PLANE, 1120, 320, 4 * PLANE, 4 * PLANE)
    wide = WIDE.plane
    last_scratch = (6 * wide, 8 * wide, 1440, 1440, 5 * wide, 13 * wide, 5 * wide)
    earlier_scratch = (1120, 5 * PLANE, 13 * PLANE, 6 * PLANE, 320)
    first_tangent = [6 * PLANE, 8 * PLANE, 2880]

    def sides(own, from_y, more, left, rows):
        (send_x,) = run(
            functools.partial(side_kernel, left),
            [own, from_y, more],
            [X_MORE + rows],
            [5 * 6 * PITCH],
        )
        return send_x

    (send_y,) = run(start_kernel, [state, eddy], [Y_MORE + 32])
    zero_y = shifted(send_y, "gy", True)
    zero_x, (column,) = shifted_beside(
        sides(state, zero_y, eddy, True, 48),
        "gx",
        True,
        functools.partial(early_column_kernel, True),
        [state, zero_y],
        [200],
        [80],
    )
    zero = [state, zero_y, zero_x, eddy]
    one, send_y = run(first_section_kernel, [*zero, column], [320, Y_MORE + 8], section_scratch)

    one_y, (zero_cells, zero_prim, zero_along_x) = shifted_beside(
        send_y, "gy", False, first_tangent_kernel, zero, first_tangent, [1120]
    )
    one_x, (zero_along_y, column) = shifted_beside(
        sides(one, one_y, eddy, False, 8),
        "gx",
        False,
        first_line_and_column_kernel,
        [zero_cells, zero_prim, one, one_y],
        [2880, 200],
        [1120, 80],
    )
    one_all = [one, one_y, one_x, zero_y, zero_x, eddy]
    two, send_up, send_down = run(
        second_section_kernel, [*one_all, state, adjoint, column], [320, 320, 320], section_scratch
    )

    low_y, high_y, (one_cells, one_prim, one_along_x), (column_part,) = shifted_both_beside(
        send_up,
        send_down,
        "gy",
        (second_tangent_kernel, one_all, first_tangent, [1120]),
        (own_column_kernel, [two, adjoint], [320], []),
    )
    send_up, send_down = run(wide_side_kernel, [two, low_y, high_y, adjoint], [340, 340])
    low_x, high_x, (one_along_y,), (one_along_z,) = shifted_both_beside(
        send_up,
        send_down,
        "gx",
        (functools.partial(line_tangent_kernel, False), [one_cells, one_prim], [2880], [1120]),
        (functools.partial(column_tangent_kernel, False), [one_cells, one_prim], [2560], []),
    )
    adjoint_two, drag_two = run(
        last_section_kernel,
        [
            *(two, low_y, high_y, low_x, high_x, zero_y, zero_x, one_y, one_x),
            *(eddy, adjoint, column_part),
        ],
        [320, 64],
        last_scratch,
    )

    one_tangents = [one_along_x, one_along_y, one_along_z]
    send_x, rest, drag_one = run(
        second_pull_kernel,
        [one_cells, one_prim, *one_tangents, adjoint_two],
        [X_MORE + 8, 640, PLANE],
        earlier_scratch,
    )
    from_x, (zero_along_z,) = shifted_beside(
        send_x,
        "gx",
        True,
        functools.partial(column_tangent_kernel, True),
        [zero_cells, zero_prim],
        [2560],
    )
    rest_one, send_y = run(second_fold_kernel, [rest, from_x, drag_one], [320, Y_MORE + 8], [640])
    folded_one = shifted(send_y, "gy", True)

    zero_tangents = [zero_along_x, zero_along_y, zero_along_z]
    send_x, rest = run(
        first_pull_kernel,
        [zero_cells, zero_prim, *zero_tangents, rest_one, folded_one, from_x, drag_two, drag_one],
        [X_MORE + 48, 768],
        earlier_scratch,
    )
    from_x = shifted(send_x, "gx", False)
    rest_zero, send_y = run(first_fold_kernel, [rest, from_x], [384, Y_MORE + 32], [768])
    folded_zero = shifted(send_y, "gy", False)
    return run(end_kernel, [adjoint, adjoint_two, rest_zero, folded_zero], [320, 64])


def on_device(state, eddy, adjoint):
    grad_state, grad_eddy = pipeline(
        state.reshape(320, 128), eddy.reshape(64, 128), adjoint.reshape(320, 128)
    )
    return grad_state.reshape(5, 8, 8, 128), grad_eddy.reshape(8, 8, 128)


def solution(mesh):
    placed = (P(None, "gx", "gy", None), P("gx", "gy", None), P(None, "gx", "gy", None))
    return jax.shard_map(
        on_device,
        mesh=mesh,
        in_specs=placed,
        out_specs=(P(None, "gx", "gy", None), P("gx", "gy", None)),
        check_vma=False,
    )
```

```python
import collections
import functools

import jax
import jax.numpy as jnp
from jax import lax
from jax.experimental import pallas as pl
from jax.experimental.pallas import tpu as pltpu
from jax.sharding import PartitionSpec as P

HEAT_RATIO = 1.4
MOLECULAR_DRAG = 0.05
PRANDTL = 0.72
TIME_STEP = 0.04
SMOOTH_EPS = 1e-06
CONDUCTION = HEAT_RATIO / ((HEAT_RATIO - 1.0) * PRANDTL)
SMALL = 0.75 * SMOOTH_EPS

PITCH = 16
PLANE = 14 * PITCH


def frame(left):
    return (2, 6, 0) if left else (0, 0, 8)


Grid = collections.namedtuple("Grid", ["pitch", "plane", "leads", "x_start", "y_start"])


def narrow(front):
    return Grid(PITCH, PLANE, 14, front + 3, 3 * PITCH + front)


WIDE = Grid(24, 18 * 24, 18, 8, 5 * 24 + 3)


NARROW = narrow(0)


def wide_row(x, y):
    return (x + 5) * 24 + 8 + y


def get(ref, start, stride=1, count=8):
    if stride == 1:
        return ref[pl.ds(start, count), :]
    return ref[pl.ds(start, count, stride=stride), :]


def put(ref, start, value, stride=1, count=8):
    if stride == 1:
        ref[pl.ds(start, count), :] = value
    else:
        ref[pl.ds(start, count, stride=stride), :] = value


def add(ref, start, value, stride=1, count=8):
    put(ref, start, get(ref, start, stride, count) + value, stride, count)


def ahead(value, offset):
    return pltpu.roll(value, (-offset) % 128, 1)


def quick_inverse(value):
    return pl.reciprocal(value, approx=True)


def loop(count, body, together=1):
    def step(i, carry):
        for k in range(together):
            body(i * together + k)
        return carry

    lax.fori_loop(0, count // together, step, 0)


class Slope:
    def __init__(self, value):
        self.value = value
        self.kept = {}

    def times(self, factor):
        if factor == 1.0:
            return self.value
        if factor not in self.kept:
            self.kept[factor] = factor * self.value
        return self.kept[factor]

    def square(self):
        if 0 not in self.kept:
            self.kept[0] = self.value * self.value + SMALL
        return self.kept[0]


def weno_parts(d1, d2, d3, d4):
    i1 = quick_inverse(d1.square() + d2.value * (d2.times(2.5) - d1.times(2.75)))
    i2 = quick_inverse(d2.square() + d3.value * (d3.value - d2.times(1.25)))
    i3 = quick_inverse(d4.square() + d3.value * (d3.times(2.5) - d4.times(2.75)))
    w1, w2, w3 = i1 * i1, 6.0 * (i2 * i2), 3.0 * (i3 * i3)
    m1 = d2.times(2.5) - d1.value
    m2 = d2.times(0.5) + d3.value
    m3 = d3.times(2.0) - d4.times(0.5)
    inverse = quick_inverse(w1 + w2 + w3)
    mean = (w1 * m1 + w2 * m2 + w3 * m3) * inverse
    return (i1, i2, i3), (w1, w2, w3), (m1, m2, m3), inverse, mean


def weno_rise(d1, d2, d3, d4):
    return weno_parts(d1, d2, d3, d4)[4]


def weno_pull(d1, d2, d3, d4, third=None):
    (i1, i2, i3), (w1, w2, w3), (m1, m2, m3), inverse, mean = weno_parts(d1, d2, d3, d4)
    scaled = inverse if third is None else third * inverse
    e1, e2, e3 = w1 * scaled, w2 * scaled, w3 * scaled
    g1 = (e1 * i1) * (mean - m1)
    g2 = (e2 * i2) * (mean - m2)
    g3 = (e3 * i3) * (mean - m3)
    c1 = g1 * (d1.times(4.0) - d2.times(5.5)) - e1
    c2 = g1 * (d2.times(10.0) - d1.times(5.5)) + g2 * (d2.times(4.0) - d3.times(2.5))
    c2 = c2 + (2.5 * e1 + 0.5 * e2)
    c3 = g2 * (d3.times(4.0) - d2.times(2.5)) + g3 * (d3.times(10.0) - d4.times(5.5))
    c3 = c3 + (e2 + 2.0 * e3)
    c4 = g3 * (d4.times(4.0) - d3.times(5.5)) - 0.5 * e3
    return c1, c2, c3, c4


def split_flux(cells, speed, push, direction):
    fluxes = [cells[1 + direction]]
    for j in range(3):
        momentum_flux = cells[1 + j] * speed
        fluxes.append(momentum_flux + push if j == direction else momentum_flux)
    fluxes.append((cells[4] + push) * speed)
    plus, minus = [], []
    for flux, cell in zip(fluxes, cells):
        half, double = 0.5 * flux, 2.0 * cell
        plus.append(half + double)
        minus.append(half - double)
    return plus, minus


def pull_flux(cells, velocity, push, inverse_rho, direction, cot, out):
    speed = velocity[direction]
    speed_cot = cot[4] * (cells[4] + push)
    for j in range(3):
        speed_cot = speed_cot + cot[1 + j] * cells[1 + j]
        out[1 + j] = out[1 + j] + cot[1 + j] * speed
    through = cot[4] * speed
    out[4] = out[4] + through
    pull_push(out, velocity, cot[1 + direction] + through)
    speed_cot = speed_cot * inverse_rho
    out[1 + direction] = out[1 + direction] + cot[0] + speed_cot
    out[0] = out[0] - speed_cot * speed


def pull_push(out, velocity, push_cot):
    scaled = 0.4 * push_cot
    out[4] = out[4] + scaled
    square = velocity[0] * velocity[0] + velocity[1] * velocity[1] + velocity[2] * velocity[2]
    out[0] = out[0] + 0.5 * (scaled * square)
    for j in range(3):
        out[1 + j] = out[1 + j] - scaled * velocity[j]


def fill_prim(padded, prim, plane=PLANE, count=32):
    def body(i):
        row = i * count
        cells = [get(padded, c * plane + row, count=count) for c in range(6)]
        inverse = 1.0 / cells[0]
        velocity = [cells[1 + j] * inverse for j in range(3)]
        kinetic = 0.5 * (
            cells[1] * velocity[0] + cells[2] * velocity[1] + cells[3] * velocity[2]
        )
        push = (HEAT_RATIO - 1.0) * (cells[4] - kinetic)
        thermal = push * inverse
        molecular = MOLECULAR_DRAG * jnp.exp(0.7 * jnp.log(thermal))
        values = velocity + [thermal, molecular + cells[5], push, inverse, molecular]
        for k, value in enumerate(values):
            put(prim, k * plane + row, value, count=count)

    loop(plane // count, body)


def line_layout(direction, g):
    if direction == 0:
        return lambda lead: lead * g.pitch + g.x_start, 1
    return lambda lead: lead + g.y_start, g.pitch


def fill_split(padded, prim, split, direction, g):
    place, stride = line_layout(direction, g)
    for lead in range(g.leads):
        row = place(lead)
        cells = [get(padded, c * g.plane + row, stride) for c in range(5)]
        speed = get(prim, direction * g.plane + row, stride)
        push = get(prim, 5 * g.plane + row, stride)
        plus, minus = split_flux(cells, speed, push, direction)
        for c in range(5):
            put(split, (c * g.leads + lead) * 8, plus[c])
            put(split, ((5 + c) * g.leads + lead) * 8, minus[c])


def line_slopes(split, c, leads):
    plus = [get(split, pl.multiple_of((c * leads + k) * 8, 8)) for k in range(leads)]
    minus = [get(split, pl.multiple_of(((5 + c) * leads + k) * 8, 8)) for k in range(leads)]
    plus_slopes = [Slope(plus[k + 1] - plus[k]) for k in range(leads - 1)]
    minus_slopes = [Slope(minus[k + 1] - minus[k]) for k in range(leads - 1)]
    return plus, minus, plus_slopes, minus_slopes


def line_rate(padded, prim, split, rate, direction, front, first):
    fill_split(padded, prim, split, direction, narrow(front))

    def body(c):
        plus, minus, ps, ms = line_slopes(split, c, 14)
        low = None
        for f in range(9):
            rise = weno_rise(*ps[f : f + 4]) - weno_rise(ms[f + 4], ms[f + 3], ms[f + 2], ms[f + 1])
            face = (plus[f + 2] + minus[f + 3]) + (1.0 / 3.0) * rise
            if f:
                row, stride = (c * 64 + (f - 1) * 8, 1) if direction == 0 else (c * 64 + f - 1, 8)
                value = low - face
                if not first:
                    value = value + get(rate, row, stride)
                put(rate, row, value, stride)
            low = face

    loop(5, body, 5)


def line_tangent(padded, prim, split, tangent, direction, front):
    fill_split(padded, prim, split, direction, narrow(front))

    def body(c):
        _, _, ps, ms = line_slopes(split, c, 14)
        for f in range(9):
            plus = weno_pull(*ps[f : f + 4])
            minus = weno_pull(ms[f + 4], ms[f + 3], ms[f + 2], ms[f + 1])
            for k, value in enumerate(plus + minus):
                put(tangent, pl.multiple_of((c * 9 + f) * 64, 8) + k * 8, value)

    loop(5, body)


def line_pull(padded, prim, split, split_cot, cot, grad, direction, g, kept, tangent=None):
    place, stride = line_layout(direction, g)
    leads, faces = g.leads, g.leads - 5
    if tangent is None:
        fill_split(padded, prim, split, direction, g)

    def body(c):
        if tangent is None:
            _, _, ps, ms = line_slopes(split, c, leads)
        own = [get(cot, c * g.plane + place(lead), stride) for lead in range(2, leads - 2)]
        plus_cot, minus_cot = [None] * leads, [None] * leads

        def gather(table, lead, value):
            if lead in kept:
                table[lead] = value if table[lead] is None else table[lead] + value

        for f in range(faces):
            face = own[f + 1] - own[f]
            third = (1.0 / 3.0) * face
            if tangent is None:
                plus = weno_pull(*ps[f : f + 4], third)
                minus = weno_pull(ms[f + 4], ms[f + 3], ms[f + 2], ms[f + 1], -third)
            else:
                first = pl.multiple_of((c * 9 + f) * 64, 8)
                plus = [third * get(tangent, first + k * 8) for k in range(4)]
                minus = [-third * get(tangent, first + k * 8) for k in range(4, 8)]
            c1, c2, c3, c4 = plus
            for k, value in enumerate((-c1, c1 - c2, (face + c2) - c3, c3 - c4, c4)):
                gather(plus_cot, f + k, value)
            c1, c2, c3, c4 = minus
            for k, value in enumerate((-c4, c4 - c3, (face + c3) - c2, c2 - c1, c1)):
                gather(minus_cot, f + 1 + k, value)
            for lead in range(f, f + 1 if f < faces - 1 else leads):
                if lead not in kept:
                    continue
                p, m = plus_cot[lead], minus_cot[lead]
                if p is None:
                    total, gap = m, -m
                elif m is None:
                    total, gap = p, p
                else:
                    total, gap = p + m, p - m
                put(split_cot, pl.multiple_of((c * leads + lead) * 8, 8), 0.5 * total)
                put(split_cot, pl.multiple_of(((5 + c) * leads + lead) * 8, 8), 2.0 * gap)

    loop(5, body)
    for lead in kept:
        row = place(lead)
        cells = [get(padded, c * g.plane + row, stride) for c in range(5)]
        velocity = [get(prim, c * g.plane + row, stride) for c in range(3)]
        push = get(prim, 5 * g.plane + row, stride)
        inverse = get(prim, 6 * g.plane + row, stride)
        flux_cot = [get(split_cot, (c * leads + lead) * 8) for c in range(5)]
        out = [get(split_cot, ((5 + c) * leads + lead) * 8) for c in range(5)]
        pull_flux(cells, velocity, push, inverse, direction, flux_cot, out)
        for c in range(5):
            add(grad, c * g.plane + row, out[c], stride)


def column_change(cells, speed, push):
    plus, minus = split_flux(cells, speed, push, 2)
    changes = []
    for c in range(5):
        next_minus = ahead(minus[c], 1)
        dp, dm = ahead(plus[c], 1) - plus[c], next_minus - minus[c]
        rise = weno_rise(*[Slope(v) for v in (ahead(dp, -2), ahead(dp, -1), dp, ahead(dp, 1))])
        rise = rise - weno_rise(
            *[Slope(v) for v in (ahead(dm, 2), ahead(dm, 1), dm, ahead(dm, -1))]
        )
        face = (plus[c] + next_minus) + (1.0 / 3.0) * rise
        changes.append(ahead(face, -1) - face)
    return changes


def column_rate(padded, prim, rate, front, rows):
    for o in rows:
        row = (o + 3) * PITCH + (front + 3)
        cells = [get(padded, c * PLANE + row) for c in range(5)]
        changes = column_change(cells, get(prim, 2 * PLANE + row), get(prim, 5 * PLANE + row))
        for c in range(5):
            add(rate, (c * 8 + o) * 8, changes[c])


def early_column_kernel(left, own, from_y, column, line):
    for i in range(5):
        x = i if left else 3 + i
        for c in range(5):
            source, row = c * 8 + x, c * 16
            if left:
                put(line, row, get(from_y, source * 6 + 3, count=3), count=3)
                put(line, row + 3, get(own, source * 8, count=5), count=5)
            else:
                put(line, row, get(own, source * 8 + 3, count=5), count=5)
                put(line, row + 5, get(from_y, source * 6, count=3), count=3)
        cells = [get(line, c * 16) for c in range(5)]
        inverse = 1.0 / cells[0]
        velocity = [cells[1 + j] * inverse for j in range(3)]
        kinetic = 0.5 * (
            cells[1] * velocity[0] + cells[2] * velocity[1] + cells[3] * velocity[2]
        )
        push = (HEAT_RATIO - 1.0) * (cells[4] - kinetic)
        changes = column_change(cells, velocity[2], push)
        for c in range(5):
            put(column, (c * 5 + i) * 8, changes[c])


def column_slopes(plus, minus):
    dp = ahead(plus, 1) - plus
    dm = ahead(minus, 1) - minus
    return (
        [Slope(value) for value in (ahead(dp, -2), ahead(dp, -1), dp, ahead(dp, 1))],
        [Slope(value) for value in (ahead(dm, 2), ahead(dm, 1), dm, ahead(dm, -1))],
    )


def column_tangent(padded, prim, tangent, front):
    def body(o):
        row = (o + 3) * PITCH + (front + 3)
        cells = [get(padded, c * PLANE + row) for c in range(5)]
        plus, minus = split_flux(cells, get(prim, 2 * PLANE + row), get(prim, 5 * PLANE + row), 2)
        for c in range(5):
            ps, ms = column_slopes(plus[c], minus[c])
            for k, value in enumerate(weno_pull(*ps) + weno_pull(*ms)):
                put(tangent, pl.multiple_of((c * 8 + o) * 64, 8) + k * 8, value)

    loop(8, body, 4)


def column_cot(cells, velocity, push, inverse, cot, factors=None):
    if factors is None:
        plus, minus = split_flux(cells, velocity[2], push, 2)
    flux_cot, out = [], []
    for c in range(5):
        face = ahead(cot[c], 1) - cot[c]
        third = (1.0 / 3.0) * face
        if factors is None:
            ps, ms = column_slopes(plus[c], minus[c])
            plus_parts, minus_parts = weno_pull(*ps, third), weno_pull(*ms, -third)
        else:
            plus_parts = [third * value for value in factors[c][:4]]
            minus_parts = [-third * value for value in factors[c][4:]]
        c1, c2, c3, c4 = plus_parts
        total = (c3 + ahead(c1, 2)) + (ahead(c2, 1) + ahead(c4, -1))
        p = face + (ahead(total, -1) - total)
        c1, c2, c3, c4 = minus_parts
        total = (c3 + ahead(c1, -2)) + (ahead(c2, -1) + ahead(c4, 1))
        m = ahead(face + total, -1) - total
        flux_cot.append(0.5 * (p + m))
        out.append(2.0 * (p - m))
    pull_flux(cells, velocity, push, inverse, 2, flux_cot, out)
    return out


def column_row_pull(padded, prim, tangent, own, o, front):
    row = (o + 3) * PITCH + (front + 3)
    cells = [get(padded, c * PLANE + row) for c in range(5)]
    velocity = [get(prim, c * PLANE + row) for c in range(3)]
    push = get(prim, 5 * PLANE + row)
    inverse = get(prim, 6 * PLANE + row)
    factors = []
    for c in range(5):
        first = (c * 8 + o) * 64
        factors.append([get(tangent, first + k * 8) for k in range(8)])
    return column_cot(cells, velocity, push, inverse, own, factors)


def column_pull(padded, prim, cot, grad, front, tangent, rows):
    for o in rows:
        row = (o + 3) * PITCH + (front + 3)
        own = [get(cot, c * PLANE + row) for c in range(5)]
        out = column_row_pull(padded, prim, tangent, own, o, front)
        for c in range(5):
            add(grad, c * PLANE + row, out[c])


def late_column_kernel(left, scale, padded, prim, tangent, folded, part):
    for i in range(5):
        o = 3 + i if left else i
        own = [(scale * TIME_STEP) * get(folded, (c * 8 + o) * 8) for c in range(5)]
        out = column_row_pull(padded, prim, tangent, own, o, frame(left)[0])
        for c in range(5):
            put(part, (c * 5 + i) * 8, out[c])


def slopes(prim, row, stride, count, g):
    fields = [get(prim, j * g.plane + row, stride) for j in range(count)]
    table = [[], [], []]
    for j in range(count):
        start = j * g.plane + row
        table[0].append(
            0.5 * (get(prim, start + g.pitch, stride) - get(prim, start - g.pitch, stride))
        )
        table[1].append(0.5 * (get(prim, start + 1, stride) - get(prim, start - 1, stride)))
        table[2].append(0.5 * (ahead(fields[j], 1) - ahead(fields[j], -1)))
    return fields, table


def strain(table, k, j):
    return table[k][j] + table[j][k]


def viscous_fluxes(prim, row, stride, directions):
    fields, table = slopes(prim, row, stride, 4, NARROW)
    drag = get(prim, 4 * PLANE + row, stride)
    spread = (2.0 / 3.0) * (table[0][0] + table[1][1] + table[2][2])
    out = {}
    for k in directions:
        stress = []
        for j in range(3):
            shape = strain(table, k, j)
            stress.append(drag * (shape - spread if j == k else shape))
        power = (
            fields[0] * stress[0]
            + fields[1] * stress[1]
            + fields[2] * stress[2]
            + CONDUCTION * (drag * table[k][3])
        )
        out[k] = stress + [power]
    return out


def viscous_rate(prim, flux_x, flux_y, rate, front):
    def store(ref, row, stride, values):
        for c in range(4):
            put(ref, c * PLANE + row, values[c], stride)

    for edge in (2, 11):
        row = edge * PITCH + (front + 3)
        store(flux_x, row, 1, viscous_fluxes(prim, row, 1, (0,))[0])
        row = 3 * PITCH + (front + edge)
        store(flux_y, row, PITCH, viscous_fluxes(prim, row, PITCH, (1,))[1])

    def body(o):
        row = (o + 3) * PITCH + (front + 3)
        values = viscous_fluxes(prim, row, 1, (0, 1, 2))
        changes = [0.5 * (ahead(value, 1) - ahead(value, -1)) for value in values[2]]
        store(flux_x, row, 1, values[0])
        store(flux_y, row, 1, values[1])
        for c in range(4):
            add(rate, pl.multiple_of(((1 + c) * 8 + o) * 8, 8), changes[c])

    loop(8, body, 8)

    for o in range(8):
        row = (o + 3) * PITCH + (front + 3)
        for c in range(4):
            start = c * PLANE + row
            change = (get(flux_x, start + PITCH) - get(flux_x, start - PITCH)) + (
                get(flux_y, start + 1) - get(flux_y, start - 1)
            )
            add(rate, ((1 + c) * 8 + o) * 8, 0.5 * change)


def total_of(terms):
    out = terms[0]
    for term in terms[1:]:
        out = out + term
    return out


def viscous_pull_at(prim, cot, prim_cot, row, stride, directions, g=NARROW):
    fields, table = slopes(prim, row, stride, 4, g)
    drag = get(prim, 4 * g.plane + row, stride)
    spread = (2.0 / 3.0) * (table[0][0] + table[1][1] + table[2][2])
    field_cot = [[], [], []]
    drag_cot, spread_cot = [], []
    slope_cot = [[[] for _ in range(4)] for _ in range(3)]
    for k in directions:
        flux_cot = []
        for c in range(4):
            start = (1 + c) * g.plane + row
            if k == 2:
                own = get(cot, start, stride)
                flux_cot.append(0.5 * (ahead(own, -1) - ahead(own, 1)))
            else:
                step = g.pitch if k == 0 else 1
                flux_cot.append(
                    0.5 * (get(cot, start - step, stride) - get(cot, start + step, stride))
                )
        power = flux_cot[3]
        heat = CONDUCTION * power
        drag_cot.append(heat * table[k][3])
        slope_cot[k][3].append(heat * drag)
        for j in range(3):
            shape = strain(table, k, j)
            if j == k:
                shape = shape - spread
            stress_cot = flux_cot[j] + fields[j] * power
            field_cot[j].append(power * (drag * shape))
            drag_cot.append(stress_cot * shape)
            scaled = drag * stress_cot
            slope_cot[k][j].append(scaled)
            slope_cot[j][k].append(scaled)
            if j == k:
                spread_cot.append(scaled)
    spread_total = (2.0 / 3.0) * total_of(spread_cot)
    for j in range(3):
        slope_cot[j][j].append(-spread_total)
    put(prim_cot, 4 * g.plane + row, total_of(drag_cot), stride)
    for j in range(4):
        here = list(field_cot[j]) if j < 3 else []
        if slope_cot[2][j]:
            value = total_of(slope_cot[2][j])
            here.append(0.5 * (ahead(value, -1) - ahead(value, 1)))
        if here:
            put(prim_cot, j * g.plane + row, total_of(here), stride)
        for k in range(2):
            if slope_cot[k][j]:
                put(
                    prim_cot,
                    (5 + 4 * k + j) * g.plane + row,
                    0.5 * total_of(slope_cot[k][j]),
                    stride,
                )


def viscous_finish(prim, prim_cot, row, count, g, out):
    velocity = [get(prim, j * g.plane + row, count=count) for j in range(3)]
    thermal = get(prim, 3 * g.plane + row, count=count)
    inverse = get(prim, 6 * g.plane + row, count=count)
    molecular = get(prim, 7 * g.plane + row, count=count)
    field_cot = []
    for j in range(4):
        along = (5 + j) * g.plane + row
        across = (9 + j) * g.plane + row
        field_cot.append(
            get(prim_cot, j * g.plane + row, count=count)
            + (
                get(prim_cot, along - g.pitch, count=count)
                - get(prim_cot, along + g.pitch, count=count)
            )
            + (get(prim_cot, across - 1, count=count) - get(prim_cot, across + 1, count=count))
        )
    drag_cot = get(prim_cot, 4 * g.plane + row, count=count)
    thermal_cot = field_cot[3] + 0.7 * (drag_cot * molecular) / thermal
    push_cot = thermal_cot * inverse
    out[0] = out[0] - push_cot * thermal
    pull_push(out, velocity, push_cot)
    for j in range(3):
        scaled = field_cot[j] * inverse
        out[1 + j] = out[1 + j] + scaled
        out[0] = out[0] - scaled * velocity[j]
    return drag_cot


def viscous_pull(prim, cot, prim_cot, grad, front):
    clear_rows(prim_cot, 13 * PLANE)
    for edge in (2, 11):
        row = edge * PITCH + (front + 3)
        viscous_pull_at(prim, cot, prim_cot, row, 1, (0,))
        row = 3 * PITCH + (front + edge)
        viscous_pull_at(prim, cot, prim_cot, row, PITCH, (1,))

    def body(o):
        row = (o + 3) * PITCH + (front + 3)
        viscous_pull_at(prim, cot, prim_cot, row, 1, (0, 1, 2))

    loop(8, body, 4)

    def finish(i):
        row = i * 16 + 16
        out = [get(grad, c * PLANE + row, count=16) for c in range(6)]
        out[5] = out[5] + viscous_finish(prim, prim_cot, row, 16, NARROW, out)
        for c in range(6):
            put(grad, c * PLANE + row, out[c], count=16)

    loop(12, finish, 4)


def wide_viscous_pull(prim, cot, prim_cot, grad, drag_part):
    def body(x):
        viscous_pull_at(prim, cot, prim_cot, wide_row(x, 0), 1, (0, 1, 2), WIDE)

    for x in (-1, 8):
        body(x)
    for y in (-1, 8):
        viscous_pull_at(prim, cot, prim_cot, wide_row(0, y), 24, (0, 1, 2), WIDE)
    loop(8, body, 4)

    def finish(x):
        row = wide_row(x, 0)
        out = [get(grad, c * WIDE.plane + row) for c in range(5)]
        drag_cot = viscous_finish(prim, prim_cot, row, 8, WIDE, out)
        put(drag_part, pl.multiple_of(x * 8, 8), drag_cot)
        for c in range(5):
            put(grad, c * WIDE.plane + row, out[c])

    loop(8, finish, 4)


def clear_rows(ref, rows):
    clear_rows_from(ref, 0, rows)


def clear_rows_from(ref, first, rows):
    for row in range(first, first + rows, 32):
        put(ref, row, jnp.zeros((32, 128), jnp.float32), count=32)


X_ROWS = 68
X_MORE = 5 * X_ROWS
Y_MORE = 5 * 48


def x_pieces(left):
    pieces, place = [], 0
    for x in range(6):
        distance = 5 - x if left else x
        first, count = (0, 14) if distance < 3 else (2, 10) if distance == 3 else (3, 8)
        pieces.append((place, x, first, count))
        place += count
    return pieces


def assemble(padded, own, from_y, from_x, left):
    front, first, outer = frame(left)
    for c in range(5):
        for x in range(8):
            row = c * PLANE + (first + x) * PITCH + front
            put(padded, row + first, get(own, (c * 8 + x) * 8))
            put(padded, row + outer, get(from_y, (c * 8 + x) * 6, count=6), count=6)
        for place, x, cell, count in x_pieces(left):
            row = c * PLANE + (outer + x) * PITCH + front + cell
            put(padded, row, get(from_x, c * X_ROWS + place, count=count), count=count)


def assemble_eddy_left(padded, eddy, zero_y, zero_x):
    front = frame(True)[0]
    for x in range(8):
        row = 5 * PLANE + (6 + x) * PITCH + front
        put(padded, row + 6, get(eddy, x * 8))
        put(padded, row + 2, get(zero_y, Y_MORE + x * 4, count=4), count=4)
    for x in range(4):
        row = 5 * PLANE + (2 + x) * PITCH + front + 2
        put(padded, row, get(zero_x, X_MORE + x * 12, count=12), count=12)


def assemble_eddy_right(padded, eddy, zero_y, zero_x, one_y, one_x):
    base = 5 * PLANE
    for x in range(8):
        row = base + (3 + x) * PITCH
        put(padded, row + 3, get(eddy, x * 8))
        put(padded, row + 2, get(zero_y, Y_MORE + x * 4 + 3, count=1), count=1)
        put(padded, row + 11, get(one_y, Y_MORE + x, count=1), count=1)
    put(padded, base + 2 * PITCH + 3, get(zero_x, X_MORE + 3 * 12 + 4))
    put(padded, base + 11 * PITCH + 3, get(one_x, X_MORE))


def start_kernel(state, eddy, send_y):
    for i in range(40):
        put(send_y, i * 6, get(state, i * 8 + 2, count=6), count=6)
    for x in range(8):
        put(send_y, Y_MORE + x * 4, get(eddy, x * 8 + 4, count=4), count=4)


def side_kernel(left, own, from_y, more, send_x, line):
    front, first, outer = frame(left)
    begin = 2 if left else 0
    for c in range(5):
        for x in range(6):
            source = c * 8 + begin + x
            row = (c * 6 + x) * PITCH + front
            put(line, row + first, get(own, source * 8))
            put(line, row + outer, get(from_y, source * 6, count=6), count=6)
        for place, x, cell, count in x_pieces(left):
            value = get(line, (c * 6 + x) * PITCH + front + cell, count=count)
            put(send_x, c * X_ROWS + place, value, count=count)
    if left:
        for x in range(4):
            row = X_MORE + x * 12
            put(send_x, row, get(from_y, Y_MORE + (4 + x) * 4, count=4), count=4)
            put(send_x, row + 4, get(more, (4 + x) * 8))
    else:
        put(send_x, X_MORE, get(more, 0))


def section_body(left, keep, weight, base, column, out, padded, prim, split, rate, flux_x, flux_y):
    front = frame(left)[0]
    fill_prim(padded, prim)
    line_rate(padded, prim, split, rate, 0, front, True)
    line_rate(padded, prim, split, rate, 1, front, False)
    column_rate(padded, prim, rate, front, range(3) if left else range(5, 8))
    early = 3 if left else 0
    for c in range(5):
        add(rate, (c * 8 + early) * 8, get(column, c * 40, count=40), count=40)
    viscous_rate(prim, flux_x, flux_y, rate, front)
    for x in range(8):
        row = (x + 3) * PITCH + (front + 3)
        for c in range(5):
            place = (c * 8 + x) * 8
            value = weight * get(padded, c * PLANE + row) + (weight * TIME_STEP) * get(rate, place)
            if keep:
                value = value + keep * get(base, place)
            put(out, place, value)


def first_section_kernel(state, zero_y, zero_x, eddy, column, out, send_y, padded, *scratch):
    assemble(padded, state, zero_y, zero_x, True)
    assemble_eddy_left(padded, eddy, zero_y, zero_x)
    section_body(True, 0.0, 1.0, None, column, out, padded, *scratch)
    for i in range(40):
        put(send_y, i * 6, get(out, i * 8, count=6), count=6)
    for x in range(8):
        put(send_y, Y_MORE + x, get(eddy, x * 8, count=1), count=1)


def second_section_kernel(
    own, one_y, one_x, zero_y, zero_x, eddy, state, adjoint, column, out, *refs
):
    send_up, send_down, padded, *scratch = refs
    assemble(padded, own, one_y, one_x, False)
    assemble_eddy_right(padded, eddy, zero_y, zero_x, one_y, one_x)
    section_body(False, 0.75, 0.25, state, column, out, padded, *scratch)
    for i in range(40):
        put(send_up, i * 5, get(out, i * 8 + 3, count=5), count=5)
        put(send_up, 200 + i * 3, get(adjoint, i * 8 + 5, count=3), count=3)
        put(send_down, i * 5, get(out, i * 8, count=5), count=5)
        put(send_down, 200 + i * 3, get(adjoint, i * 8, count=3), count=3)


def first_tangent_kernel(state, zero_y, zero_x, eddy, padded, prim, tangent, split):
    assemble(padded, state, zero_y, zero_x, True)
    assemble_eddy_left(padded, eddy, zero_y, zero_x)
    fill_prim(padded, prim)
    line_tangent(padded, prim, split, tangent, 0, frame(True)[0])


def second_tangent_kernel(own, one_y, one_x, zero_y, zero_x, eddy, padded, prim, tangent, split):
    assemble(padded, own, one_y, one_x, False)
    assemble_eddy_right(padded, eddy, zero_y, zero_x, one_y, one_x)
    fill_prim(padded, prim)
    line_tangent(padded, prim, split, tangent, 0, frame(False)[0])


def line_tangent_kernel(left, padded, prim, tangent, split):
    line_tangent(padded, prim, split, tangent, 1, frame(left)[0])


def first_line_and_column_kernel(padded, prim, own, from_y, tangent, column, split, line):
    line_tangent_kernel(True, padded, prim, tangent, split)
    early_column_kernel(False, own, from_y, column, line)


def column_tangent_kernel(left, padded, prim, tangent):
    column_tangent(padded, prim, tangent, frame(left)[0])


def own_column_kernel(own, adjoint, part):
    def body(x):
        rows = [pl.multiple_of((c * 8 + x) * 8, 8) for c in range(5)]
        cells = [get(own, row) for row in rows]
        inverse = 1.0 / cells[0]
        velocity = [cells[1 + j] * inverse for j in range(3)]
        kinetic = 0.5 * (
            cells[1] * velocity[0] + cells[2] * velocity[1] + cells[3] * velocity[2]
        )
        push = (HEAT_RATIO - 1.0) * (cells[4] - kinetic)
        cot = [(2.0 / 3.0 * TIME_STEP) * get(adjoint, row) for row in rows]
        out = column_cot(cells, velocity, push, inverse, cot)
        for row, value in zip(rows, out):
            put(part, row, value)

    loop(8, body, 4)


def hand_back(left, grad, send_x, rest):
    front, first, outer = frame(left)
    for c in range(5):
        for place, x, cell, count in x_pieces(left):
            row = c * PLANE + (outer + x) * PITCH + front + cell
            put(send_x, c * X_ROWS + place, get(grad, row, count=count), count=count)
        row = c * PLANE + first * PITCH
        put(rest, c * 128, get(grad, row, count=128), count=128)


def wide_side_kernel(own, low_y, high_y, adjoint, send_up, send_down):
    for send, first, layer, near in ((send_up, 3, 5, 7), (send_down, 0, 0, 0)):
        for c in range(5):
            put(send, c * 40, get(own, (c * 8 + first) * 8, count=40), count=40)
            put(send, 200 + c * 24, get(adjoint, (c * 8 + layer) * 8, count=24), count=24)
            corner = c * 8 + near
            put(send, 320 + c * 4, get(low_y, corner * 5 + 4, count=1), count=1)
            put(send, 321 + c * 4, get(high_y, corner * 5, count=1), count=1)
            put(send, 322 + c * 4, get(low_y, 202 + corner * 3, count=1), count=1)
            put(send, 323 + c * 4, get(high_y, 200 + corner * 3, count=1), count=1)


def wide_assemble(padded, cot, own, low_y, high_y, low_x, high_x, adjoint, edges):
    zero_y, zero_x, one_y, one_x, eddy = edges
    for c in range(5):
        base = c * WIDE.plane
        for x in range(8):
            row, source = base + wide_row(x, 0), c * 8 + x
            put(padded, row, get(own, source * 8))
            put(padded, row - 5, get(low_y, source * 5, count=5), count=5)
            put(padded, row + 8, get(high_y, source * 5, count=5), count=5)
            put(cot, row, get(adjoint, source * 8))
            put(cot, row - 3, get(low_y, 200 + source * 3, count=3), count=3)
            put(cot, row + 8, get(high_y, 200 + source * 3, count=3), count=3)
        for r in range(5):
            put(padded, base + wide_row(r - 5, 0), get(low_x, (c * 5 + r) * 8))
            put(padded, base + wide_row(r + 8, 0), get(high_x, (c * 5 + r) * 8))
        for r in range(3):
            put(cot, base + wide_row(r - 3, 0), get(low_x, 200 + (c * 3 + r) * 8))
            put(cot, base + wide_row(r + 8, 0), get(high_x, 200 + (c * 3 + r) * 8))
        for x, source in ((-1, low_x), (8, high_x)):
            for k, (ref, y) in enumerate(((padded, -1), (padded, 8), (cot, -1), (cot, 8))):
                row = base + wide_row(x, y)
                put(ref, row, get(source, 320 + c * 4 + k, count=1), count=1)
    base = 5 * WIDE.plane
    for x in range(8):
        put(padded, base + wide_row(x, 0), get(eddy, x * 8))
        put(padded, base + wide_row(x, -1), get(zero_y, Y_MORE + x * 4 + 3, count=1), count=1)
        put(padded, base + wide_row(x, 8), get(one_y, Y_MORE + x, count=1), count=1)
    put(padded, base + wide_row(-1, 0), get(zero_x, X_MORE + 3 * 12 + 4))
    put(padded, base + wide_row(8, 0), get(one_x, X_MORE))


def last_section_kernel(
    own, low_y, high_y, low_x, high_x, zero_y, zero_x, one_y, one_x, eddy, adjoint, column_part, *refs
):
    adjoint_two, drag_part, padded, prim, split, split_cot, cot, prim_cot, grad = refs
    scale = 2.0 / 3.0
    edges = zero_y, zero_x, one_y, one_x, eddy
    wide_assemble(padded, cot, own, low_y, high_y, low_x, high_x, adjoint, edges)
    fill_prim(padded, prim, WIDE.plane, 48)
    for c in range(5):
        for x in range(8):
            put(grad, c * WIDE.plane + wide_row(x, 0), jnp.zeros((8, 128), jnp.float32))
    wide_viscous_pull(prim, cot, prim_cot, grad, drag_part)
    kept = range(5, 13)
    line_pull(padded, prim, split, split_cot, cot, grad, 1, WIDE, kept)
    line_pull(padded, prim, split, split_cot, cot, grad, 0, WIDE, kept)
    for c in range(5):
        for x in range(8):
            row, place = c * WIDE.plane + wide_row(x, 0), (c * 8 + x) * 8
            value = scale * get(adjoint, place) + (scale * TIME_STEP) * get(grad, row)
            put(adjoint_two, place, value + get(column_part, place))
    for x in range(8):
        put(drag_part, x * 8, (scale * TIME_STEP) * get(drag_part, x * 8))


def earlier_section(left, scale, cells, tangents, rest_in, folded_y, scratch):
    padded, prim = cells
    along_x, along_y, along_z = tangents
    split_cot, cot, prim_cot, grad, folded = scratch
    front = frame(left)[0]
    clear_rows(cot, 5 * PLANE)
    clear_rows(grad, 5 * PLANE)
    begin = 0 if left else 2
    for i in range(40):
        put(folded, i * 8, get(rest_in, i * 8))
        if folded_y is not None:
            add(folded, i * 8 + begin, get(folded_y, i * 6, count=6), count=6)
    for c in range(5):
        for x in range(8):
            row = c * PLANE + (3 + x) * PITCH + (front + 3)
            value = scale * get(folded, (c * 8 + x) * 8)
            put(cot, row, TIME_STEP * value)
            put(grad, row, value)
    viscous_pull(prim, cot, prim_cot, grad, front)
    g = narrow(front)
    line_pull(padded, prim, None, split_cot, cot, grad, 1, g, range(14), along_y)
    line_pull(padded, prim, None, split_cot, cot, grad, 0, g, range(14), along_x)
    column_pull(padded, prim, cot, grad, front, along_z, range(3) if left else range(5, 8))


def second_pull_kernel(
    padded, prim, along_x, along_y, along_z, adjoint_two, send_x, rest, drag_part, *scratch
):
    grad = scratch[3]
    clear_rows_from(grad, 5 * PLANE, PLANE)
    earlier_section(
        False, 0.25, (padded, prim), (along_x, along_y, along_z), adjoint_two, None, scratch
    )
    hand_back(False, grad, send_x, rest)
    put(send_x, X_MORE, get(grad, 5 * PLANE + 11 * PITCH + 3))
    put(drag_part, 0, get(grad, 5 * PLANE, count=PLANE), count=PLANE)


def first_pull_kernel(
    padded, prim, along_x, along_y, along_z, rest_in, folded_y, folded_x, drag_two, drag_one, *refs
):
    send_x, rest, folded = refs[:3]
    scratch = [*refs[3:], folded]
    grad = scratch[3]
    front = frame(True)[0]
    clear_rows_from(grad, 5 * PLANE, PLANE)
    for x in range(8):
        put(grad, 5 * PLANE + (6 + x) * PITCH + front + 6, get(drag_two, x * 8))
    for x in range(9):
        row = 5 * PLANE + (5 + x) * PITCH + front + 5
        add(grad, row, get(drag_one, (2 + x) * PITCH + 2, count=9), count=9)
    add(grad, 5 * PLANE + 6 * PITCH + front + 6, get(folded_x, X_MORE))
    for x in range(8):
        row = 5 * PLANE + (6 + x) * PITCH + front + 6
        add(grad, row, get(folded_y, Y_MORE + x, count=1), count=1)
    earlier_section(
        True, 1.0, (padded, prim), (along_x, along_y, along_z), rest_in, folded_y, scratch
    )
    hand_back(True, grad, send_x, rest)
    for x in range(4):
        row = 5 * PLANE + (2 + x) * PITCH + front + 2
        put(send_x, X_MORE + x * 12, get(grad, row, count=12), count=12)
    put(rest, 640, get(grad, 5 * PLANE + 6 * PITCH, count=128), count=128)


def fold_rows(left, rest_in, from_x, part, rest, send_y, work):
    front, first, outer = frame(left)
    begin = 2 if left else 0
    put(work, 0, get(rest_in, 0, count=640), count=640)
    for c in range(5):
        for i in range(5):
            x = i if left else 3 + i
            add(work, (c * 8 + x) * PITCH + front + 3, get(part, (c * 5 + i) * 8))
        for place, x, cell, count in x_pieces(left):
            row = (c * 8 + begin + x) * PITCH + front + cell
            add(work, row, get(from_x, c * X_ROWS + place, count=count), count=count)
    for i in range(40):
        put(rest, i * 8, get(work, i * PITCH + front + first))
        put(send_y, i * 6, get(work, i * PITCH + front + outer, count=6), count=6)


def second_fold_kernel(rest_in, from_x, part, drag_part, rest, send_y, work):
    fold_rows(False, rest_in, from_x, part, rest, send_y, work)
    for x in range(8):
        put(send_y, Y_MORE + x, get(drag_part, (3 + x) * PITCH + 11, count=1), count=1)


def first_fold_kernel(rest_in, from_x, part, rest, send_y, work):
    fold_rows(True, rest_in, from_x, part, rest, send_y, work)
    put(work, 640, get(rest_in, 640, count=128), count=128)
    front = frame(True)[0]
    for x in range(4):
        row = 640 + (4 + x) * PITCH + front + 2
        add(work, row, get(from_x, X_MORE + x * 12, count=12), count=12)
    for x in range(8):
        put(rest, 320 + x * 8, get(work, 640 + x * PITCH + front + 6))
        row = 640 + x * PITCH + front + 2
        put(send_y, Y_MORE + x * 4, get(work, row, count=4), count=4)


def end_kernel(adjoint, adjoint_two, rest_zero, folded_zero, grad_state, grad_eddy):
    for i in range(40):
        value = (1.0 / 3.0) * get(adjoint, i * 8) + 0.75 * get(adjoint_two, i * 8)
        put(grad_state, i * 8, value + get(rest_zero, i * 8))
        add(grad_state, i * 8 + 2, get(folded_zero, i * 6, count=6), count=6)
    for i in range(8):
        put(grad_eddy, i * 8, get(rest_zero, 320 + i * 8))
        add(grad_eddy, i * 8 + 4, get(folded_zero, Y_MORE + i * 4, count=4), count=4)


def run(kernel, operands, outs, scratch=(), work=0):
    cost = pl.CostEstimate(flops=work, bytes_accessed=4 * work, transcendentals=0) if work else None
    return pl.pallas_call(
        kernel,
        out_shape=[jax.ShapeDtypeStruct((rows, 128), jnp.float32) for rows in outs],
        in_specs=[pl.BlockSpec(memory_space=pltpu.VMEM)] * len(operands),
        out_specs=[pl.BlockSpec(memory_space=pltpu.VMEM)] * len(outs),
        scratch_shapes=[pltpu.VMEM((rows, 128), jnp.float32) for rows in scratch],
        compiler_params=pltpu.CompilerParams(vmem_limit_bytes=20 * 1024 * 1024),
        cost_estimate=cost,
    )(*operands)


def shifted(values, axis, up):
    count = lax.axis_size(axis)
    step = 1 if up else count - 1
    return lax.ppermute(values, axis, [(i, (i + step) % count) for i in range(count)])


def together(*values):
    return lax.optimization_barrier(values)


def shifted_beside(values, axis, up, kernel, operands, outs, scratch=()):
    values, *operands = together(values, *operands)
    moved = shifted(values, axis, up)
    moved, *results = together(moved, *run(kernel, operands, outs, scratch, 2_000_000))
    return moved, results


def shifted_both_beside(up, down, axis, jobs):
    operands = [operand for job in jobs for operand in job[1]]
    up, down, *operands = together(up, down, *operands)
    low, high = shifted(up, axis, True), shifted(down, axis, False)
    results, place, counts = [], 0, []
    for kernel, given, outs, scratch in jobs:
        made = run(kernel, operands[place : place + len(given)], outs, scratch, 2_000_000)
        place += len(given)
        counts.append(len(made))
        results += made
    low, high, *results = together(low, high, *results)
    grouped = []
    for count in counts:
        grouped.append(results[:count])
        results = results[count:]
    return low, high, grouped


def pipeline(state, eddy, adjoint):
    section_scratch = (6 * PLANE, 8 * PLANE, 1120, 320, 4 * PLANE, 4 * PLANE)
    wide = WIDE.plane
    last_scratch = (6 * wide, 8 * wide, 1440, 1440, 5 * wide, 13 * wide, 5 * wide)
    earlier_scratch = (1120, 5 * PLANE, 13 * PLANE, 6 * PLANE, 320)
    first_tangent = [6 * PLANE, 8 * PLANE, 2880]

    def sides(own, from_y, more, left, rows):
        (send_x,) = run(
            functools.partial(side_kernel, left),
            [own, from_y, more],
            [X_MORE + rows],
            [5 * 6 * PITCH],
        )
        return send_x

    (send_y,) = run(start_kernel, [state, eddy], [Y_MORE + 32])
    zero_y = shifted(send_y, "gy", True)
    zero_x, (column,) = shifted_beside(
        sides(state, zero_y, eddy, True, 48),
        "gx",
        True,
        functools.partial(early_column_kernel, True),
        [state, zero_y],
        [200],
        [80],
    )
    zero = [state, zero_y, zero_x, eddy]
    one, send_y = run(first_section_kernel, [*zero, column], [320, Y_MORE + 8], section_scratch)

    one_y, (zero_cells, zero_prim, zero_along_x) = shifted_beside(
        send_y, "gy", False, first_tangent_kernel, zero, first_tangent, [1120]
    )
    one_x, (zero_along_y, column) = shifted_beside(
        sides(one, one_y, eddy, False, 8),
        "gx",
        False,
        first_line_and_column_kernel,
        [zero_cells, zero_prim, one, one_y],
        [2880, 200],
        [1120, 80],
    )
    one_all = [one, one_y, one_x, zero_y, zero_x, eddy]
    two, send_up, send_down = run(
        second_section_kernel, [*one_all, state, adjoint, column], [320, 320, 320], section_scratch
    )

    low_y, high_y, ((column_part,), (one_cells, one_prim, one_along_x)) = shifted_both_beside(
        send_up,
        send_down,
        "gy",
        [
            (own_column_kernel, [two, adjoint], [320], []),
            (second_tangent_kernel, one_all, first_tangent, [1120]),
        ],
    )
    send_up, send_down = run(wide_side_kernel, [two, low_y, high_y, adjoint], [340, 340])
    low_x, high_x, ((one_along_y,), (one_along_z,)) = shifted_both_beside(
        send_up,
        send_down,
        "gx",
        [
            (
                functools.partial(line_tangent_kernel, False),
                [one_cells, one_prim],
                [2880],
                [1120],
            ),
            (functools.partial(column_tangent_kernel, False), [one_cells, one_prim], [2560], []),
        ],
    )
    adjoint_two, drag_two = run(
        last_section_kernel,
        [
            *(two, low_y, high_y, low_x, high_x, zero_y, zero_x, one_y, one_x),
            *(eddy, adjoint, column_part),
        ],
        [320, 64],
        last_scratch,
    )

    one_tangents = [one_along_x, one_along_y, one_along_z]
    send_x, rest, drag_one = run(
        second_pull_kernel,
        [one_cells, one_prim, *one_tangents, adjoint_two],
        [X_MORE + 8, 640, PLANE],
        earlier_scratch,
    )
    from_x, (part,) = shifted_beside(
        send_x,
        "gx",
        True,
        functools.partial(late_column_kernel, False, 0.25),
        [one_cells, one_prim, one_along_z, adjoint_two],
        [200],
    )
    rest_one, send_y = run(
        second_fold_kernel, [rest, from_x, part, drag_one], [320, Y_MORE + 8], [640]
    )
    folded_one, (zero_along_z,) = shifted_beside(
        send_y,
        "gy",
        True,
        functools.partial(column_tangent_kernel, True),
        [zero_cells, zero_prim],
        [2560],
    )

    zero_tangents = [zero_along_x, zero_along_y, zero_along_z]
    send_x, rest, folded = run(
        first_pull_kernel,
        [zero_cells, zero_prim, *zero_tangents, rest_one, folded_one, from_x, drag_two, drag_one],
        [X_MORE + 48, 768, 320],
        earlier_scratch[:-1],
    )
    from_x, (part,) = shifted_beside(
        send_x,
        "gx",
        False,
        functools.partial(late_column_kernel, True, 1.0),
        [zero_cells, zero_prim, zero_along_z, folded],
        [200],
    )
    rest_zero, send_y = run(first_fold_kernel, [rest, from_x, part], [384, Y_MORE + 32], [768])
    folded_zero = shifted(send_y, "gy", False)
    return run(end_kernel, [adjoint, adjoint_two, rest_zero, folded_zero], [320, 64])


def on_device(state, eddy, adjoint):
    grad_state, grad_eddy = pipeline(
        state.reshape(320, 128), eddy.reshape(64, 128), adjoint.reshape(320, 128)
    )
    return grad_state.reshape(5, 8, 8, 128), grad_eddy.reshape(8, 8, 128)


def solution(mesh):
    placed = (P(None, "gx", "gy", None), P("gx", "gy", None), P(None, "gx", "gy", None))
    return jax.shard_map(
        on_device,
        mesh=mesh,
        in_specs=placed,
        out_specs=(P(None, "gx", "gy", None), P("gx", "gy", None)),
        check_vma=False,
    )
```

```python
import collections
import functools

import jax
import jax.numpy as jnp
from jax import lax
from jax.experimental import pallas as pl
from jax.experimental.pallas import tpu as pltpu
from jax.sharding import PartitionSpec as P

HEAT_RATIO = 1.4
MOLECULAR_DRAG = 0.05
PRANDTL = 0.72
TIME_STEP = 0.04
SMOOTH_EPS = 1e-06
CONDUCTION = HEAT_RATIO / ((HEAT_RATIO - 1.0) * PRANDTL)
SMALL = 0.75 * SMOOTH_EPS

PITCH = 16
PLANE = 14 * PITCH


def frame(left):
    return (2, 6, 0) if left else (0, 0, 8)


Grid = collections.namedtuple("Grid", ["pitch", "plane", "leads", "x_start", "y_start"])


def narrow(front):
    return Grid(PITCH, PLANE, 14, front + 3, 3 * PITCH + front)


WIDE = Grid(24, 18 * 24, 18, 8, 5 * 24 + 3)


NARROW = narrow(0)


def wide_row(x, y):
    return (x + 5) * 24 + 8 + y


def get(ref, start, stride=1, count=8):
    if stride == 1:
        return ref[pl.ds(start, count), :]
    return ref[pl.ds(start, count, stride=stride), :]


def put(ref, start, value, stride=1, count=8):
    if stride == 1:
        ref[pl.ds(start, count), :] = value
    else:
        ref[pl.ds(start, count, stride=stride), :] = value


def add(ref, start, value, stride=1, count=8):
    put(ref, start, get(ref, start, stride, count) + value, stride, count)


def ahead(value, offset):
    return pltpu.roll(value, (-offset) % 128, 1)


def quick_inverse(value):
    return pl.reciprocal(value, approx=True)


def loop(count, body, together=1):
    def step(i, carry):
        for k in range(together):
            body(i * together + k)
        return carry

    lax.fori_loop(0, count // together, step, 0)


class Slope:
    def __init__(self, value):
        self.value = value
        self.kept = {}

    def times(self, factor):
        if factor == 1.0:
            return self.value
        if factor not in self.kept:
            self.kept[factor] = factor * self.value
        return self.kept[factor]

    def square(self):
        if 0 not in self.kept:
            self.kept[0] = self.value * self.value + SMALL
        return self.kept[0]


def weno_parts(d1, d2, d3, d4):
    i1 = quick_inverse(d1.square() + d2.value * (d2.times(2.5) - d1.times(2.75)))
    i2 = quick_inverse(d2.square() + d3.value * (d3.value - d2.times(1.25)))
    i3 = quick_inverse(d4.square() + d3.value * (d3.times(2.5) - d4.times(2.75)))
    w1, w2, w3 = i1 * i1, 6.0 * (i2 * i2), 3.0 * (i3 * i3)
    m1 = d2.times(2.5) - d1.value
    m2 = d2.times(0.5) + d3.value
    m3 = d3.times(2.0) - d4.times(0.5)
    inverse = quick_inverse(w1 + w2 + w3)
    mean = (w1 * m1 + w2 * m2 + w3 * m3) * inverse
    return (i1, i2, i3), (w1, w2, w3), (m1, m2, m3), inverse, mean


def weno_rise(d1, d2, d3, d4):
    return weno_parts(d1, d2, d3, d4)[4]


def weno_pull(d1, d2, d3, d4, third=None):
    (i1, i2, i3), (w1, w2, w3), (m1, m2, m3), inverse, mean = weno_parts(d1, d2, d3, d4)
    scaled = inverse if third is None else third * inverse
    e1, e2, e3 = w1 * scaled, w2 * scaled, w3 * scaled
    g1 = (e1 * i1) * (mean - m1)
    g2 = (e2 * i2) * (mean - m2)
    g3 = (e3 * i3) * (mean - m3)
    c1 = g1 * (d1.times(4.0) - d2.times(5.5)) - e1
    c2 = g1 * (d2.times(10.0) - d1.times(5.5)) + g2 * (d2.times(4.0) - d3.times(2.5))
    c2 = c2 + (2.5 * e1 + 0.5 * e2)
    c3 = g2 * (d3.times(4.0) - d2.times(2.5)) + g3 * (d3.times(10.0) - d4.times(5.5))
    c3 = c3 + (e2 + 2.0 * e3)
    c4 = g3 * (d4.times(4.0) - d3.times(5.5)) - 0.5 * e3
    return c1, c2, c3, c4


def split_flux(cells, speed, push, direction):
    fluxes = [cells[1 + direction]]
    for j in range(3):
        momentum_flux = cells[1 + j] * speed
        fluxes.append(momentum_flux + push if j == direction else momentum_flux)
    fluxes.append((cells[4] + push) * speed)
    plus, minus = [], []
    for flux, cell in zip(fluxes, cells):
        half, double = 0.5 * flux, 2.0 * cell
        plus.append(half + double)
        minus.append(half - double)
    return plus, minus


def pull_flux(cells, velocity, push, inverse_rho, direction, cot, out):
    speed = velocity[direction]
    speed_cot = cot[4] * (cells[4] + push)
    for j in range(3):
        speed_cot = speed_cot + cot[1 + j] * cells[1 + j]
        out[1 + j] = out[1 + j] + cot[1 + j] * speed
    through = cot[4] * speed
    out[4] = out[4] + through
    pull_push(out, velocity, cot[1 + direction] + through)
    speed_cot = speed_cot * inverse_rho
    out[1 + direction] = out[1 + direction] + cot[0] + speed_cot
    out[0] = out[0] - speed_cot * speed


def pull_push(out, velocity, push_cot):
    scaled = 0.4 * push_cot
    out[4] = out[4] + scaled
    square = velocity[0] * velocity[0] + velocity[1] * velocity[1] + velocity[2] * velocity[2]
    out[0] = out[0] + 0.5 * (scaled * square)
    for j in range(3):
        out[1 + j] = out[1 + j] - scaled * velocity[j]


def fill_prim(padded, prim, plane=PLANE, count=32, first=0, blocks=7):
    def body(i):
        row = first + i * count
        cells = [get(padded, c * plane + row, count=count) for c in range(6)]
        inverse = 1.0 / cells[0]
        velocity = [cells[1 + j] * inverse for j in range(3)]
        kinetic = 0.5 * (
            cells[1] * velocity[0] + cells[2] * velocity[1] + cells[3] * velocity[2]
        )
        push = (HEAT_RATIO - 1.0) * (cells[4] - kinetic)
        thermal = push * inverse
        molecular = MOLECULAR_DRAG * jnp.exp(0.7 * jnp.log(thermal))
        values = velocity + [thermal, molecular + cells[5], push, inverse, molecular]
        for k, value in enumerate(values):
            put(prim, k * plane + row, value, count=count)

    loop(blocks, body)


def line_layout(direction, g):
    if direction == 0:
        return lambda lead: lead * g.pitch + g.x_start, 1
    return lambda lead: lead + g.y_start, g.pitch


def fill_split(padded, prim, split, direction, g):
    place, stride = line_layout(direction, g)
    for lead in range(g.leads):
        row = place(lead)
        cells = [get(padded, c * g.plane + row, stride) for c in range(5)]
        speed = get(prim, direction * g.plane + row, stride)
        push = get(prim, 5 * g.plane + row, stride)
        plus, minus = split_flux(cells, speed, push, direction)
        for c in range(5):
            put(split, (c * g.leads + lead) * 8, plus[c])
            put(split, ((5 + c) * g.leads + lead) * 8, minus[c])


def line_slopes(split, c, leads):
    plus = [get(split, pl.multiple_of((c * leads + k) * 8, 8)) for k in range(leads)]
    minus = [get(split, pl.multiple_of(((5 + c) * leads + k) * 8, 8)) for k in range(leads)]
    plus_slopes = [Slope(plus[k + 1] - plus[k]) for k in range(leads - 1)]
    minus_slopes = [Slope(minus[k + 1] - minus[k]) for k in range(leads - 1)]
    return plus, minus, plus_slopes, minus_slopes


def line_rate(padded, prim, split, rate, direction, front, first):
    fill_split(padded, prim, split, direction, narrow(front))

    def body(c):
        plus, minus, ps, ms = line_slopes(split, c, 14)
        low = None
        for f in range(9):
            rise = weno_rise(*ps[f : f + 4]) - weno_rise(ms[f + 4], ms[f + 3], ms[f + 2], ms[f + 1])
            face = (plus[f + 2] + minus[f + 3]) + (1.0 / 3.0) * rise
            if f:
                row, stride = (c * 64 + (f - 1) * 8, 1) if direction == 0 else (c * 64 + f - 1, 8)
                value = low - face
                if not first:
                    value = value + get(rate, row, stride)
                put(rate, row, value, stride)
            low = face

    loop(5, body, 5)


def line_tangent(padded, prim, split, tangent, direction, front):
    fill_split(padded, prim, split, direction, narrow(front))

    def body(c):
        _, _, ps, ms = line_slopes(split, c, 14)
        for f in range(9):
            plus = weno_pull(*ps[f : f + 4])
            minus = weno_pull(ms[f + 4], ms[f + 3], ms[f + 2], ms[f + 1])
            for k, value in enumerate(plus + minus):
                put(tangent, pl.multiple_of((c * 9 + f) * 64, 8) + k * 8, value)

    loop(5, body)


def line_pull(padded, prim, split, split_cot, cot, grad, direction, g, kept, tangent=None):
    place, stride = line_layout(direction, g)
    leads, faces = g.leads, g.leads - 5
    if tangent is None:
        fill_split(padded, prim, split, direction, g)

    def body(c):
        if tangent is None:
            _, _, ps, ms = line_slopes(split, c, leads)
        own = [get(cot, c * g.plane + place(lead), stride) for lead in range(2, leads - 2)]
        plus_cot, minus_cot = [None] * leads, [None] * leads

        def gather(table, lead, value):
            if lead in kept:
                table[lead] = value if table[lead] is None else table[lead] + value

        for f in range(faces):
            face = own[f + 1] - own[f]
            third = (1.0 / 3.0) * face
            if tangent is None:
                plus = weno_pull(*ps[f : f + 4], third)
                minus = weno_pull(ms[f + 4], ms[f + 3], ms[f + 2], ms[f + 1], -third)
            else:
                first = pl.multiple_of((c * 9 + f) * 64, 8)
                plus = [third * get(tangent, first + k * 8) for k in range(4)]
                minus = [-third * get(tangent, first + k * 8) for k in range(4, 8)]
            c1, c2, c3, c4 = plus
            for k, value in enumerate((-c1, c1 - c2, (face + c2) - c3, c3 - c4, c4)):
                gather(plus_cot, f + k, value)
            c1, c2, c3, c4 = minus
            for k, value in enumerate((-c4, c4 - c3, (face + c3) - c2, c2 - c1, c1)):
                gather(minus_cot, f + 1 + k, value)
            for lead in range(f, f + 1 if f < faces - 1 else leads):
                if lead not in kept:
                    continue
                p, m = plus_cot[lead], minus_cot[lead]
                if p is None:
                    total, gap = m, -m
                elif m is None:
                    total, gap = p, p
                else:
                    total, gap = p + m, p - m
                put(split_cot, pl.multiple_of((c * leads + lead) * 8, 8), 0.5 * total)
                put(split_cot, pl.multiple_of(((5 + c) * leads + lead) * 8, 8), 2.0 * gap)

    loop(5, body)
    for lead in kept:
        row = place(lead)
        cells = [get(padded, c * g.plane + row, stride) for c in range(5)]
        velocity = [get(prim, c * g.plane + row, stride) for c in range(3)]
        push = get(prim, 5 * g.plane + row, stride)
        inverse = get(prim, 6 * g.plane + row, stride)
        flux_cot = [get(split_cot, (c * leads + lead) * 8) for c in range(5)]
        out = [get(split_cot, ((5 + c) * leads + lead) * 8) for c in range(5)]
        pull_flux(cells, velocity, push, inverse, direction, flux_cot, out)
        for c in range(5):
            add(grad, c * g.plane + row, out[c], stride)


def column_change(cells, speed, push):
    plus, minus = split_flux(cells, speed, push, 2)
    changes = []
    for c in range(5):
        next_minus = ahead(minus[c], 1)
        dp, dm = ahead(plus[c], 1) - plus[c], next_minus - minus[c]
        rise = weno_rise(*[Slope(v) for v in (ahead(dp, -2), ahead(dp, -1), dp, ahead(dp, 1))])
        rise = rise - weno_rise(
            *[Slope(v) for v in (ahead(dm, 2), ahead(dm, 1), dm, ahead(dm, -1))]
        )
        face = (plus[c] + next_minus) + (1.0 / 3.0) * rise
        changes.append(ahead(face, -1) - face)
    return changes


def column_rate(padded, prim, rate, front, rows):
    for o in rows:
        row = (o + 3) * PITCH + (front + 3)
        cells = [get(padded, c * PLANE + row) for c in range(5)]
        changes = column_change(cells, get(prim, 2 * PLANE + row), get(prim, 5 * PLANE + row))
        for c in range(5):
            add(rate, (c * 8 + o) * 8, changes[c])


def early_column_kernel(left, own, from_y, column, line):
    for i in range(5):
        x = i if left else 3 + i
        for c in range(5):
            source, row = c * 8 + x, c * 16
            if left:
                put(line, row, get(from_y, source * 6 + 3, count=3), count=3)
                put(line, row + 3, get(own, source * 8, count=5), count=5)
            else:
                put(line, row, get(own, source * 8 + 3, count=5), count=5)
                put(line, row + 5, get(from_y, source * 6, count=3), count=3)
        cells = [get(line, c * 16) for c in range(5)]
        inverse = 1.0 / cells[0]
        velocity = [cells[1 + j] * inverse for j in range(3)]
        kinetic = 0.5 * (
            cells[1] * velocity[0] + cells[2] * velocity[1] + cells[3] * velocity[2]
        )
        push = (HEAT_RATIO - 1.0) * (cells[4] - kinetic)
        changes = column_change(cells, velocity[2], push)
        for c in range(5):
            put(column, (c * 5 + i) * 8, changes[c])


def column_slopes(plus, minus):
    dp = ahead(plus, 1) - plus
    dm = ahead(minus, 1) - minus
    return (
        [Slope(value) for value in (ahead(dp, -2), ahead(dp, -1), dp, ahead(dp, 1))],
        [Slope(value) for value in (ahead(dm, 2), ahead(dm, 1), dm, ahead(dm, -1))],
    )


def column_tangent(padded, prim, tangent, front):
    def body(o):
        row = (o + 3) * PITCH + (front + 3)
        cells = [get(padded, c * PLANE + row) for c in range(5)]
        plus, minus = split_flux(cells, get(prim, 2 * PLANE + row), get(prim, 5 * PLANE + row), 2)
        for c in range(5):
            ps, ms = column_slopes(plus[c], minus[c])
            for k, value in enumerate(weno_pull(*ps) + weno_pull(*ms)):
                put(tangent, pl.multiple_of((c * 8 + o) * 64, 8) + k * 8, value)

    loop(8, body, 4)


def column_cot(cells, velocity, push, inverse, cot, factors=None):
    if factors is None:
        plus, minus = split_flux(cells, velocity[2], push, 2)
    flux_cot, out = [], []
    for c in range(5):
        face = ahead(cot[c], 1) - cot[c]
        third = (1.0 / 3.0) * face
        if factors is None:
            ps, ms = column_slopes(plus[c], minus[c])
            plus_parts, minus_parts = weno_pull(*ps, third), weno_pull(*ms, -third)
        else:
            plus_parts = [third * value for value in factors[c][:4]]
            minus_parts = [-third * value for value in factors[c][4:]]
        c1, c2, c3, c4 = plus_parts
        total = (c3 + ahead(c1, 2)) + (ahead(c2, 1) + ahead(c4, -1))
        p = face + (ahead(total, -1) - total)
        c1, c2, c3, c4 = minus_parts
        total = (c3 + ahead(c1, -2)) + (ahead(c2, -1) + ahead(c4, 1))
        m = ahead(face + total, -1) - total
        flux_cot.append(0.5 * (p + m))
        out.append(2.0 * (p - m))
    pull_flux(cells, velocity, push, inverse, 2, flux_cot, out)
    return out


def column_row_pull(padded, prim, tangent, own, o, front):
    row = (o + 3) * PITCH + (front + 3)
    cells = [get(padded, c * PLANE + row) for c in range(5)]
    velocity = [get(prim, c * PLANE + row) for c in range(3)]
    push = get(prim, 5 * PLANE + row)
    inverse = get(prim, 6 * PLANE + row)
    factors = []
    for c in range(5):
        first = (c * 8 + o) * 64
        factors.append([get(tangent, first + k * 8) for k in range(8)])
    return column_cot(cells, velocity, push, inverse, own, factors)


def column_pull(padded, prim, cot, grad, front, tangent, rows):
    for o in rows:
        row = (o + 3) * PITCH + (front + 3)
        own = [get(cot, c * PLANE + row) for c in range(5)]
        out = column_row_pull(padded, prim, tangent, own, o, front)
        for c in range(5):
            add(grad, c * PLANE + row, out[c])


def late_column_kernel(left, scale, padded, prim, tangent, folded, part):
    for i in range(5):
        o = 3 + i if left else i
        own = [(scale * TIME_STEP) * get(folded, (c * 8 + o) * 8) for c in range(5)]
        out = column_row_pull(padded, prim, tangent, own, o, frame(left)[0])
        for c in range(5):
            put(part, (c * 5 + i) * 8, out[c])


def slopes(prim, row, stride, count, g):
    fields = [get(prim, j * g.plane + row, stride) for j in range(count)]
    table = [[], [], []]
    for j in range(count):
        start = j * g.plane + row
        table[0].append(
            0.5 * (get(prim, start + g.pitch, stride) - get(prim, start - g.pitch, stride))
        )
        table[1].append(0.5 * (get(prim, start + 1, stride) - get(prim, start - 1, stride)))
        table[2].append(0.5 * (ahead(fields[j], 1) - ahead(fields[j], -1)))
    return fields, table


def strain(table, k, j):
    return table[k][j] + table[j][k]


def viscous_fluxes(prim, row, stride, directions):
    fields, table = slopes(prim, row, stride, 4, NARROW)
    drag = get(prim, 4 * PLANE + row, stride)
    spread = (2.0 / 3.0) * (table[0][0] + table[1][1] + table[2][2])
    out = {}
    for k in directions:
        stress = []
        for j in range(3):
            shape = strain(table, k, j)
            stress.append(drag * (shape - spread if j == k else shape))
        power = (
            fields[0] * stress[0]
            + fields[1] * stress[1]
            + fields[2] * stress[2]
            + CONDUCTION * (drag * table[k][3])
        )
        out[k] = stress + [power]
    return out


def viscous_rate(prim, flux_x, flux_y, rate, front):
    def store(ref, row, stride, values):
        for c in range(4):
            put(ref, c * PLANE + row, values[c], stride)

    for edge in (2, 11):
        row = edge * PITCH + (front + 3)
        store(flux_x, row, 1, viscous_fluxes(prim, row, 1, (0,))[0])
        row = 3 * PITCH + (front + edge)
        store(flux_y, row, PITCH, viscous_fluxes(prim, row, PITCH, (1,))[1])

    def body(o):
        row = (o + 3) * PITCH + (front + 3)
        values = viscous_fluxes(prim, row, 1, (0, 1, 2))
        changes = [0.5 * (ahead(value, 1) - ahead(value, -1)) for value in values[2]]
        store(flux_x, row, 1, values[0])
        store(flux_y, row, 1, values[1])
        for c in range(4):
            add(rate, pl.multiple_of(((1 + c) * 8 + o) * 8, 8), changes[c])

    loop(8, body, 8)

    for o in range(8):
        row = (o + 3) * PITCH + (front + 3)
        for c in range(4):
            start = c * PLANE + row
            change = (get(flux_x, start + PITCH) - get(flux_x, start - PITCH)) + (
                get(flux_y, start + 1) - get(flux_y, start - 1)
            )
            add(rate, ((1 + c) * 8 + o) * 8, 0.5 * change)


def total_of(terms):
    out = terms[0]
    for term in terms[1:]:
        out = out + term
    return out


def viscous_pull_at(prim, cot, prim_cot, row, stride, directions, g=NARROW):
    fields, table = slopes(prim, row, stride, 4, g)
    drag = get(prim, 4 * g.plane + row, stride)
    spread = (2.0 / 3.0) * (table[0][0] + table[1][1] + table[2][2])
    field_cot = [[], [], []]
    drag_cot, spread_cot = [], []
    slope_cot = [[[] for _ in range(4)] for _ in range(3)]
    for k in directions:
        flux_cot = []
        for c in range(4):
            start = (1 + c) * g.plane + row
            if k == 2:
                own = get(cot, start, stride)
                flux_cot.append(0.5 * (ahead(own, -1) - ahead(own, 1)))
            else:
                step = g.pitch if k == 0 else 1
                flux_cot.append(
                    0.5 * (get(cot, start - step, stride) - get(cot, start + step, stride))
                )
        power = flux_cot[3]
        heat = CONDUCTION * power
        drag_cot.append(heat * table[k][3])
        slope_cot[k][3].append(heat * drag)
        for j in range(3):
            shape = strain(table, k, j)
            if j == k:
                shape = shape - spread
            stress_cot = flux_cot[j] + fields[j] * power
            field_cot[j].append(power * (drag * shape))
            drag_cot.append(stress_cot * shape)
            scaled = drag * stress_cot
            slope_cot[k][j].append(scaled)
            slope_cot[j][k].append(scaled)
            if j == k:
                spread_cot.append(scaled)
    spread_total = (2.0 / 3.0) * total_of(spread_cot)
    for j in range(3):
        slope_cot[j][j].append(-spread_total)
    put(prim_cot, 4 * g.plane + row, total_of(drag_cot), stride)
    for j in range(4):
        here = list(field_cot[j]) if j < 3 else []
        if slope_cot[2][j]:
            value = total_of(slope_cot[2][j])
            here.append(0.5 * (ahead(value, -1) - ahead(value, 1)))
        if here:
            put(prim_cot, j * g.plane + row, total_of(here), stride)
        for k in range(2):
            if slope_cot[k][j]:
                put(
                    prim_cot,
                    (5 + 4 * k + j) * g.plane + row,
                    0.5 * total_of(slope_cot[k][j]),
                    stride,
                )


def viscous_finish(prim, prim_cot, row, count, g, out):
    velocity = [get(prim, j * g.plane + row, count=count) for j in range(3)]
    thermal = get(prim, 3 * g.plane + row, count=count)
    inverse = get(prim, 6 * g.plane + row, count=count)
    molecular = get(prim, 7 * g.plane + row, count=count)
    field_cot = []
    for j in range(4):
        along = (5 + j) * g.plane + row
        across = (9 + j) * g.plane + row
        field_cot.append(
            get(prim_cot, j * g.plane + row, count=count)
            + (
                get(prim_cot, along - g.pitch, count=count)
                - get(prim_cot, along + g.pitch, count=count)
            )
            + (get(prim_cot, across - 1, count=count) - get(prim_cot, across + 1, count=count))
        )
    drag_cot = get(prim_cot, 4 * g.plane + row, count=count)
    thermal_cot = field_cot[3] + 0.7 * (drag_cot * molecular) / thermal
    push_cot = thermal_cot * inverse
    out[0] = out[0] - push_cot * thermal
    pull_push(out, velocity, push_cot)
    for j in range(3):
        scaled = field_cot[j] * inverse
        out[1 + j] = out[1 + j] + scaled
        out[0] = out[0] - scaled * velocity[j]
    return drag_cot


def viscous_pull(prim, cot, prim_cot, grad, front):
    clear_rows(prim_cot, 13 * PLANE)
    for edge in (2, 11):
        row = edge * PITCH + (front + 3)
        viscous_pull_at(prim, cot, prim_cot, row, 1, (0,))
        row = 3 * PITCH + (front + edge)
        viscous_pull_at(prim, cot, prim_cot, row, PITCH, (1,))

    def body(o):
        row = (o + 3) * PITCH + (front + 3)
        viscous_pull_at(prim, cot, prim_cot, row, 1, (0, 1, 2))

    loop(8, body, 4)

    def finish(i):
        row = i * 16 + 16
        out = [get(grad, c * PLANE + row, count=16) for c in range(6)]
        out[5] = out[5] + viscous_finish(prim, prim_cot, row, 16, NARROW, out)
        for c in range(6):
            put(grad, c * PLANE + row, out[c], count=16)

    loop(12, finish, 4)


def wide_viscous_pull(prim, cot, prim_cot, grad, drag_part):
    def body(x):
        viscous_pull_at(prim, cot, prim_cot, wide_row(x, 0), 1, (0, 1, 2), WIDE)

    for x in (-1, 8):
        body(x)
    for y in (-1, 8):
        viscous_pull_at(prim, cot, prim_cot, wide_row(0, y), 24, (0, 1, 2), WIDE)
    loop(8, body, 4)

    def finish(x):
        row = wide_row(x, 0)
        out = [get(grad, c * WIDE.plane + row) for c in range(5)]
        drag_cot = viscous_finish(prim, prim_cot, row, 8, WIDE, out)
        put(drag_part, pl.multiple_of(x * 8, 8), drag_cot)
        for c in range(5):
            put(grad, c * WIDE.plane + row, out[c])

    loop(8, finish, 4)


def clear_rows(ref, rows):
    clear_rows_from(ref, 0, rows)


def clear_rows_from(ref, first, rows):
    for row in range(first, first + rows, 32):
        put(ref, row, jnp.zeros((32, 128), jnp.float32), count=32)


X_ROWS = 68
X_MORE = 5 * X_ROWS
Y_MORE = 5 * 48


def x_pieces(left):
    pieces, place = [], 0
    for x in range(6):
        distance = 5 - x if left else x
        first, count = (0, 14) if distance < 3 else (2, 10) if distance == 3 else (3, 8)
        pieces.append((place, x, first, count))
        place += count
    return pieces


def assemble(padded, own, from_y, from_x, left):
    front, first, outer = frame(left)
    for c in range(5):
        for x in range(8):
            row = c * PLANE + (first + x) * PITCH + front
            put(padded, row + first, get(own, (c * 8 + x) * 8))
            put(padded, row + outer, get(from_y, (c * 8 + x) * 6, count=6), count=6)
        for place, x, cell, count in x_pieces(left):
            row = c * PLANE + (outer + x) * PITCH + front + cell
            put(padded, row, get(from_x, c * X_ROWS + place, count=count), count=count)


def assemble_eddy_left(padded, eddy, zero_y, zero_x):
    front = frame(True)[0]
    for x in range(8):
        row = 5 * PLANE + (6 + x) * PITCH + front
        put(padded, row + 6, get(eddy, x * 8))
        put(padded, row + 2, get(zero_y, Y_MORE + x * 4, count=4), count=4)
    for x in range(4):
        row = 5 * PLANE + (2 + x) * PITCH + front + 2
        put(padded, row, get(zero_x, X_MORE + x * 12, count=12), count=12)


def assemble_eddy_right(padded, eddy, zero_y, zero_x, one_y, one_x):
    base = 5 * PLANE
    for x in range(8):
        row = base + (3 + x) * PITCH
        put(padded, row + 3, get(eddy, x * 8))
        put(padded, row + 2, get(zero_y, Y_MORE + x * 4 + 3, count=1), count=1)
        put(padded, row + 11, get(one_y, Y_MORE + x, count=1), count=1)
    put(padded, base + 2 * PITCH + 3, get(zero_x, X_MORE + 3 * 12 + 4))
    put(padded, base + 11 * PITCH + 3, get(one_x, X_MORE))


def start_kernel(state, eddy, send_y):
    for i in range(40):
        put(send_y, i * 6, get(state, i * 8 + 2, count=6), count=6)
    for x in range(8):
        put(send_y, Y_MORE + x * 4, get(eddy, x * 8 + 4, count=4), count=4)


def side_kernel(left, own, from_y, more, send_x, line):
    front, first, outer = frame(left)
    begin = 2 if left else 0
    for c in range(5):
        for x in range(6):
            source = c * 8 + begin + x
            row = (c * 6 + x) * PITCH + front
            put(line, row + first, get(own, source * 8))
            put(line, row + outer, get(from_y, source * 6, count=6), count=6)
        for place, x, cell, count in x_pieces(left):
            value = get(line, (c * 6 + x) * PITCH + front + cell, count=count)
            put(send_x, c * X_ROWS + place, value, count=count)
    if left:
        for x in range(4):
            row = X_MORE + x * 12
            put(send_x, row, get(from_y, Y_MORE + (4 + x) * 4, count=4), count=4)
            put(send_x, row + 4, get(more, (4 + x) * 8))
    else:
        put(send_x, X_MORE, get(more, 0))


def section_body(left, keep, weight, base, column, out, padded, prim, split, rate, flux_x, flux_y):
    front = frame(left)[0]
    fill_prim(padded, prim)
    line_rate(padded, prim, split, rate, 0, front, True)
    line_rate(padded, prim, split, rate, 1, front, False)
    column_rate(padded, prim, rate, front, range(3) if left else range(5, 8))
    early = 3 if left else 0
    for c in range(5):
        add(rate, (c * 8 + early) * 8, get(column, c * 40, count=40), count=40)
    viscous_rate(prim, flux_x, flux_y, rate, front)
    for x in range(8):
        row = (x + 3) * PITCH + (front + 3)
        for c in range(5):
            place = (c * 8 + x) * 8
            value = weight * get(padded, c * PLANE + row) + (weight * TIME_STEP) * get(rate, place)
            if keep:
                value = value + keep * get(base, place)
            put(out, place, value)


def first_section_kernel(state, zero_y, zero_x, eddy, column, out, send_y, padded, *scratch):
    assemble(padded, state, zero_y, zero_x, True)
    assemble_eddy_left(padded, eddy, zero_y, zero_x)
    section_body(True, 0.0, 1.0, None, column, out, padded, *scratch)
    for i in range(40):
        put(send_y, i * 6, get(out, i * 8, count=6), count=6)
    for x in range(8):
        put(send_y, Y_MORE + x, get(eddy, x * 8, count=1), count=1)


def second_section_kernel(
    own, one_y, one_x, zero_y, zero_x, eddy, state, adjoint, column, out, *refs
):
    send_up, send_down, padded, *scratch = refs
    assemble(padded, own, one_y, one_x, False)
    assemble_eddy_right(padded, eddy, zero_y, zero_x, one_y, one_x)
    section_body(False, 0.75, 0.25, state, column, out, padded, *scratch)
    for i in range(40):
        put(send_up, i * 5, get(out, i * 8 + 3, count=5), count=5)
        put(send_up, 200 + i * 3, get(adjoint, i * 8 + 5, count=3), count=3)
        put(send_down, i * 5, get(out, i * 8, count=5), count=5)
        put(send_down, 200 + i * 3, get(adjoint, i * 8, count=3), count=3)


def first_tangent_kernel(state, zero_y, zero_x, eddy, padded, prim, tangent, split):
    assemble(padded, state, zero_y, zero_x, True)
    assemble_eddy_left(padded, eddy, zero_y, zero_x)
    fill_prim(padded, prim)
    line_tangent(padded, prim, split, tangent, 0, frame(True)[0])


def second_tangent_kernel(own, one_y, one_x, zero_y, zero_x, eddy, padded, prim, tangent, column, split):
    assemble(padded, own, one_y, one_x, False)
    assemble_eddy_right(padded, eddy, zero_y, zero_x, one_y, one_x)
    fill_prim(padded, prim)
    line_tangent(padded, prim, split, tangent, 0, frame(False)[0])
    column_tangent(padded, prim, column, frame(False)[0])


def line_tangent_kernel(left, padded, prim, tangent, split):
    line_tangent(padded, prim, split, tangent, 1, frame(left)[0])


def first_line_and_column_kernel(padded, prim, own, from_y, tangent, column, split, line):
    line_tangent_kernel(True, padded, prim, tangent, split)
    early_column_kernel(False, own, from_y, column, line)


def column_tangent_kernel(left, padded, prim, tangent):
    column_tangent(padded, prim, tangent, frame(left)[0])


def own_column_kernel(own, adjoint, part):
    def body(x):
        rows = [pl.multiple_of((c * 8 + x) * 8, 8) for c in range(5)]
        cells = [get(own, row) for row in rows]
        inverse = 1.0 / cells[0]
        velocity = [cells[1 + j] * inverse for j in range(3)]
        kinetic = 0.5 * (
            cells[1] * velocity[0] + cells[2] * velocity[1] + cells[3] * velocity[2]
        )
        push = (HEAT_RATIO - 1.0) * (cells[4] - kinetic)
        cot = [(2.0 / 3.0 * TIME_STEP) * get(adjoint, row) for row in rows]
        out = column_cot(cells, velocity, push, inverse, cot)
        for row, value in zip(rows, out):
            put(part, row, value)

    loop(8, body, 4)


def hand_back(left, grad, send_x, rest):
    front, first, outer = frame(left)
    for c in range(5):
        for place, x, cell, count in x_pieces(left):
            row = c * PLANE + (outer + x) * PITCH + front + cell
            put(send_x, c * X_ROWS + place, get(grad, row, count=count), count=count)
        row = c * PLANE + first * PITCH
        put(rest, c * 128, get(grad, row, count=128), count=128)


def wide_side_kernel(own, low_y, high_y, adjoint, send_up, send_down):
    for send, first, layer, near in ((send_up, 3, 5, 7), (send_down, 0, 0, 0)):
        for c in range(5):
            put(send, c * 40, get(own, (c * 8 + first) * 8, count=40), count=40)
            put(send, 200 + c * 24, get(adjoint, (c * 8 + layer) * 8, count=24), count=24)
            corner = c * 8 + near
            put(send, 320 + c * 4, get(low_y, corner * 5 + 4, count=1), count=1)
            put(send, 321 + c * 4, get(high_y, corner * 5, count=1), count=1)
            put(send, 322 + c * 4, get(low_y, 202 + corner * 3, count=1), count=1)
            put(send, 323 + c * 4, get(high_y, 200 + corner * 3, count=1), count=1)


def wide_assemble(padded, cot, own, low_y, high_y, low_x, high_x, adjoint, edges):
    zero_y, zero_x, one_y, one_x, eddy = edges
    for c in range(5):
        base = c * WIDE.plane
        for x in range(8):
            row, source = base + wide_row(x, 0), c * 8 + x
            put(padded, row, get(own, source * 8))
            put(padded, row - 5, get(low_y, source * 5, count=5), count=5)
            put(padded, row + 8, get(high_y, source * 5, count=5), count=5)
            put(cot, row, get(adjoint, source * 8))
            put(cot, row - 3, get(low_y, 200 + source * 3, count=3), count=3)
            put(cot, row + 8, get(high_y, 200 + source * 3, count=3), count=3)
        for r in range(5):
            put(padded, base + wide_row(r - 5, 0), get(low_x, (c * 5 + r) * 8))
            put(padded, base + wide_row(r + 8, 0), get(high_x, (c * 5 + r) * 8))
        for r in range(3):
            put(cot, base + wide_row(r - 3, 0), get(low_x, 200 + (c * 3 + r) * 8))
            put(cot, base + wide_row(r + 8, 0), get(high_x, 200 + (c * 3 + r) * 8))
        for x, source in ((-1, low_x), (8, high_x)):
            for k, (ref, y) in enumerate(((padded, -1), (padded, 8), (cot, -1), (cot, 8))):
                row = base + wide_row(x, y)
                put(ref, row, get(source, 320 + c * 4 + k, count=1), count=1)
    base = 5 * WIDE.plane
    for x in range(8):
        put(padded, base + wide_row(x, 0), get(eddy, x * 8))
        put(padded, base + wide_row(x, -1), get(zero_y, Y_MORE + x * 4 + 3, count=1), count=1)
        put(padded, base + wide_row(x, 8), get(one_y, Y_MORE + x, count=1), count=1)
    put(padded, base + wide_row(-1, 0), get(zero_x, X_MORE + 3 * 12 + 4))
    put(padded, base + wide_row(8, 0), get(one_x, X_MORE))


def last_line_kernel(
    own, low_y, high_y, adjoint, column_part, part, padded, prim, split, split_cot, cot, grad
):
    for c in range(5):
        for x in range(8):
            row, source = c * WIDE.plane + wide_row(x, 0), c * 8 + x
            put(padded, row, get(own, source * 8))
            put(padded, row - 5, get(low_y, source * 5, count=5), count=5)
            put(padded, row + 8, get(high_y, source * 5, count=5), count=5)
            put(cot, row, get(adjoint, source * 8))
            put(cot, row - 3, get(low_y, 200 + source * 3, count=3), count=3)
            put(cot, row + 8, get(high_y, 200 + source * 3, count=3), count=3)
            put(grad, row, jnp.zeros((8, 128), jnp.float32))
    clear_rows_from(padded, 5 * WIDE.plane + 5 * 24, 192)
    fill_prim(padded, prim, WIDE.plane, 48, 5 * 24, 4)
    line_pull(padded, prim, split, split_cot, cot, grad, 1, WIDE, range(5, 13))
    for c in range(5):
        for x in range(8):
            row, place = c * WIDE.plane + wide_row(x, 0), (c * 8 + x) * 8
            value = (2.0 / 3.0 * TIME_STEP) * get(grad, row)
            put(part, place, value + get(column_part, place))


def last_section_kernel(
    own, low_y, high_y, low_x, high_x, zero_y, zero_x, one_y, one_x, eddy, adjoint, part, *refs
):
    adjoint_two, drag_part, padded, prim, split, split_cot, cot, prim_cot, grad = refs
    scale = 2.0 / 3.0
    edges = zero_y, zero_x, one_y, one_x, eddy
    wide_assemble(padded, cot, own, low_y, high_y, low_x, high_x, adjoint, edges)
    fill_prim(padded, prim, WIDE.plane, 48, 0, 9)
    for c in range(5):
        for x in range(8):
            put(grad, c * WIDE.plane + wide_row(x, 0), jnp.zeros((8, 128), jnp.float32))
    wide_viscous_pull(prim, cot, prim_cot, grad, drag_part)
    line_pull(padded, prim, split, split_cot, cot, grad, 0, WIDE, range(5, 13))
    for c in range(5):
        for x in range(8):
            row, place = c * WIDE.plane + wide_row(x, 0), (c * 8 + x) * 8
            value = scale * get(adjoint, place) + (scale * TIME_STEP) * get(grad, row)
            put(adjoint_two, place, value + get(part, place))
    for x in range(8):
        put(drag_part, x * 8, (scale * TIME_STEP) * get(drag_part, x * 8))


def earlier_section(left, scale, cells, tangents, rest_in, folded_y, scratch):
    padded, prim = cells
    along_x, along_y, along_z = tangents
    split_cot, cot, prim_cot, grad, folded = scratch
    front = frame(left)[0]
    clear_rows(cot, 5 * PLANE)
    clear_rows(grad, 5 * PLANE)
    begin = 0 if left else 2
    for i in range(40):
        put(folded, i * 8, get(rest_in, i * 8))
        if folded_y is not None:
            add(folded, i * 8 + begin, get(folded_y, i * 6, count=6), count=6)
    for c in range(5):
        for x in range(8):
            row = c * PLANE + (3 + x) * PITCH + (front + 3)
            value = scale * get(folded, (c * 8 + x) * 8)
            put(cot, row, TIME_STEP * value)
            put(grad, row, value)
    viscous_pull(prim, cot, prim_cot, grad, front)
    g = narrow(front)
    line_pull(padded, prim, None, split_cot, cot, grad, 1, g, range(14), along_y)
    line_pull(padded, prim, None, split_cot, cot, grad, 0, g, range(14), along_x)
    column_pull(padded, prim, cot, grad, front, along_z, range(3) if left else range(5, 8))


def second_pull_kernel(
    padded, prim, along_x, along_y, along_z, adjoint_two, send_x, rest, drag_part, *scratch
):
    grad = scratch[3]
    clear_rows_from(grad, 5 * PLANE, PLANE)
    earlier_section(
        False, 0.25, (padded, prim), (along_x, along_y, along_z), adjoint_two, None, scratch
    )
    hand_back(False, grad, send_x, rest)
    put(send_x, X_MORE, get(grad, 5 * PLANE + 11 * PITCH + 3))
    put(drag_part, 0, get(grad, 5 * PLANE, count=PLANE), count=PLANE)


def first_pull_kernel(
    padded, prim, along_x, along_y, along_z, rest_in, folded_y, folded_x, drag_two, drag_one, *refs
):
    send_x, rest, folded = refs[:3]
    scratch = [*refs[3:], folded]
    grad = scratch[3]
    front = frame(True)[0]
    clear_rows_from(grad, 5 * PLANE, PLANE)
    for x in range(8):
        put(grad, 5 * PLANE + (6 + x) * PITCH + front + 6, get(drag_two, x * 8))
    for x in range(9):
        row = 5 * PLANE + (5 + x) * PITCH + front + 5
        add(grad, row, get(drag_one, (2 + x) * PITCH + 2, count=9), count=9)
    add(grad, 5 * PLANE + 6 * PITCH + front + 6, get(folded_x, X_MORE))
    for x in range(8):
        row = 5 * PLANE + (6 + x) * PITCH + front + 6
        add(grad, row, get(folded_y, Y_MORE + x, count=1), count=1)
    earlier_section(
        True, 1.0, (padded, prim), (along_x, along_y, along_z), rest_in, folded_y, scratch
    )
    hand_back(True, grad, send_x, rest)
    for x in range(4):
        row = 5 * PLANE + (2 + x) * PITCH + front + 2
        put(send_x, X_MORE + x * 12, get(grad, row, count=12), count=12)
    put(rest, 640, get(grad, 5 * PLANE + 6 * PITCH, count=128), count=128)


def fold_rows(left, rest_in, from_x, part, rest, send_y, work):
    front, first, outer = frame(left)
    begin = 2 if left else 0
    put(work, 0, get(rest_in, 0, count=640), count=640)
    for c in range(5):
        for i in range(5):
            x = i if left else 3 + i
            add(work, (c * 8 + x) * PITCH + front + 3, get(part, (c * 5 + i) * 8))
        for place, x, cell, count in x_pieces(left):
            row = (c * 8 + begin + x) * PITCH + front + cell
            add(work, row, get(from_x, c * X_ROWS + place, count=count), count=count)
    for i in range(40):
        put(rest, i * 8, get(work, i * PITCH + front + first))
        put(send_y, i * 6, get(work, i * PITCH + front + outer, count=6), count=6)


def second_fold_kernel(rest_in, from_x, part, drag_part, rest, send_y, work):
    fold_rows(False, rest_in, from_x, part, rest, send_y, work)
    for x in range(8):
        put(send_y, Y_MORE + x, get(drag_part, (3 + x) * PITCH + 11, count=1), count=1)


def first_fold_kernel(rest_in, from_x, part, rest, send_y, work):
    fold_rows(True, rest_in, from_x, part, rest, send_y, work)
    put(work, 640, get(rest_in, 640, count=128), count=128)
    front = frame(True)[0]
    for x in range(4):
        row = 640 + (4 + x) * PITCH + front + 2
        add(work, row, get(from_x, X_MORE + x * 12, count=12), count=12)
    for x in range(8):
        put(rest, 320 + x * 8, get(work, 640 + x * PITCH + front + 6))
        row = 640 + x * PITCH + front + 2
        put(send_y, Y_MORE + x * 4, get(work, row, count=4), count=4)


def end_kernel(adjoint, adjoint_two, rest_zero, folded_zero, grad_state, grad_eddy):
    for i in range(40):
        value = (1.0 / 3.0) * get(adjoint, i * 8) + 0.75 * get(adjoint_two, i * 8)
        put(grad_state, i * 8, value + get(rest_zero, i * 8))
        add(grad_state, i * 8 + 2, get(folded_zero, i * 6, count=6), count=6)
    for i in range(8):
        put(grad_eddy, i * 8, get(rest_zero, 320 + i * 8))
        add(grad_eddy, i * 8 + 4, get(folded_zero, Y_MORE + i * 4, count=4), count=4)


def run(kernel, operands, outs, scratch=(), work=0):
    cost = pl.CostEstimate(flops=work, bytes_accessed=4 * work, transcendentals=0) if work else None
    return pl.pallas_call(
        kernel,
        out_shape=[jax.ShapeDtypeStruct((rows, 128), jnp.float32) for rows in outs],
        in_specs=[pl.BlockSpec(memory_space=pltpu.VMEM)] * len(operands),
        out_specs=[pl.BlockSpec(memory_space=pltpu.VMEM)] * len(outs),
        scratch_shapes=[pltpu.VMEM((rows, 128), jnp.float32) for rows in scratch],
        compiler_params=pltpu.CompilerParams(vmem_limit_bytes=20 * 1024 * 1024),
        cost_estimate=cost,
    )(*operands)


def shifted(values, axis, up):
    count = lax.axis_size(axis)
    step = 1 if up else count - 1
    return lax.ppermute(values, axis, [(i, (i + step) % count) for i in range(count)])


def together(*values):
    return lax.optimization_barrier(values)


def shifted_beside(values, axis, up, kernel, operands, outs, scratch=()):
    values, *operands = together(values, *operands)
    moved = shifted(values, axis, up)
    moved, *results = together(moved, *run(kernel, operands, outs, scratch, 2_000_000))
    return moved, results


def shifted_both_beside(up, down, axis, jobs):
    operands = [operand for job in jobs for operand in job[1]]
    up, down, *operands = together(up, down, *operands)
    low, high = shifted(up, axis, True), shifted(down, axis, False)
    results, place, counts = [], 0, []
    for kernel, given, outs, scratch in jobs:
        made = run(kernel, operands[place : place + len(given)], outs, scratch, 2_000_000)
        place += len(given)
        counts.append(len(made))
        results += made
    low, high, *results = together(low, high, *results)
    grouped = []
    for count in counts:
        grouped.append(results[:count])
        results = results[count:]
    return low, high, grouped


def pipeline(state, eddy, adjoint):
    section_scratch = (6 * PLANE, 8 * PLANE, 1120, 320, 4 * PLANE, 4 * PLANE)
    wide = WIDE.plane
    last_scratch = (6 * wide, 8 * wide, 1440, 1440, 5 * wide, 13 * wide, 5 * wide)
    earlier_scratch = (1120, 5 * PLANE, 13 * PLANE, 6 * PLANE, 320)
    first_tangent = [6 * PLANE, 8 * PLANE, 2880]

    def sides(own, from_y, more, left, rows):
        (send_x,) = run(
            functools.partial(side_kernel, left),
            [own, from_y, more],
            [X_MORE + rows],
            [5 * 6 * PITCH],
        )
        return send_x

    (send_y,) = run(start_kernel, [state, eddy], [Y_MORE + 32])
    zero_y = shifted(send_y, "gy", True)
    zero_x, (column,) = shifted_beside(
        sides(state, zero_y, eddy, True, 48),
        "gx",
        True,
        functools.partial(early_column_kernel, True),
        [state, zero_y],
        [200],
        [80],
    )
    zero = [state, zero_y, zero_x, eddy]
    one, send_y = run(first_section_kernel, [*zero, column], [320, Y_MORE + 8], section_scratch)

    one_y, (zero_cells, zero_prim, zero_along_x) = shifted_beside(
        send_y, "gy", False, first_tangent_kernel, zero, first_tangent, [1120]
    )
    one_x, (zero_along_y, column) = shifted_beside(
        sides(one, one_y, eddy, False, 8),
        "gx",
        False,
        first_line_and_column_kernel,
        [zero_cells, zero_prim, one, one_y],
        [2880, 200],
        [1120, 80],
    )
    one_all = [one, one_y, one_x, zero_y, zero_x, eddy]
    two, send_up, send_down = run(
        second_section_kernel, [*one_all, state, adjoint, column], [320, 320, 320], section_scratch
    )

    low_y, high_y, ((column_part,), one_made) = shifted_both_beside(
        send_up,
        send_down,
        "gy",
        [
            (own_column_kernel, [two, adjoint], [320], []),
            (second_tangent_kernel, one_all, [*first_tangent, 2560], [1120]),
        ],
    )
    one_cells, one_prim, one_along_x, one_along_z = one_made
    send_up, send_down = run(wide_side_kernel, [two, low_y, high_y, adjoint], [340, 340])
    low_x, high_x, ((one_along_y,), (part,)) = shifted_both_beside(
        send_up,
        send_down,
        "gx",
        [
            (
                functools.partial(line_tangent_kernel, False),
                [one_cells, one_prim],
                [2880],
                [1120],
            ),
            (
                last_line_kernel,
                [two, low_y, high_y, adjoint, column_part],
                [320],
                [*last_scratch[:5], 5 * wide],
            ),
        ],
    )
    adjoint_two, drag_two = run(
        last_section_kernel,
        [
            *(two, low_y, high_y, low_x, high_x, zero_y, zero_x, one_y, one_x),
            *(eddy, adjoint, part),
        ],
        [320, 64],
        last_scratch,
    )

    one_tangents = [one_along_x, one_along_y, one_along_z]
    send_x, rest, drag_one = run(
        second_pull_kernel,
        [one_cells, one_prim, *one_tangents, adjoint_two],
        [X_MORE + 8, 640, PLANE],
        earlier_scratch,
    )
    from_x, (part,) = shifted_beside(
        send_x,
        "gx",
        True,
        functools.partial(late_column_kernel, False, 0.25),
        [one_cells, one_prim, one_along_z, adjoint_two],
        [200],
    )
    rest_one, send_y = run(
        second_fold_kernel, [rest, from_x, part, drag_one], [320, Y_MORE + 8], [640]
    )
    folded_one, (zero_along_z,) = shifted_beside(
        send_y,
        "gy",
        True,
        functools.partial(column_tangent_kernel, True),
        [zero_cells, zero_prim],
        [2560],
    )

    zero_tangents = [zero_along_x, zero_along_y, zero_along_z]
    send_x, rest, folded = run(
        first_pull_kernel,
        [zero_cells, zero_prim, *zero_tangents, rest_one, folded_one, from_x, drag_two, drag_one],
        [X_MORE + 48, 768, 320],
        earlier_scratch[:-1],
    )
    from_x, (part,) = shifted_beside(
        send_x,
        "gx",
        False,
        functools.partial(late_column_kernel, True, 1.0),
        [zero_cells, zero_prim, zero_along_z, folded],
        [200],
    )
    rest_zero, send_y = run(first_fold_kernel, [rest, from_x, part], [384, Y_MORE + 32], [768])
    folded_zero = shifted(send_y, "gy", False)
    return run(end_kernel, [adjoint, adjoint_two, rest_zero, folded_zero], [320, 64])


def on_device(state, eddy, adjoint):
    grad_state, grad_eddy = pipeline(
        state.reshape(320, 128), eddy.reshape(64, 128), adjoint.reshape(320, 128)
    )
    return grad_state.reshape(5, 8, 8, 128), grad_eddy.reshape(8, 8, 128)


def solution(mesh):
    placed = (P(None, "gx", "gy", None), P("gx", "gy", None), P(None, "gx", "gy", None))
    return jax.shard_map(
        on_device,
        mesh=mesh,
        in_specs=placed,
        out_specs=(P(None, "gx", "gy", None), P("gx", "gy", None)),
        check_vma=False,
    )
```
